32 devices in a mesh: section: 2 (over core), fsdp: 2 (over x), context: 2 (over y), tensor: 4 (over z).
Axes of the slice: x: 2, y: 2, z: 4, core: 2. Of those that a mesh axis runs over, the one named last changes fastest.
Arguments:
- block_input: bfloat16 [4, 1024, 1536], P('fsdp', 'context'), may hold values from -6 to 6
- doc_start: int32 [4, 1024], P('fsdp', 'context'), may hold values from 0 to 1, as said below
- cotangent: bfloat16 [4, 1024, 1536], P('fsdp', 'context'), may hold values from -6 to 6
- norm_gain: float32 [2, 1536], P('section'), may hold values from 0.5 to 1.5
- proj_main: bfloat16 [2, 1536, 2, 3072], P('section', 'fsdp', None, 'tensor'), may hold values from -0.15625 to 0.15625
- proj_states: bfloat16 [2, 1536, 256], P('section', 'fsdp'), may hold values from -0.15625 to 0.15625
- proj_step: bfloat16 [2, 1536, 48], P('section', 'fsdp', 'tensor'), may hold values from -0.15625 to 0.15625
- conv_main: float32 [2, 4, 3072], P('section', None, 'tensor'), may hold values from -3 to 3
- conv_main_bias: float32 [2, 3072], P('section', 'tensor'), may hold values from -1.5 to 1.5
- conv_states: float32 [2, 4, 256], P('section'), may hold values from -3 to 3
- conv_states_bias: float32 [2, 256], P('section'), may hold values from -1.5 to 1.5
- step_bias: float32 [2, 48], P('section', 'tensor'), may hold values from -6 to -4
- log_decay: float32 [2, 48], P('section', 'tensor'), may hold values from -3.9 to 1.4
- skip_gain: float32 [2, 48], P('section', 'tensor'), may hold values from 0.5 to 1.5
- gated_gain: float32 [2, 3072], P('section', 'tensor'), may hold values from 0.5 to 1.5
- proj_out: bfloat16 [2, 1536, 3072], P('section', 'fsdp', 'tensor'), may hold values from -0.109375 to 0.109375
Outputs:
- layer_out: float32 [2, 4, 1024, 1536], P('section', 'fsdp', 'context')
- layer_in_grad: float32 [2, 4, 1024, 1536], P('section', 'fsdp', 'context')
- grad_norm_gain: float32 [2, 1536], P('section')
- grad_proj_main: float32 [2, 1536, 2, 3072], P('section', ('fsdp', 'context'), None, 'tensor')
- grad_proj_states: float32 [2, 1536, 256], P('section', ('fsdp', 'context'))
- grad_proj_step: float32 [2, 1536, 48], P('section', ('fsdp', 'context'), 'tensor')
- grad_conv_main: float32 [2, 4, 3072], P('section', None, 'tensor')
- grad_conv_main_bias: float32 [2, 3072], P('section', 'tensor')
- grad_conv_states: float32 [2, 4, 256], P('section')
- grad_conv_states_bias: float32 [2, 256], P('section')
- grad_step_bias: float32 [2, 48], P('section', 'tensor')
- grad_log_decay: float32 [2, 48], P('section', 'tensor')
- grad_skip_gain: float32 [2, 48], P('section', 'tensor')
- grad_gated_gain: float32 [2, 3072], P('section', 'tensor')
- grad_proj_out: float32 [2, 1536, 3072], P('section', ('fsdp', 'context'), 'tensor')
The draws below stay inside these ranges and needn't reach their ends.
Inputs may be any that keep to these rules, and one draw needn't show every extreme that they name: `doc_start`: 1 at the first token of each document and 0 elsewhere; position 0 of every sequence is 1; documents have 60 to 800 tokens unless cut by their sequence's end; among the 2 sequences of each fsdp index one is a single document.
All inputs are finite; a program needn't handle non-finite values.
Results may differ from the reference program's by a relative error of at most 0.01.
Values may be sent and summed in bfloat16 or wider, within the bound.
No kernel may reach another device: no remote copies, remote signals or barrier semaphores. Data moves between devices by JAX's collectives and lax.ppermute only.
A program may use at most 256 MiB of HBM per device.

```python
import jax
import jax.numpy as jnp
from jax import lax

D = 1536
HEADS = 48
HEAD_DIM = 64
NSTATE = 128
CONV = 4
SEQ = 1024
MICRO = 2
DOC_MIN = 60
DOC_MAX = 800
INNER = 3072
SEQS = 4
LAYERS = 2
BLOCK_ROWS = 256


def draw_doc_start(key, part):
    key = jax.random.fold_in(key, 7)
    key_lengths, key_pick = jax.random.split(key)
    doc_count = SEQ // DOC_MIN + 2
    doc_lengths = jax.random.randint(key_lengths, (SEQS, doc_count), DOC_MIN, DOC_MAX + 1)
    doc_ends = jnp.cumsum(doc_lengths, axis=1)
    position = jnp.arange(SEQ)
    boundary = jnp.any(position[None, :, None] == doc_ends[:, None, :], axis=2)
    opening = position[None, :] == 0
    packed = jnp.logical_or(boundary, opening)
    groups = SEQS // MICRO
    chosen = jax.random.randint(key_pick, (groups,), 0, MICRO)
    sequence = jnp.arange(SEQS)
    single = sequence % MICRO == chosen[sequence // MICRO]
    return jnp.where(single[:, None], opening, packed).astype(jnp.int32)


def levels(stream_key, dims, cuts, smallest, top_value):
    def one(dim, blocks):
        steps = jax.random.uniform(jax.random.fold_in(jax.random.fold_in(stream_key, 6), dim), (blocks,), jnp.float32, smallest / len(cuts), top_value / len(cuts))
        return jnp.repeat(jnp.exp(steps), dims[dim] // blocks).reshape((-1,) + (1,) * (len(dims) - dim - 1))

    loudness = one(*cuts[0])
    for cut in cuts[1:]:
        loudness = loudness * one(*cut)
    return loudness


def bell_draw(key, shape, scale, limit, shards=(), kind=jnp.bfloat16):
    entries = jax.random.normal(key, shape, jnp.float32) * scale
    if len(shards) > 0:
        entries = levels(key, shape, shards, -0.22, 0.18) * entries
    return jnp.clip(entries, min=-limit, max=limit).astype(kind)


def setup_inputs(seed: int = 0) -> dict:
    key_list = jax.random.split(jax.random.key(seed), 17)
    block_input = bell_draw(key_list[0], (SEQS, SEQ, D), 1.0, 6.0, ((0, 2), (1, 2)))
    doc_start = draw_doc_start(jax.random.fold_in(key_list[16], 71), 0)
    cotangent = bell_draw(key_list[2], (SEQS, SEQ, D), 1.0, 6.0, ((0, 2), (1, 2)))
    norm_gain = jnp.clip(1.0 + 0.1 * jax.random.normal(key_list[3], (LAYERS, D), jnp.float32), 0.5, 1.5)
    proj_main = bell_draw(key_list[4], (LAYERS, D, 2, INNER), D ** -0.5, 0.15625, ((0, 2), (1, 2), (3, 4)))
    proj_states = bell_draw(key_list[5], (LAYERS, D, 2 * NSTATE), D ** -0.5, 0.15625, ((0, 2), (1, 2)))
    proj_step = bell_draw(key_list[6], (LAYERS, D, HEADS), D ** -0.5, 0.15625, ((0, 2), (1, 2), (2, 4)))
    conv_main = bell_draw(key_list[7], (LAYERS, CONV, INNER), CONV ** -0.5, 3.0, ((0, 2), (2, 4)), jnp.float32)
    conv_main_bias = bell_draw(key_list[8], (LAYERS, INNER), 0.3, 1.5, ((0, 2), (1, 4)), jnp.float32)
    conv_states = bell_draw(key_list[9], (LAYERS, CONV, 2 * NSTATE), CONV ** -0.5, 3.0, ((0, 2),), jnp.float32)
    conv_states_bias = bell_draw(key_list[10], (LAYERS, 2 * NSTATE), 0.3, 1.5, ((0, 2),), jnp.float32)
    step_bias = jnp.clip(-6.0 + 2.0 * jax.random.uniform(key_list[11], (LAYERS, HEADS), jnp.float32) ** levels(key_list[11], (LAYERS, HEADS), ((0, 2), (1, 4)), -0.2, 0.2), -6.0, -4.0)
    log_decay = jnp.clip(-3.9 + 5.3 * jax.random.uniform(key_list[12], (LAYERS, HEADS), jnp.float32) ** levels(key_list[12], (LAYERS, HEADS), ((0, 2), (1, 4)), -0.2, 0.2), -3.9, 1.4)
    skip_gain = jnp.clip(1.0 + 0.1 * jax.random.normal(key_list[13], (LAYERS, HEADS), jnp.float32), 0.5, 1.5)
    gated_gain = jnp.clip(1.0 + 0.1 * jax.random.normal(key_list[14], (LAYERS, INNER), jnp.float32), 0.5, 1.5)
    proj_out = bell_draw(key_list[15], (LAYERS, D, INNER), INNER ** -0.5, 0.109375, ((0, 2), (1, 2), (2, 4)))
    return {"block_input": block_input, "doc_start": doc_start, "cotangent": cotangent, "norm_gain": norm_gain, "proj_main": proj_main, "proj_states": proj_states, "proj_step": proj_step, "conv_main": conv_main, "conv_main_bias": conv_main_bias, "conv_states": conv_states, "conv_states_bias": conv_states_bias, "step_bias": step_bias, "log_decay": log_decay, "skip_gain": skip_gain, "gated_gain": gated_gain, "proj_out": proj_out}


EPS = 1e-05
HIGH = lax.Precision.HIGHEST

@jax.custom_vjp
def low(v):
    return lax.optimization_barrier(v.astype(jnp.bfloat16)).astype(jnp.float32)

@jax.custom_vjp
def low_back(v):
    return v

def low_keep(v):
    return (low(v), None)

def low_pass(kept, grad):
    return (grad,)

def back_keep(v):
    return (v, None)

def back_low(kept, grad):
    return (low(grad),)
low.defvjp(low_keep, low_pass)
low_back.defvjp(back_keep, back_low)

def mixer_inputs(full_rows, start_marks, conv_main, conv_main_bias, conv_states, conv_states_bias, step_raw, step_bias, log_decay):
    weight = jnp.concatenate([conv_main, conv_states], axis=1)
    bias_all = jnp.concatenate([conv_main_bias, conv_states_bias])
    length = full_rows.shape[0] - (CONV - 1)
    counts = jnp.cumsum(start_marks)
    conv_sum = jnp.zeros((length, weight.shape[1]), jnp.float32) + bias_all[None, :]
    for offset in range(CONV):
        start_row = CONV - 1 - offset
        window = full_rows[start_row:start_row + length]
        same_doc = counts[CONV - 1:] - counts[start_row:start_row + length] == 0.0
        conv_sum = conv_sum + weight[offset][None, :] * window * same_doc[:, None].astype(jnp.float32)
    active = jax.nn.silu(conv_sum)
    inner_width = conv_main.shape[1]
    state_width = conv_states.shape[1] // 2
    values = active[:, :inner_width].reshape(length, -1, HEAD_DIM)
    b_proj = active[:, inner_width:inner_width + state_width]
    c_proj = active[:, inner_width + state_width:]
    step_size = jax.nn.softplus(step_raw + step_bias[None, :])
    decay_rate = -jnp.exp(log_decay)[None, :] * step_size
    return (values, b_proj, c_proj, step_size, decay_rate)

def span_step(state_now, pieces):
    values, b_proj, c_proj, step_size, decay_rate, starts = pieces
    counts = jnp.cumsum(starts).astype(jnp.int32)
    cumulative = jnp.cumsum(decay_rate, axis=0)
    final_sum = cumulative[-1]
    position = jnp.arange(starts.shape[0])
    same_doc = (counts[:, None] == counts[None, :]) & (position[:, None] >= position[None, :])
    decay_gap = jnp.where(same_doc[:, :, None], cumulative[:, None, :] - cumulative[None, :, :], 0.0)
    weights = jnp.where(same_doc[:, :, None], jnp.exp(decay_gap), 0.0)
    scores = jnp.dot(c_proj, b_proj.T, precision=HIGH)
    mixing = scores[:, :, None] * weights * step_size[None, :, :]
    output = jnp.einsum('tsh,shp->thp', mixing, values, precision=HIGH)
    entry_rate = jnp.where((counts == 0)[:, None], jnp.exp(cumulative), 0.0)
    output = output + entry_rate[:, :, None] * jnp.einsum('tn,hpn->thp', c_proj, state_now, precision=HIGH)
    carried = jnp.where((counts == counts[-1])[:, None], jnp.exp(final_sum[None, :] - cumulative), 0.0) * step_size
    keep_rate = jnp.where(counts[-1] == 0, jnp.exp(final_sum), 0.0)
    new_state = keep_rate[:, None, None] * state_now + jnp.einsum('th,thp,tn->hpn', carried, values, b_proj, precision=HIGH)
    return (new_state, output)

def scan_spans(values, b_proj, c_proj, step_size, decay_rate, starts, state_in):
    length = values.shape[0]
    span_count = length // BLOCK_ROWS
    head_count = values.shape[1]
    pieces = (values.reshape(span_count, BLOCK_ROWS, head_count, HEAD_DIM), b_proj.reshape(span_count, BLOCK_ROWS, -1), c_proj.reshape(span_count, BLOCK_ROWS, -1), step_size.reshape(span_count, BLOCK_ROWS, head_count), decay_rate.reshape(span_count, BLOCK_ROWS, head_count), starts.reshape(span_count, BLOCK_ROWS))
    state_out, outputs = lax.scan(jax.checkpoint(span_step), state_in, pieces)
    return (outputs.reshape(length, head_count, HEAD_DIM), state_out)

def gated_part(mixed_out, values, gate_z, skip_gain):
    length = values.shape[0]
    combined = (mixed_out + skip_gain[None, :, None] * values).reshape(length, -1)
    return combined * jax.nn.silu(gate_z)

def mixer_layer(inputs, starts, params):
    norm_gain, proj_main, proj_states, proj_step, conv_main, conv_main_bias, conv_states, conv_states_bias, step_bias, log_decay, skip_gain, gated_gain, proj_out = params
    inv_rms = lax.rsqrt(lax.optimization_barrier(jnp.mean(inputs * inputs, axis=-1)) + EPS)
    normed = low(inputs * inv_rms[:, None] * norm_gain[None, :])
    main_cols = low_back(jnp.einsum('ld,dki->lki', normed, proj_main, precision=HIGH))
    state_cols = low_back(jnp.dot(normed, proj_states, precision=HIGH))
    step_raw = low_back(jnp.dot(normed, proj_step, precision=HIGH))
    pre_conv = jnp.concatenate([main_cols[:, 1], state_cols], axis=1)
    full_rows = jnp.concatenate([jnp.zeros((CONV - 1, pre_conv.shape[1]), jnp.float32), pre_conv], axis=0)
    start_marks = jnp.concatenate([jnp.zeros((CONV - 1,), jnp.float32), starts.astype(jnp.float32)])
    values, b_proj, c_proj, step_size, decay_rate = mixer_inputs(full_rows, start_marks, conv_main, conv_main_bias, conv_states, conv_states_bias, step_raw, step_bias, log_decay)
    zero_state = jnp.zeros((values.shape[1], HEAD_DIM, NSTATE), jnp.float32)
    mixed_out, state_end = scan_spans(values, b_proj, c_proj, step_size, decay_rate, starts, zero_state)
    gated = gated_part(mixed_out, values, main_cols[:, 0], skip_gain)
    inv_rms_gated = lax.rsqrt(lax.optimization_barrier(jnp.mean(gated * gated, axis=-1)) + EPS)
    scaled = low(gated * inv_rms_gated[:, None] * gated_gain[None, :])
    branch = low_back(jnp.dot(scaled, proj_out.T, precision=HIGH))
    return inputs + branch

def reference(block_input, doc_start, cotangent, norm_gain, proj_main, proj_states, proj_step, conv_main, conv_main_bias, conv_states, conv_states_bias, step_bias, log_decay, skip_gain, gated_gain, proj_out):
    stacked = tuple((param.astype(jnp.float32) for param in (norm_gain, proj_main, proj_states, proj_step, conv_main, conv_main_bias, conv_states, conv_states_bias, step_bias, log_decay, skip_gain, gated_gain, proj_out)))
    first_params = tuple((param[0] for param in stacked))
    second_params = tuple((param[1] for param in stacked))

    def one_sequence(gradients, items):
        seq_input, starts, seq_cot = items

        def apply_layer(inputs, params):
            return mixer_layer(inputs, starts, params)
        hidden, pull_first = jax.vjp(apply_layer, seq_input, first_params)
        final_out, pull_second = jax.vjp(apply_layer, hidden, second_params)
        hidden_grad, second_grad = pull_second(seq_cot)
        input_grad, first_grad = pull_first(hidden_grad)
        gradients = jax.tree.map(jnp.add, gradients, (first_grad, second_grad))
        return (gradients, (hidden, final_out, input_grad, hidden_grad))
    initial = jax.tree.map(jnp.zeros_like, (first_params, second_params))
    gradients, results = lax.scan(one_sequence, initial, (block_input.astype(jnp.float32), doc_start, cotangent.astype(jnp.float32)))
    hidden, final_out, input_grad, hidden_grad = results
    layer_out = jnp.stack([hidden, final_out])
    layer_in_grad = jnp.stack([input_grad, hidden_grad])
    merged = [jnp.stack([lower_grad, upper_grad]) for lower_grad, upper_grad in zip(gradients[0], gradients[1])]
    return (layer_out, layer_in_grad, merged[0], merged[1], merged[2], merged[3], merged[4], merged[5], merged[6], merged[7], merged[8], merged[9], merged[10], merged[11], merged[12])
```

```python
import functools

import jax
import jax.numpy as jnp
import numpy as np
from jax import lax
from jax.experimental import pallas as pl
from jax.experimental.pallas import tpu as pltpu
from jax.sharding import PartitionSpec as P

HEAD_DIM = 64
NSTATE = 128
CONV = 4
SPAN = 128
INNER = 3072
LANES = 128
EPS = 1e-05
BREAK = 128.0
HIGH = lax.Precision.HIGHEST
F32 = jnp.float32
BF16 = jnp.bfloat16
VMEM_BYTES = 24 * 1024 * 1024

NT = (((1,), (1,)), ((), ()))
TN = (((0,), (0,)), ((), ()))


def mm(a, b, dims=(((1,), (0,)), ((), ()))):
    return lax.dot_general(a, b, dims, preferred_element_type=F32)


def exact(a, b):
    return lax.dot_general(a, b, (((1,), (0,)), ((), ())), precision=HIGH, preferred_element_type=F32)


def halves(a):
    top = a.astype(BF16)
    return top, (a - top.astype(F32)).astype(BF16)


def spread(a, spread_matrix):
    top, rest = halves(a)
    return mm(jnp.concatenate([top, rest], axis=1), spread_matrix)


def gather_heads(a, gather_matrix):
    top, rest = halves(a)
    return mm(jnp.concatenate([top, rest], axis=1), gather_matrix)


def logistic(v):
    return 0.5 * jnp.tanh(0.5 * v) + 0.5


def softplus(v):
    u = jnp.exp(-jnp.abs(v))
    small = u * (1.0 - u * (0.5 - u * (1.0 / 3.0)))
    return jnp.maximum(v, 0.0) + jnp.where(u < 1e-3, small, jnp.log(1.0 + u))


def lower_ones(rows):
    t = lax.broadcasted_iota(jnp.int32, (rows, rows), 0)
    s = lax.broadcasted_iota(jnp.int32, (rows, rows), 1)
    return t >= s


def pair_masks():
    lane = lax.broadcasted_iota(jnp.int32, (1, LANES), 1)
    first = (lane < HEAD_DIM).astype(BF16)
    return first, (1.0 - first.astype(F32)).astype(BF16)


def both_halves(a):
    top, rest = halves(a)
    return jnp.concatenate([top, rest], axis=1)


def triple(a, b):
    a_top, a_rest = halves(a)
    b_top, b_rest = halves(b)
    return (
        jnp.concatenate([a_top, a_rest, a_top], axis=1),
        jnp.concatenate([b_top, b_top, b_rest], axis=1),
    )


def twice(a):
    return jnp.concatenate([a, a], axis=0)


def chunk_of(rows, width, reverse=0):
    if reverse:
        return pl.BlockSpec((rows, width), lambda c: (reverse - 1 - c, 0))
    return pl.BlockSpec((rows, width), lambda c: (c, 0))


def lanes_of(rows, reverse=0):
    if reverse:
        return pl.BlockSpec((8, rows), lambda c: (0, reverse - 1 - c))
    return pl.BlockSpec((8, rows), lambda c: (0, c))


def stack_of(rows, width, reverse=0):
    if reverse:
        return pl.BlockSpec((1, rows, width), lambda c: (reverse - 1 - c, 0, 0))
    return pl.BlockSpec((1, rows, width), lambda c: (c, 0, 0))


def whole_of(rows, width):
    return pl.BlockSpec((rows, width), lambda c: (0, 0))


def scalars_of():
    return pl.BlockSpec(memory_space=pltpu.SMEM)


def anywhere(count):
    return [pl.BlockSpec(memory_space=pl.ANY)] * count


def params_of():
    return pltpu.CompilerParams(dimension_semantics=("arbitrary",), vmem_limit_bytes=VMEM_BYTES)


def shape(*dims, dtype=F32):
    return jax.ShapeDtypeStruct(dims, dtype)


def cost(flops, moved):
    return pl.CostEstimate(flops=int(flops), bytes_accessed=int(moved), transcendentals=0)


def weight_copies(where_ref, refs, buffer, sems):
    first, core = where_ref[1], where_ref[2]
    rows = buffer.shape[0] // 2
    width = buffer.shape[1]
    near_at = pl.ds(pl.multiple_of((1 - first) * rows, rows), rows)
    far = first * rows
    step = rows // 2
    *near, far_mine, far_other = refs
    pairs = []
    column = 0
    for (start, size), held, other in near:
        part = buffer.at[near_at, column : column + size]
        sem = sems.at[len(pairs)]
        pairs.append(
            (
                pltpu.make_async_copy(held.at[:, start : start + size], part, sem),
                pltpu.make_async_copy(other.at[:, start : start + size], part, sem),
            )
        )
        column += size
    for ref, which in ((far_mine, core), (far_other, 1 - core)):
        part = buffer.at[pl.ds(pl.multiple_of(far + which * step, step), step)]
        copy = pltpu.make_async_copy(ref, part, sems.at[len(pairs)])
        pairs.append((copy, copy))
    return pairs


def start_weights(where_ref, refs, buffer, sems):
    pairs = weight_copies(where_ref, refs, buffer, sems)

    @pl.when(where_ref[0] == 1)
    def _():
        for held, _ in pairs:
            held.start()

    @pl.when(where_ref[0] == 0)
    def _():
        for _, other in pairs:
            other.start()


def wait_weights(where_ref, refs, buffer, sems):
    for held, _ in weight_copies(where_ref, refs, buffer, sems):
        held.wait()


def load_weights(where_ref, refs, buffer, sems):
    start_weights(where_ref, refs, buffer, sems)
    wait_weights(where_ref, refs, buffer, sems)


def front_refs(refs):
    main, main_other, rest, rest_other, mine, other = refs
    width = main.shape[1] // 2
    return ((width, width), main, main_other), ((0, rest.shape[1]), rest, rest_other), mine, other


def gate_refs(refs):
    main, main_other, mine, other = refs
    return ((0, main.shape[1] // 2), main, main_other), mine, other


def out_refs(refs):
    held, held_other, mine, other = refs
    return ((0, held.shape[1]), held, held_other), mine, other


def weight_scratch(weights):
    rows, width = weights[-1].shape
    return [pltpu.VMEM((4 * rows, width), BF16), pltpu.SemaphoreType.DMA((4,))]


TAPS, BIAS, SKIP, GATED, NORM, STEP, DECAY, PACK = 0, 4, 8, 9, 10, 12, 13, 16


def pack_kernel(taps_a, taps_b, bias_a, bias_b, skip, gated, norm, step, decay, pack_ref):
    width = taps_a.shape[1]
    half = norm.shape[1] // 2
    pack_ref[...] = jnp.zeros_like(pack_ref)
    pack_ref[TAPS : TAPS + CONV, :width] = taps_a[...]
    pack_ref[TAPS : TAPS + CONV, width:] = taps_b[...]
    pack_ref[BIAS : BIAS + 1, :width] = bias_a[...]
    pack_ref[BIAS : BIAS + 1, width:] = bias_b[...]
    pack_ref[SKIP : SKIP + 1, :width] = skip[...]
    pack_ref[GATED : GATED + 1, :width] = gated[...]
    pack_ref[NORM : NORM + 1, :half] = norm[:, :half]
    pack_ref[NORM + 1 : NORM + 2, :half] = norm[:, half:]
    pack_ref[STEP : STEP + 1, :LANES] = step[...]
    pack_ref[DECAY : DECAY + 1, :LANES] = decay[...]


def norm_row(pack_ref, half):
    return jnp.concatenate([pack_ref[NORM : NORM + 1, :half], pack_ref[NORM + 1 : NORM + 2, :half]], axis=1)


def front_kernel(
    where_ref,
    x_ref,
    halo_ref,
    tok_ref,
    pack_ref,
    spread_ref,
    w0,
    w1,
    w2,
    w3,
    w4,
    w5,
    normed_ref,
    inv_ref,
    pre_ref,
    conv_x_ref,
    conv_s_ref,
    raw_ref,
    step_ref,
    cum_ref,
    entry_ref,
    rate_ref,
    end_ref,
    end_rate_ref,
    weights,
    sems,
    ext,
    cols,
    state,
    total,
):
    rows, width = conv_x_ref.shape
    length, model = x_ref.shape
    both = width + 2 * NSTATE
    chunk = pl.program_id(0)
    held = front_refs((w0, w1, w2, w3, w4, w5))

    @pl.when(chunk == 0)
    def _():
        start_weights(where_ref, held, weights, sems)
        gain = norm_row(pack_ref, model // 2)

        def normalize(v):
            inv = lax.rsqrt(jnp.mean(v * v, axis=-1, keepdims=True) + EPS)
            return (v * inv * gain).astype(BF16), inv

        for r in range(length // rows):
            at = slice(r * rows, (r + 1) * rows)
            normed, inv = normalize(x_ref[at, :].astype(F32))
            normed_ref[at, :] = normed
            inv_ref[at, :] = jnp.broadcast_to(inv, (rows, LANES))
        halo, _ = normalize(halo_ref[...].astype(F32))
        wait_weights(where_ref, held, weights, sems)
        ext[0:8, :] = mm(halo, weights[:, :both])
        cols[...] = mm(normed_ref[...], weights[...])
        state[...] = jnp.zeros_like(state)
        total[...] = jnp.ones_like(total)

    @pl.when(chunk > 0)
    def _():
        ext[0:8, :] = ext[rows : rows + 8, :]

    here = pl.ds(pl.multiple_of(chunk * rows, rows), rows)
    pre = cols[here, :both]
    raw = cols[here, both:]
    pre_ref[...] = pre
    raw_ref[...] = raw
    ext[8 : 8 + rows, :] = pre
    conv = pack_ref[BIAS : BIAS + 1, :] + pack_ref[TAPS : TAPS + 1, :] * pre
    for k in range(1, CONV):
        conv = conv + tok_ref[:, k : k + 1] * (
            pack_ref[TAPS + k : TAPS + k + 1, :] * ext[8 - k : 8 - k + rows, :]
        )
    conv_x_ref[...] = conv[:, :width]
    conv_s_ref[...] = conv[:, width:]
    conv_x = conv[:, :width]
    conv_b = conv[:, width : width + NSTATE]
    values = conv_x * logistic(conv_x)
    b_part = conv_b * logistic(conv_b)
    step = softplus(raw + pack_ref[STEP : STEP + 1, :LANES])
    decay = -jnp.exp(pack_ref[DECAY : DECAY + 1, :LANES]) * step
    cum = exact(lower_ones(rows).astype(F32), decay - BREAK * tok_ref[:, 0:1])
    step_ref[...] = step
    cum_ref[...] = cum
    last = cum[rows - 1 : rows, :]
    spread_matrix = spread_ref[...]
    carried = (spread(jnp.exp(last - cum) * step, spread_matrix) * values).astype(BF16)
    before = state[...]
    entry_ref[0] = before
    rate_ref[0] = total[...]
    kept = spread(jnp.exp(cum[rows - 8 : rows, :]), spread_matrix)[7:8, :]
    grown = mm(both_halves(b_part), carried, TN)
    new_state = kept * before + (grown[:NSTATE] + grown[NSTATE:])
    state[...] = new_state
    end_ref[...] = new_state
    new_total = total[...] * jnp.exp(last)
    total[...] = new_total
    end_rate_ref[...] = new_total


def front_call(where, x, halo, tok, pack, spread_matrix, weights):
    length, model = x.shape
    all_width = weights[-1].shape[1]
    both = all_width - LANES
    width = both - 2 * NSTATE
    rows = min(SPAN, length)
    chunks = length // rows
    return pl.pallas_call(
        front_kernel,
        grid=(chunks,),
        in_specs=[
            scalars_of(),
            whole_of(length, model),
            whole_of(8, model),
            chunk_of(rows, LANES),
            whole_of(PACK, both),
            whole_of(2 * LANES, width),
        ]
        + anywhere(6),
        out_specs=[
            whole_of(length, model),
            whole_of(length, LANES),
            chunk_of(rows, both),
            chunk_of(rows, width),
            chunk_of(rows, 2 * NSTATE),
            chunk_of(rows, LANES),
            chunk_of(rows, LANES),
            chunk_of(rows, LANES),
            stack_of(NSTATE, width),
            stack_of(8, LANES),
            whole_of(NSTATE, width),
            whole_of(8, LANES),
        ],
        out_shape=[
            shape(length, model, dtype=BF16),
            shape(length, LANES),
            shape(length, both),
            shape(length, width),
            shape(length, 2 * NSTATE),
            shape(length, LANES),
            shape(length, LANES),
            shape(length, LANES),
            shape(chunks, NSTATE, width),
            shape(chunks, 8, LANES),
            shape(NSTATE, width),
            shape(8, LANES),
        ],
        scratch_shapes=weight_scratch(weights)
        + [
            pltpu.VMEM((rows + 8, both), F32),
            pltpu.VMEM((length, all_width), F32),
            pltpu.VMEM((NSTATE, width), F32),
            pltpu.VMEM((8, LANES), F32),
        ],
        compiler_params=params_of(),
        cost_estimate=cost(2 * length * model * all_width, 24 * length * width),
        name="front",
    )(where, x, halo, tok, pack, spread_matrix, *weights)


def project_kernel(kind, where_ref, a_ref, w0, w1, w2, w3, out_ref, weights, sems):
    tile = out_ref.shape[1]

    @pl.when(pl.program_id(0) == 0)
    def _():
        load_weights(where_ref, kind((w0, w1, w2, w3)), weights, sems)

    at = pl.ds(pl.multiple_of(pl.program_id(0) * tile, tile), tile)
    out_ref[...] = mm(a_ref[...], weights[:, at])


def project_call(where, a, kind, weights):
    length, model = a.shape
    width = weights[-1].shape[1]
    tile = 2 * LANES
    return pl.pallas_call(
        functools.partial(project_kernel, kind),
        grid=(width // tile,),
        in_specs=[scalars_of(), whole_of(length, model)] + anywhere(4),
        out_specs=pl.BlockSpec((length, tile), lambda n: (0, n)),
        out_shape=shape(length, width),
        scratch_shapes=weight_scratch(weights),
        compiler_params=params_of(),
        cost_estimate=cost(2 * length * model * width, 4 * length * width),
        name="project",
    )(where, a, *weights)


def mix_kernel(conv_x_ref, conv_s_ref, step_ref, cum_ref, entry_ref, spread_ref, y_ref):
    rows, width = conv_x_ref.shape
    conv_x = conv_x_ref[...]
    conv_s = conv_s_ref[...]
    values = conv_x * logistic(conv_x)
    bc = conv_s * logistic(conv_s)
    b_part, c_part = bc[:, :NSTATE], bc[:, NSTATE:]
    cum = cum_ref[...]
    spread_matrix = spread_ref[...]
    grown = spread(jnp.exp(cum), spread_matrix)
    stepped = (spread(step_ref[...], spread_matrix) * values).astype(BF16)
    from_entry = grown * mm(both_halves(c_part), twice(entry_ref[0].astype(BF16)))
    scores = jnp.where(lower_ones(rows), mm(*triple(c_part, b_part), NT), 0.0)
    cum_t = cum.T
    first, second = pair_masks()
    for j in range(width // LANES):
        parts = []
        for h in (2 * j, 2 * j + 1):
            gap = jnp.minimum(cum[:, h : h + 1] - cum_t[h : h + 1, :], 0.0)
            parts.append((scores * jnp.exp(gap)).astype(BF16))
        pair = stepped[:, j * LANES : (j + 1) * LANES]
        y_ref[:, j * LANES : (j + 1) * LANES] = from_entry[:, j * LANES : (j + 1) * LANES] + mm(
            jnp.concatenate(parts, axis=1), jnp.concatenate([pair * first, pair * second], axis=0)
        )


def mix_call(conv_x, conv_s, step, cum, entry, spread_matrix):
    length, width = conv_x.shape
    rows = min(SPAN, length)
    return pl.pallas_call(
        mix_kernel,
        grid=(length // rows,),
        in_specs=[
            chunk_of(rows, width),
            chunk_of(rows, 2 * NSTATE),
            chunk_of(rows, LANES),
            chunk_of(rows, LANES),
            stack_of(NSTATE, width),
            whole_of(2 * LANES, width),
        ],
        out_specs=chunk_of(rows, width),
        out_shape=shape(length, width),
        compiler_params=params_of(),
        cost_estimate=cost(16 * length * rows * width, 12 * length * width),
        name="mix",
    )(conv_x, conv_s, step, cum, entry, spread_matrix)


def gate_kernel(
    with_dot,
    y_ref,
    z_ref,
    conv_x_ref,
    conv_s_ref,
    cum_ref,
    rate_ref,
    entry_ref,
    pack_ref,
    spread_ref,
    *refs,
):
    comb_ref, gated_ref, sums_ref = refs[-3:]
    rows, width = y_ref.shape
    spread_matrix = spread_ref[...]
    c_part = conv_s_ref[:, NSTATE:]
    c_part = c_part * logistic(c_part)
    reach = spread(rate_ref[0], spread_matrix)[0:1, :]
    grown = spread(jnp.exp(cum_ref[...]), spread_matrix)
    mixed = y_ref[...] + grown * mm(
        both_halves(c_part), twice((reach * entry_ref[...]).astype(BF16))
    )
    conv = conv_x_ref[...]
    comb = mixed + pack_ref[SKIP : SKIP + 1, :width] * (conv * logistic(conv))
    comb_ref[...] = comb
    z = z_ref[...]
    gated = comb * (z * logistic(z))
    gated_ref[...] = gated
    square = jnp.sum(gated * gated, axis=1, keepdims=True)
    lane = lax.broadcasted_iota(jnp.int32, (rows, LANES), 1)
    sums = jnp.where(lane == 0, square, 0.0)
    if with_dot:
        gain = pack_ref[GATED : GATED + 1, :width]
        dot = jnp.sum(gated * gain * refs[0][...], axis=1, keepdims=True)
        sums = jnp.where(lane == 1, dot, sums)
    sums_ref[...] = sums.T[0:8, :]


def gate_call(y, z, conv_x, conv_s, cum, rate, entry, pack, spread_matrix, *grad_scaled):
    length, width = y.shape
    rows = min(SPAN, length)
    chunks = length // rows
    return pl.pallas_call(
        functools.partial(gate_kernel, bool(grad_scaled)),
        grid=(chunks,),
        in_specs=[
            chunk_of(rows, width),
            chunk_of(rows, width),
            chunk_of(rows, width),
            chunk_of(rows, 2 * NSTATE),
            chunk_of(rows, LANES),
            stack_of(8, LANES),
            whole_of(NSTATE, width),
            whole_of(*pack.shape),
            whole_of(2 * LANES, width),
        ]
        + [chunk_of(rows, width)] * len(grad_scaled),
        out_specs=[chunk_of(rows, width), chunk_of(rows, width), lanes_of(rows)],
        out_shape=[shape(length, width), shape(length, width), shape(8, length)],
        compiler_params=params_of(),
        cost_estimate=cost(4 * length * NSTATE * width, 28 * length * width),
        name="gate",
    )(y, z, conv_x, conv_s, cum, rate, entry, pack, spread_matrix, *grad_scaled)


def columns(lanes):
    rows = lanes.shape[1]
    return jnp.concatenate([lanes, jnp.zeros((LANES - 8, rows), F32)], axis=0).T


def out_kernel(
    where_ref, gated_ref, sums_ref, pack_ref, w0, w1, w2, w3, low_ref, other_ref, branch_ref, weights, sems, full
):
    tile = branch_ref.shape[1]
    length, width = gated_ref.shape
    half = width // 2

    @pl.when(pl.program_id(0) == 0)
    def _():
        start_weights(where_ref, out_refs((w0, w1, w2, w3)), weights, sems)
        gain = pack_ref[GATED : GATED + 1, :width]
        rows = min(SPAN, length)
        for r in range(length // rows):
            at = slice(r * rows, (r + 1) * rows)
            inv = lax.rsqrt(columns(sums_ref[:, at])[:, 0:1] * (1.0 / INNER) + EPS)
            full[at, :] = (gated_ref[at, :] * inv * gain).astype(BF16)
        low_ref[...] = full[:, pl.ds(pl.multiple_of(where_ref[2] * half, LANES), half)]
        other_ref[...] = full[:, pl.ds(pl.multiple_of((1 - where_ref[2]) * half, LANES), half)]
        wait_weights(where_ref, out_refs((w0, w1, w2, w3)), weights, sems)

    at = pl.ds(pl.multiple_of(pl.program_id(0) * tile, tile), tile)
    branch_ref[...] = mm(full[...], weights[at, :], NT)


def out_call(where, gated, sums, pack, weights):
    length, width = gated.shape
    model = 4 * weights[-1].shape[0]
    tile = model // 4
    half = width // 2
    return pl.pallas_call(
        out_kernel,
        grid=(model // tile,),
        in_specs=[scalars_of(), whole_of(length, width), whole_of(8, length), whole_of(*pack.shape)]
        + anywhere(4),
        out_specs=[
            whole_of(length, half),
            whole_of(length, half),
            pl.BlockSpec((length, tile), lambda n: (0, n)),
        ],
        out_shape=[
            shape(length, half, dtype=BF16),
            shape(length, half, dtype=BF16),
            shape(length, model),
        ],
        scratch_shapes=weight_scratch(weights) + [pltpu.VMEM((length, width), BF16)],
        compiler_params=params_of(),
        cost_estimate=cost(2 * length * model * width, 8 * length * width),
        name="out",
    )(where, gated, sums, pack, *weights)


def finish_kernel(last, where_ref, grad_ref, g_ref, x_ref, inv_ref, pack_ref, *refs):
    rows, model = grad_ref.shape
    chunk = pl.program_id(0)
    gain = norm_row(pack_ref, model // 2)
    x = x_ref[...].astype(F32)
    inv = inv_ref[:, 0:1]
    weighted = grad_ref[...].astype(F32) * gain
    mean = jnp.mean(weighted * x, axis=-1, keepdims=True)
    result = g_ref[...].astype(F32) + inv * weighted - x * (inv * inv * inv * mean)
    if last:
        refs[0][...] = result
        return
    branch_ref, sums_ref, w0, w1, w2, w3, out_ref, low_ref, scaled_ref, new_sums_ref, weights, sems = refs
    candidates = out_refs((w0, w1, w2, w3))

    @pl.when(chunk == 0)
    def _():
        start_weights(where_ref, candidates, weights, sems)

    out_ref[...] = result
    low = result.astype(BF16)
    low_ref[pl.ds(pl.multiple_of(chunk * rows, rows), rows), :] = low
    dot = jnp.sum(low.astype(F32) * branch_ref[...], axis=1, keepdims=True)
    square = columns(sums_ref[...])[:, 0:1]
    dot = dot / lax.rsqrt(square * (1.0 / INNER) + EPS)
    lane = lax.broadcasted_iota(jnp.int32, (rows, LANES), 1)
    sums = jnp.where(lane == 0, square, jnp.where(lane == 1, dot, 0.0))
    new_sums_ref[...] = sums.T[0:8, :]

    @pl.when(chunk == pl.num_programs(0) - 1)
    def _():
        wait_weights(where_ref, candidates, weights, sems)
        scaled_ref[...] = mm(low_ref[...], weights[...])


def finish_call(where, grad, g, x, inv, pack, *more):
    length, model = grad.shape
    rows = min(SPAN, length)
    last = not more
    in_specs = [
        scalars_of(),
        chunk_of(rows, model),
        chunk_of(rows, model),
        chunk_of(rows, model),
        chunk_of(rows, LANES),
        whole_of(*pack.shape),
    ]
    out_specs = [chunk_of(rows, model)]
    out_shape = [shape(length, model)]
    scratch = []
    if more:
        branch, sums, *weights = more
        width = weights[-1].shape[1]
        in_specs += [chunk_of(rows, model), lanes_of(rows)] + anywhere(4)
        out_specs += [whole_of(length, model), whole_of(length, width), lanes_of(rows)]
        out_shape += [shape(length, model, dtype=BF16), shape(length, width), shape(8, length)]
        scratch = weight_scratch(weights)
    return pl.pallas_call(
        functools.partial(finish_kernel, last),
        grid=(length // rows,),
        in_specs=in_specs,
        out_specs=out_specs,
        out_shape=out_shape,
        scratch_shapes=scratch,
        compiler_params=params_of(),
        cost_estimate=cost(length * model * 800, 16 * length * model),
        name="finish",
    )(where, grad, g, x, inv, pack, *more)


def gate_back_kernel(
    scaled_ref,
    comb_ref,
    z_ref,
    conv_s_ref,
    cum_ref,
    sums_ref,
    pack_ref,
    spread_ref,
    dmix_ref,
    dz_ref,
    adj_ref,
    rate_ref,
    begin_ref,
    gain_ref,
    state,
    total,
):
    chunk = pl.program_id(0)
    rows, width = z_ref.shape

    @pl.when(chunk == 0)
    def _():
        state[...] = jnp.zeros_like(state)
        total[...] = jnp.ones_like(total)
        gain_ref[...] = jnp.zeros_like(gain_ref)

    sums = columns(sums_ref[...])
    inv = lax.rsqrt(sums[:, 0:1] * (1.0 / INNER) + EPS)
    dot = sums[:, 1:2]
    grad_scaled = scaled_ref[...]
    comb = comb_ref[...]
    z = z_ref[...]
    sig = logistic(z)
    act = z * sig
    gated = comb * act
    gain_ref[0:1, :] += jnp.sum(grad_scaled * (gated * inv), axis=0, keepdims=True)
    grad_gated = inv * (grad_scaled * pack_ref[GATED : GATED + 1, :width]) - gated * (inv * inv * inv * dot * (1.0 / INNER))
    dmix = grad_gated * act
    dmix_ref[...] = dmix
    dz_ref[...] = (grad_gated * comb * (sig * (1.0 + z * (1.0 - sig)))).astype(BF16)
    c_part = conv_s_ref[:, NSTATE:]
    c_part = c_part * logistic(c_part)
    cum = cum_ref[...]
    grown = spread(jnp.exp(cum), spread_ref[...])
    held = state[...]
    adj_ref[0] = held
    rate_ref[0] = total[...]
    added = mm(both_halves(c_part), (grown * dmix).astype(BF16), TN)
    new_state = grown[rows - 1 : rows, :] * held + (added[:NSTATE] + added[NSTATE:])
    state[...] = new_state
    begin_ref[...] = new_state
    total[...] = total[...] * jnp.exp(cum[rows - 1 : rows, :])


def gate_back_call(grad_scaled, comb, z, conv_s, cum, sums, pack, spread_matrix):
    length, width = z.shape
    rows = min(SPAN, length)
    chunks = length // rows
    return pl.pallas_call(
        gate_back_kernel,
        grid=(chunks,),
        in_specs=[
            chunk_of(rows, width, chunks),
            chunk_of(rows, width, chunks),
            chunk_of(rows, width, chunks),
            chunk_of(rows, 2 * NSTATE, chunks),
            chunk_of(rows, LANES, chunks),
            lanes_of(rows, chunks),
            whole_of(*pack.shape),
            whole_of(2 * LANES, width),
        ],
        out_specs=[
            chunk_of(rows, width, chunks),
            chunk_of(rows, width, chunks),
            stack_of(NSTATE, width, chunks),
            stack_of(8, LANES, chunks),
            whole_of(NSTATE, width),
            whole_of(8, width),
        ],
        out_shape=[
            shape(length, width),
            shape(length, width, dtype=BF16),
            shape(chunks, NSTATE, width),
            shape(chunks, 8, LANES),
            shape(NSTATE, width),
            shape(8, width),
        ],
        scratch_shapes=[pltpu.VMEM((NSTATE, width), F32), pltpu.VMEM((8, LANES), F32)],
        compiler_params=params_of(),
        cost_estimate=cost(4 * length * NSTATE * width, 28 * length * width),
        name="gate_back",
    )(grad_scaled, comb, z, conv_s, cum, sums, pack, spread_matrix)


def mix_back_kernel(
    conv_x_ref,
    conv_s_ref,
    dmix_ref,
    step_ref,
    cum_ref,
    entry_ref,
    entry_rate_ref,
    entry_in_ref,
    adj_ref,
    spread_ref,
    gather_ref,
    ones_ref,
    grad_step_ref,
    grad_b_ref,
    grad_c_ref,
    decay_ref,
    skip_ref,
    flows,
):
    chunk = pl.program_id(0)
    rows, width = conv_x_ref.shape

    @pl.when(chunk == 0)
    def _():
        skip_ref[...] = jnp.zeros_like(skip_ref)

    spread_matrix = spread_ref[...]
    gather_matrix = gather_ref[...]
    conv = conv_x_ref[...]
    values = conv * logistic(conv)
    conv_s = conv_s_ref[...]
    bc = conv_s * logistic(conv_s)
    b_part, c_part = bc[:, :NSTATE], bc[:, NSTATE:]
    cum = cum_ref[...]
    dmix = dmix_ref[...]
    dmix_low = dmix.astype(BF16)
    last = cum[rows - 1 : rows, :]
    grown = spread(jnp.exp(cum), spread_matrix)
    left_wide = spread(jnp.exp(last - cum), spread_matrix)
    entry = entry_ref[0] + spread(entry_rate_ref[0], spread_matrix)[0:1, :] * entry_in_ref[...]
    adj = adj_ref[0]
    entry_low = entry.astype(BF16)
    adj_low = adj.astype(BF16)
    skip_ref[0:1, :] += jnp.sum(dmix * values, axis=0, keepdims=True)

    stepped = spread(step_ref[...], spread_matrix) * values
    stepped_low = stepped.astype(BF16)
    from_entry = grown * mm(both_halves(c_part), twice(entry_low))
    later = left_wide * mm(both_halves(b_part), twice(adj_low))
    grad_c = mm((grown * dmix).astype(BF16), entry_low, NT)
    grad_b = mm((left_wide * stepped).astype(BF16), adj_low, NT)

    t_after = lower_ones(rows).T
    scores = jnp.where(t_after, mm(*triple(b_part, c_part), NT), 0.0)
    cum_t = cum.T
    first, second = pair_masks()
    grad_scores = jnp.zeros((rows, rows), F32)
    for j in range(width // LANES):
        lanes = slice(j * LANES, (j + 1) * LANES)
        dmix_pair = dmix_low[:, lanes]
        stacked = jnp.concatenate([dmix_pair * first, dmix_pair * second], axis=0)
        grad_pair = mm(stepped_low[:, lanes], stacked, NT)
        parts = []
        for i in range(2):
            h = 2 * j + i
            gap = jnp.minimum(cum_t[h : h + 1, :] - cum[:, h : h + 1], 0.0)
            reach = jnp.exp(gap)
            mixing = scores * reach
            grad_mixing = grad_pair[:, i * rows : (i + 1) * rows]
            grad_scores = grad_scores + grad_mixing * reach
            flows[:, h * rows : (h + 1) * rows] = (grad_mixing * mixing).astype(BF16)
            parts.append(mixing.astype(BF16))
        grad_step_ref[:, lanes] = later[:, lanes] + mm(jnp.concatenate(parts, axis=1), stacked)
    grad_scores = jnp.where(t_after, grad_scores, 0.0)
    s_top, s_rest = halves(grad_scores)
    c_top, c_rest = halves(c_part)
    b_top, b_rest = halves(b_part)
    grad_b_ref[...] = grad_b + mm(
        jnp.concatenate([s_top, s_rest, s_top], axis=1),
        jnp.concatenate([c_top, c_top, c_rest], axis=0),
    )
    grad_c_ref[...] = grad_c + mm(
        jnp.concatenate([s_top, s_rest, s_top], axis=0),
        jnp.concatenate([b_top, b_top, b_rest], axis=0),
        TN,
    )

    out_flow = gather_heads(dmix * from_entry, gather_matrix)
    in_flow = gather_heads(later * stepped, gather_matrix)
    kept = jnp.sum(entry * adj, axis=0, keepdims=True) * grown[rows - 1 : rows, :]
    kept = gather_heads(jnp.broadcast_to(kept, (8, width)), gather_matrix)[0:1, :]
    flow = flows[...]
    source = mm(flow, ones_ref[...])
    target = mm(jnp.ones((8, rows), BF16), flow)
    heads = width // HEAD_DIM
    target = jnp.concatenate(
        [target[0:1, h * rows : (h + 1) * rows] for h in range(heads)]
        + [jnp.zeros((LANES - heads, rows), F32)],
        axis=0,
    ).T
    after = exact(t_after.astype(F32), target - source + out_flow)
    before = exact(lower_ones(rows).astype(F32), in_flow) - in_flow
    decay_ref[...] = kept + after + before


def mix_back_call(kept, dmix, adj, consts):
    conv_x, conv_s, step, cum, _, entry, rate, entry_in = kept
    length, width = conv_x.shape
    rows = min(SPAN, length)
    chunks = length // rows
    spread_matrix, gather_matrix, ones = consts
    head_count = width // HEAD_DIM
    return pl.pallas_call(
        mix_back_kernel,
        grid=(chunks,),
        in_specs=[
            chunk_of(rows, width),
            chunk_of(rows, 2 * NSTATE),
            chunk_of(rows, width),
            chunk_of(rows, LANES),
            chunk_of(rows, LANES),
            stack_of(NSTATE, width),
            stack_of(8, LANES),
            whole_of(NSTATE, width),
            stack_of(NSTATE, width),
            whole_of(2 * LANES, width),
            whole_of(2 * width, LANES),
            whole_of(head_count * rows, LANES),
        ],
        out_specs=[
            chunk_of(rows, width),
            chunk_of(rows, NSTATE),
            chunk_of(rows, NSTATE),
            chunk_of(rows, LANES),
            whole_of(8, width),
        ],
        out_shape=[
            shape(length, width),
            shape(length, NSTATE),
            shape(length, NSTATE),
            shape(length, LANES),
            shape(8, width),
        ],
        scratch_shapes=[pltpu.VMEM((rows, head_count * rows), BF16)],
        compiler_params=params_of(),
        cost_estimate=cost(40 * length * rows * width, 20 * length * width),
        name="mix_back",
    )(conv_x, conv_s, dmix, step, cum, entry, rate, entry_in, adj, spread_matrix, gather_matrix, ones)


def later_kernel(
    conv_x_ref,
    conv_s_ref,
    dmix_ref,
    step_ref,
    cum_ref,
    raw_ref,
    entry_ref,
    entry_rate_ref,
    entry_in_ref,
    adj_rate_ref,
    adj_in_ref,
    grad_step_ref,
    grad_b_ref,
    grad_c_ref,
    decay_ref,
    pack_ref,
    spread_ref,
    gather_ref,
    grad_ref,
    grad_raw_ref,
    small_ref,
):
    chunk = pl.program_id(0)
    rows, width = conv_x_ref.shape

    @pl.when(chunk == 0)
    def _():
        small_ref[...] = jnp.zeros_like(small_ref)

    spread_matrix = spread_ref[...]
    gather_matrix = gather_ref[...]
    conv = conv_x_ref[...]
    sig = logistic(conv)
    values = conv * sig
    conv_s = conv_s_ref[...]
    sig_s = logistic(conv_s)
    b_part = conv_s[:, :NSTATE] * sig_s[:, :NSTATE]
    step = step_ref[...]
    cum = cum_ref[...]
    last = cum[rows - 1 : rows, :]
    step_wide = spread(step, spread_matrix)
    left_wide = spread(jnp.exp(last - cum), spread_matrix)
    kept = spread(jnp.exp(cum[rows - 8 : rows, :]), spread_matrix)[7:8, :]
    entry = entry_ref[0] + spread(entry_rate_ref[0], spread_matrix)[0:1, :] * entry_in_ref[...]
    adj = spread(adj_rate_ref[0], spread_matrix)[0:1, :] * adj_in_ref[...]
    adj_low = adj.astype(BF16)
    stepped = step_wide * values
    later = left_wide * mm(both_halves(b_part), twice(adj_low))
    grad_b = grad_b_ref[...] + mm((left_wide * stepped).astype(BF16), adj_low, NT)
    in_flow = gather_heads(later * stepped, gather_matrix)
    kept = jnp.sum(entry * adj, axis=0, keepdims=True) * kept
    kept = gather_heads(jnp.broadcast_to(kept, (8, width)), gather_matrix)[0:1, :]
    before = exact(lower_ones(rows).astype(F32), in_flow) - in_flow
    grad_decay = decay_ref[...] + kept + before
    grad_stepped = grad_step_ref[...] + later
    grad_step = gather_heads(grad_stepped * values, gather_matrix)
    grad_values = step_wide * grad_stepped + pack_ref[SKIP : SKIP + 1, :width] * dmix_ref[...]
    grad_ref[:, :width] = grad_values * (sig * (1.0 + conv * (1.0 - sig)))
    slope = sig_s * (1.0 + conv_s * (1.0 - sig_s))
    grad_ref[:, width : width + NSTATE] = grad_b * slope[:, :NSTATE]
    grad_ref[:, width + NSTATE :] = grad_c_ref[...] * slope[:, NSTATE:]
    rate = -jnp.exp(pack_ref[DECAY : DECAY + 1, :LANES])
    grad_raw = (grad_step + rate * grad_decay) * logistic(raw_ref[...] + pack_ref[STEP : STEP + 1, :LANES])
    grad_raw_ref[...] = grad_raw.astype(BF16)
    small_ref[0:1, :] += jnp.sum(grad_raw, axis=0, keepdims=True)
    small_ref[1:2, :] += jnp.sum(grad_decay * (rate * step), axis=0, keepdims=True)


def later_call(kept, dmix, adj_rate, adj_in, parts, pack, consts):
    conv_x, conv_s, step, cum, raw, entry, rate, entry_in = kept
    length, width = conv_x.shape
    rows = min(SPAN, length)
    chunks = length // rows
    spread_matrix, gather_matrix, _ = consts
    return pl.pallas_call(
        later_kernel,
        grid=(chunks,),
        in_specs=[
            chunk_of(rows, width),
            chunk_of(rows, 2 * NSTATE),
            chunk_of(rows, width),
            chunk_of(rows, LANES),
            chunk_of(rows, LANES),
            chunk_of(rows, LANES),
            stack_of(NSTATE, width),
            stack_of(8, LANES),
            whole_of(NSTATE, width),
            stack_of(8, LANES),
            whole_of(NSTATE, width),
            chunk_of(rows, width),
            chunk_of(rows, NSTATE),
            chunk_of(rows, NSTATE),
            chunk_of(rows, LANES),
            whole_of(*pack.shape),
            whole_of(2 * LANES, width),
            whole_of(2 * width, LANES),
        ],
        out_specs=[chunk_of(rows, width + 2 * NSTATE), chunk_of(rows, LANES), whole_of(8, LANES)],
        out_shape=[
            shape(length, width + 2 * NSTATE),
            shape(length, LANES, dtype=BF16),
            shape(8, LANES),
        ],
        compiler_params=params_of(),
        cost_estimate=cost(8 * length * NSTATE * width, 24 * length * width),
        name="later",
    )(
        conv_x,
        conv_s,
        dmix,
        step,
        cum,
        raw,
        entry,
        rate,
        entry_in,
        adj_rate,
        adj_in,
        *parts,
        pack,
        spread_matrix,
        gather_matrix,
    )


def conv_back_kernel(
    chunks,
    where_ref,
    grad_ref,
    pre_ref,
    raw_ref,
    dz_ref,
    tok_ref,
    halo_ref,
    halo_tok_ref,
    pack_ref,
    x_ref,
    inv_ref,
    head_ref,
    skip_ref,
    gained_ref,
    gather_ref,
    f0,
    f1,
    f2,
    f3,
    f4,
    f5,
    z0,
    z1,
    z2,
    z3,
    keep_ref,
    send_ref,
    part_ref,
    small_ref,
    front,
    front_sems,
    gate,
    gate_sems,
    ext,
    ext_tok,
    grads,
):
    step = pl.program_id(0)
    rows, both = pre_ref.shape
    width = both - 2 * NSTATE
    half = width // 2
    tile = part_ref.shape[1]
    core = where_ref[2]
    held_front = front_refs((f0, f1, f2, f3, f4, f5))
    held_gate = gate_refs((z0, z1, z2, z3))

    @pl.when(step == 0)
    def _():
        start_weights(where_ref, held_front, front, front_sems)
        start_weights(where_ref, held_gate, gate, gate_sems)
        ext[rows : rows + 8, :] = halo_ref[...]
        ext_tok[rows : rows + 8, :] = halo_tok_ref[...]
        small_ref[...] = jnp.zeros_like(small_ref)

    @pl.when(jnp.logical_and(step > 0, step < chunks))
    def _():
        ext[rows : rows + 8, :] = ext[0:8, :]
        ext_tok[rows : rows + 8, :] = ext_tok[0:8, :]

    @pl.when(step < chunks)
    def _():
        grad = grad_ref[...]
        ext[0:rows, :] = grad
        ext_tok[0:rows, :] = tok_ref[...]
        pre = pre_ref[...]
        out = pack_ref[TAPS : TAPS + 1, :] * grad
        small_ref[TAPS : TAPS + 1, :] += jnp.sum(grad * pre, axis=0, keepdims=True)
        small_ref[BIAS : BIAS + 1, :] += jnp.sum(grad, axis=0, keepdims=True)
        for k in range(1, CONV):
            shifted = ext_tok[k : k + rows, k : k + 1] * ext[k : k + rows, :]
            out = out + pack_ref[TAPS + k : TAPS + k + 1, :] * shifted
            small_ref[TAPS + k : TAPS + k + 1, :] += jnp.sum(shifted * pre, axis=0, keepdims=True)
        out_x = out[:, :width].astype(BF16)
        s_top, s_rest = halves(out[:, width:])
        raw = raw_ref[...]
        dz = dz_ref[...]
        at = pl.ds(pl.multiple_of((chunks - 1 - step) * rows, rows), rows)
        grads[at, :] = jnp.concatenate([out_x, s_top, raw, dz, s_rest], axis=1)
        none = jnp.zeros((rows, LANES), BF16)
        for_lower = [dz[:, :half], out_x[:, :half], s_top, s_rest]
        for_upper = [dz[:, half:], out_x[:, half:], raw, none, none, none]

        @pl.when(core == 0)
        def _():
            keep_ref[...] = jnp.concatenate(for_lower, axis=1)
            send_ref[...] = jnp.concatenate(for_upper, axis=1)

        @pl.when(core == 1)
        def _():
            keep_ref[...] = jnp.concatenate(for_upper, axis=1)
            send_ref[...] = jnp.concatenate(for_lower, axis=1)

    @pl.when(step == chunks)
    def _():
        wait_weights(where_ref, held_front, front, front_sems)
        wait_weights(where_ref, held_gate, gate, gate_sems)
        skip = gather_heads(skip_ref[...], gather_ref[...])
        small_ref[SKIP : SKIP + 1, :LANES] = skip[0:1, :]
        small_ref[GATED : GATED + 1, :width] = gained_ref[0:1, :]
        small_ref[STEP : STEP + 2, :LANES] = head_ref[0:2, :]

    for n in range(2 * front.shape[0] // (2 * tile)):

        @pl.when(step == chunks + n)
        def _():
            at = slice(n * tile, (n + 1) * tile)
            part = (
                mm(grads[:, : both + LANES], front[at, :], NT)
                + mm(grads[:, both + LANES : both + LANES + width], gate[at, :], NT)
                + mm(grads[:, both + LANES + width :], front[at, width:both], NT)
            )
            part_ref[...] = part
            row = jnp.sum(part * (x_ref[...].astype(F32) * inv_ref[:, 0:1]), axis=0, keepdims=True)
            per_row = front.shape[0] // 2 // tile
            place = slice((n % per_row) * tile, (n % per_row + 1) * tile)
            small_ref[NORM + n // per_row : NORM + n // per_row + 1, place] = row


def conv_back_call(
    where, grad, pre, grad_raw, dz, tok, halo, halo_tok, pack, x, inv, head, skip, gained, gather_matrix, front, gate
):
    length, both = pre.shape
    width = both - 2 * NSTATE
    model = 4 * front[-1].shape[0]
    rows = min(SPAN, length)
    chunks = length // rows
    tile = model // 4
    out_width = width + 4 * NSTATE

    def chunk_spec(size):
        return pl.BlockSpec((rows, size), lambda c: (jnp.maximum(chunks - 1 - c, 0), 0))

    def tile_spec(rows_):
        return pl.BlockSpec((rows_, tile), lambda c: (0, jnp.maximum(c - chunks, 0)))

    return pl.pallas_call(
        functools.partial(conv_back_kernel, chunks),
        grid=(chunks + model // tile,),
        in_specs=[
            scalars_of(),
            chunk_spec(both),
            chunk_spec(both),
            chunk_spec(LANES),
            chunk_spec(width),
            chunk_spec(LANES),
            whole_of(8, both),
            whole_of(8, LANES),
            whole_of(*pack.shape),
            tile_spec(length),
            whole_of(length, LANES),
            whole_of(8, LANES),
            whole_of(8, width),
            whole_of(8, width),
            whole_of(2 * width, LANES),
        ]
        + anywhere(10),
        out_specs=[
            chunk_spec(out_width),
            chunk_spec(out_width),
            tile_spec(length),
            whole_of(*pack.shape),
        ],
        out_shape=[
            shape(length, out_width, dtype=BF16),
            shape(length, out_width, dtype=BF16),
            shape(length, model),
            shape(*pack.shape),
        ],
        scratch_shapes=weight_scratch(front)
        + weight_scratch(gate)
        + [
            pltpu.VMEM((rows + 8, both), F32),
            pltpu.VMEM((rows + 8, LANES), F32),
            pltpu.VMEM((length, both + LANES + width + 2 * NSTATE), BF16),
        ],
        compiler_params=params_of(),
        cost_estimate=cost(4 * length * model * both, 24 * length * width),
        name="conv_back",
    )(where, grad, pre, grad_raw, dz, tok, halo, halo_tok, pack, x, inv, head, skip, gained, gather_matrix, *front, *gate)


def swap(value, axis):
    return lax.ppermute(value, axis, [(0, 1), (1, 0)])


def shifted_along(value, axis, by):
    count = lax.axis_size(axis)
    return lax.ppermute(
        value, axis, [(i, i + by) for i in range(count) if 0 <= i + by < count]
    )


def sum_over(value, axis):
    if lax.axis_size(axis) == 2:
        return value + swap(value, axis)
    return lax.psum(value, axis)


def after(value, *earlier):
    return lax.optimization_barrier((value,) + earlier)[0]


def carried_state(state, rate_wide, axis, backward):
    count = lax.axis_size(axis)
    if count == 2:
        return shifted_along(state, axis, -1 if backward else 1)
    here = lax.axis_index(axis)
    states = lax.all_gather(state, axis)
    rates = lax.all_gather(rate_wide, axis)
    result = jnp.zeros_like(state)
    for k in range(count):
        at = count - 1 - k if backward else k
        reached = at > here if backward else at < here
        result = jnp.where(reached, rates[at] * result + states[at], result)
    return result


def small_sum(value):
    count = lax.axis_size("tensor")
    total = value
    for by in range(1, count):
        total = total + lax.ppermute(
            value, "tensor", [(i, (i + by) % count) for i in range(count)]
        )
    return total


def tensor_sum(value, kind, pieces):
    index = lax.axis_index("tensor")
    odd = index % 2
    pair = [(0, 1), (1, 0), (2, 3), (3, 2)]
    cross = [(0, 2), (2, 0), (1, 3), (3, 1)]
    rows = value.shape[0] // (2 * pieces)
    results = []
    for p in range(pieces):
        base = 2 * rows * p
        give = lax.dynamic_slice_in_dim(value, base + (1 - odd) * rows, rows, 0).astype(kind)
        keep = lax.dynamic_slice_in_dim(value, base + odd * rows, rows, 0)
        part = (keep + lax.ppermute(give, "tensor", pair).astype(F32)).astype(kind)
        total = part.astype(F32) + lax.ppermute(part, "tensor", cross).astype(F32)
        total = total.astype(kind)
        other = lax.ppermute(total, "tensor", pair)
        results.append(jnp.where(odd == 0, total, other))
        results.append(jnp.where(odd == 0, other, total))
    return jnp.concatenate(results, axis=0)


def scatter_sum(value, kind):
    return lax.psum_scatter(
        value.astype(kind), ("fsdp", "context"), scatter_dimension=0, tiled=False
    )


def shards(
    block_input,
    doc_start,
    cotangent,
    norm_gain,
    proj_main,
    proj_states,
    proj_step,
    conv_main,
    conv_main_bias,
    conv_states,
    conv_states_bias,
    step_bias,
    log_decay,
    skip_gain,
    gated_gain,
    proj_out,
):
    core = lax.axis_index("section")
    lower_core = core == 0
    length = block_input.shape[1]
    model = block_input.shape[2]
    heads = proj_step.shape[2]
    width = heads * HEAD_DIM
    half = width // 2
    both = width + 2 * NSTATE
    rows = min(SPAN, length)
    first = (1 - lax.axis_index("fsdp")).astype(jnp.int32)
    places = [
        jnp.stack([(core == layer).astype(jnp.int32), first, core.astype(jnp.int32)]) for layer in (0, 1)
    ]

    main_own = lax.optimization_barrier(proj_main[0].reshape(-1, 2 * width))
    rest_own = jnp.concatenate(
        [proj_states[0], jnp.pad(proj_step[0], ((0, 0), (0, LANES - heads)))], axis=1
    )
    out_own = proj_out[0]
    main_near = swap(main_own, "section")
    rest_near = swap(rest_own, "section")
    out_near = swap(out_own, "section")
    near_rows = main_own.shape[0]

    def half_of(layer, own, near):
        shard = jnp.where(core == layer, own, near)
        return lax.dynamic_slice_in_dim(shard, core * (near_rows // 2), near_rows // 2, 0)

    def across(piece):
        mine = swap(piece, "fsdp")
        return mine, swap(mine, "section")

    def front_piece(layer):
        return jnp.concatenate(
            [
                half_of(layer, main_own[:, width:], main_near[:, width:]),
                half_of(layer, rest_own, rest_near),
            ],
            axis=1,
        )

    def gate_piece(layer):
        return half_of(layer, main_own[:, :width], main_near[:, :width])

    def out_piece(layer):
        return half_of(layer, out_own, out_near)

    front_far0 = across(front_piece(0))
    gate_far0 = across(after(gate_piece(0), front_far0[0]))
    out_far0 = across(after(out_piece(0), gate_far0[0]))
    front_far1 = across(after(front_piece(1), out_far0[0]))
    out_far1 = across(after(out_piece(1), front_far1[0]))
    gate_far1 = across(after(gate_piece(1), out_far1[0]))
    mains = (main_own, main_near)
    fronts = [mains + (rest_own, rest_near) + far for far in (front_far0, front_far1)]
    gates = [mains + far for far in (gate_far0, gate_far1)]
    outs = [(out_own, out_near) + far for far in (out_far0, out_far1)]

    head_of = np.arange(width) // HEAD_DIM
    one_hot = (np.arange(LANES)[:, None] == head_of[None, :]).astype(np.float32)
    spread_matrix = jnp.asarray(np.concatenate([one_hot, one_hot], axis=0), BF16)
    gather_matrix = jnp.asarray(np.concatenate([one_hot.T, one_hot.T], axis=0), BF16)
    row_head = np.arange(heads * rows) // rows
    ones = jnp.asarray((row_head[:, None] == np.arange(LANES)[None, :]).astype(np.float32), BF16)
    consts = (spread_matrix, gather_matrix, ones)

    tokens = lax.dynamic_index_in_dim(block_input, core, 0, keepdims=False)
    cot = lax.dynamic_index_in_dim(cotangent, core, 0, keepdims=False)
    starts = lax.dynamic_index_in_dim(doc_start, core, 0, keepdims=False).astype(F32)
    earlier = shifted_along(starts[length - 8 :], "context", 1)
    later = shifted_along(starts[:8], "context", -1)
    line = jnp.concatenate([earlier, starts, later])
    keep = 1.0 - line
    one_back = keep[8:]
    two_back = one_back * keep[7:-1]
    three_back = two_back * keep[6:-2]
    tok_all = jnp.stack([line[8:], one_back, two_back, three_back], axis=1)
    tok_all = jnp.pad(tok_all, ((0, 0), (0, LANES - 4)))
    tok, tok_after = tok_all[:length], tok_all[length:]

    def head_lanes(row):
        return jnp.pad(row, ((0, 0), (0, LANES - heads)))

    pack_own = pl.pallas_call(pack_kernel, out_shape=shape(PACK, both), name="pack")(
        conv_main[0],
        conv_states[0],
        conv_main_bias,
        conv_states_bias,
        jnp.repeat(skip_gain, HEAD_DIM, axis=1),
        gated_gain,
        norm_gain,
        head_lanes(step_bias),
        head_lanes(log_decay),
    )
    pack_other = swap(pack_own, "section")
    packs = [jnp.where(core == layer, pack_own, pack_other) for layer in (0, 1)]

    def layer_forward(x, halo, layer, *grad_scaled):
        pack = packs[layer]
        place = places[layer]
        normed, inv, pre, conv_x, conv_s, raw, step, cum, entry, rate, end, end_rate = front_call(
            place, x, halo, tok, pack, spread_matrix, fronts[layer]
        )
        rate_wide = jnp.repeat(end_rate[0:1, :heads], HEAD_DIM, axis=1)
        entry_in = carried_state(end, rate_wide, "context", False)
        z = project_call(place, normed, gate_refs, gates[layer])
        y = mix_call(conv_x, conv_s, step, cum, entry, spread_matrix)
        comb, gated, sums = gate_call(
            y, z, conv_x, conv_s, cum, rate, entry_in, pack, spread_matrix, *grad_scaled
        )
        sums = small_sum(sums)
        low_keep, low_send, branch = out_call(place, gated, sums, pack, outs[layer])
        kept = (conv_x, conv_s, step, cum, raw, entry, rate, entry_in)
        return branch, (normed, inv, pre, z, kept, comb, (low_keep, low_send), sums, rate_wide)

    def layer_backward(grad_scaled, sums, x, forward, layer):
        normed, inv, pre, z, kept, comb, _, _, rate_wide = forward
        pack = packs[layer]
        dmix, dz, adj, adj_rate, begin, gained = gate_back_call(
            grad_scaled, comb, z, kept[1], kept[3], sums, pack, spread_matrix
        )
        adj_in = carried_state(begin, rate_wide, "context", True)
        *parts, skip = mix_back_call(kept, dmix, adj, consts)
        grad, grad_raw, head = later_call(kept, dmix, adj_rate, adj_in, parts, pack, consts)
        edge = shifted_along(grad[:8], "context", -1)
        return conv_back_call(
            places[layer],
            grad,
            pre,
            grad_raw,
            dz,
            tok,
            edge,
            tok_after,
            pack,
            x,
            inv,
            head,
            skip,
            gained,
            gather_matrix,
            fronts[layer],
            gates[layer],
        )

    blocks = lax.axis_size("fsdp") * lax.axis_size("context")
    share = model // blocks

    def matrix_grads(normed, g_low, low, keep, send):
        received = swap(send, "section")
        normed_other = swap(normed, "section")
        low_keep, low_send = low
        low_received = swap(low_send, "section")
        g_other = swap(g_low, "section")
        cols = mm(normed, keep[:, :width], TN) + mm(normed_other, received[:, :width], TN)
        top = slice(width, width + 2 * NSTATE)
        rest = slice(width + 2 * NSTATE, width + 4 * NSTATE)
        states = (
            mm(normed, keep[:, top], TN)
            + mm(normed, keep[:, rest], TN)
            + mm(normed_other, received[:, top], TN)
            + mm(normed_other, received[:, rest], TN)
        )
        outer = mm(g_low, low_keep, TN) + mm(g_other, low_received, TN)
        states = scatter_sum(states.reshape(blocks, share, -1), F32)
        states = jnp.where(lower_core, lax.psum(states, "tensor"), states)
        matrices = jnp.concatenate([cols.astype(BF16), outer.astype(BF16)], axis=1)
        return states, scatter_sum(matrices.reshape(blocks, share, -1), BF16)

    halo0 = shifted_along(tokens[length - 8 :], "context", 1)
    branch0, forward0 = layer_forward(tokens, halo0, 0)
    edge0 = tokens[length - 8 :].astype(F32) + small_sum(branch0[length - 8 :])
    halo1 = shifted_along(edge0, "context", 1)
    branch0 = tensor_sum(branch0, jnp.float16, 2).astype(F32)
    x1 = tokens.astype(F32) + branch0
    grad_scaled1 = project_call(places[1], cot, out_refs, outs[1])
    branch1, forward1 = layer_forward(x1, halo1, 1, grad_scaled1)
    x2 = x1 + lax.psum(branch1.astype(BF16), "tensor").astype(F32)

    keep1, send1, part1, small1 = layer_backward(grad_scaled1, forward1[7], x1, forward1, 1)
    normed_grad1 = tensor_sum(part1, BF16, 2)
    grad1, g_low0, grad_scaled0, sums0 = finish_call(
        places[0], normed_grad1, cot, x1, forward1[1], packs[1], branch0, forward0[7], *outs[0]
    )
    keep0, send0, part0, small0 = layer_backward(grad_scaled0, sums0, tokens, forward0, 0)
    normed_grad0 = tensor_sum(part0, BF16, 2)
    grad0 = finish_call(places[0], normed_grad0, grad1, tokens, forward0[1], packs[0])[0]

    mats1 = matrix_grads(forward1[0], cot, forward1[6], keep1, send1)
    mats0 = matrix_grads(forward0[0], g_low0, forward0[6], keep0, send0)

    def to_layer(first, second, kind):
        mine = jnp.where(lower_core, first, second).astype(kind)
        theirs = swap(jnp.where(lower_core, second, first).astype(kind), "section")
        return jnp.where(lower_core, mine, theirs).astype(F32), jnp.where(lower_core, theirs, mine).astype(F32)

    grad_states, step_wide = to_layer(mats0[0], mats1[0], F32)
    lower, upper = to_layer(mats0[1], mats1[1], BF16)
    grad_main = jnp.stack(
        [
            jnp.concatenate([lower[:, :half], upper[:, :half]], axis=1),
            jnp.concatenate([lower[:, half:width], upper[:, half:width]], axis=1),
        ],
        axis=1,
    )
    grad_out = jnp.concatenate([lower[:, width:], upper[:, width:]], axis=1)

    row = np.arange(PACK)[:, None]
    lane = np.arange(both)[None, :]
    shared = ((row < SKIP) & (lane >= width)) | (row == NORM) | (row == NORM + 1)

    def over_tensor(small):
        return jnp.where(shared, small_sum(small), small)

    vector = jnp.where(lower_core, small0, small1) + swap(
        jnp.where(lower_core, small1, small0), "section"
    )
    vector = over_tensor(sum_over(sum_over(vector, "fsdp"), "context"))

    def to_sections(first, second):
        mine = jnp.where(lower_core, first, second)
        theirs = swap(jnp.where(lower_core, second, first), "section")
        return jnp.stack([jnp.where(lower_core, mine, theirs), jnp.where(lower_core, theirs, mine)])

    layer_out = to_sections(x1, x2)
    layer_in_grad = to_sections(grad0, grad1)
    return (
        layer_out[None],
        layer_in_grad[None],
        vector[NORM : NORM + 2, : model // 2].reshape(1, model),
        grad_main[None],
        grad_states[None],
        step_wide[None, :, :heads],
        vector[None, TAPS : TAPS + CONV, :width],
        vector[BIAS : BIAS + 1, :width],
        vector[None, TAPS : TAPS + CONV, width:],
        vector[BIAS : BIAS + 1, width:],
        vector[STEP : STEP + 1, :heads],
        vector[DECAY : DECAY + 1, :heads],
        vector[SKIP : SKIP + 1, :heads],
        vector[GATED : GATED + 1, :width],
        grad_out[None],
    )


def solution(mesh):
    placed = (
        P("fsdp", "context", None),
        P("fsdp", "context"),
        P("fsdp", "context", None),
        P("section", None),
        P("section", "fsdp", None, "tensor"),
        P("section", "fsdp", None),
        P("section", "fsdp", "tensor"),
        P("section", None, "tensor"),
        P("section", "tensor"),
        P("section", None, None),
        P("section", None),
        P("section", "tensor"),
        P("section", "tensor"),
        P("section", "tensor"),
        P("section", "tensor"),
        P("section", "fsdp", "tensor"),
    )
    return jax.shard_map(
        shards,
        mesh=mesh,
        in_specs=placed,
        out_specs=(
            P("section", "fsdp", "context", None),
            P("section", "fsdp", "context", None),
            P("section", None),
            P("section", ("fsdp", "context"), None, "tensor"),
            P("section", ("fsdp", "context"), None),
            P("section", ("fsdp", "context"), "tensor"),
            P("section", None, "tensor"),
            P("section", "tensor"),
            P("section", None, None),
            P("section", None),
            P("section", "tensor"),
            P("section", "tensor"),
            P("section", "tensor"),
            P("section", "tensor"),
            P("section", ("fsdp", "context"), "tensor"),
        ),
        check_vma=False,
    )
```

```python
import functools

import jax
import jax.numpy as jnp
import numpy as np
from jax import lax
from jax.experimental import pallas as pl
from jax.experimental.pallas import tpu as pltpu
from jax.sharding import PartitionSpec as P

HEAD_DIM = 64
NSTATE = 128
CONV = 4
SPAN = 128
INNER = 3072
LANES = 128
EPS = 1e-05
BREAK = 128.0
HIGH = lax.Precision.HIGHEST
F32 = jnp.float32
BF16 = jnp.bfloat16

NT = (((1,), (1,)), ((), ()))
TN = (((0,), (0,)), ((), ()))


def mm(a, b, dims=(((1,), (0,)), ((), ()))):
    return lax.dot_general(a, b, dims, preferred_element_type=F32)


def exact(a, b):
    return lax.dot_general(a, b, (((1,), (0,)), ((), ())), precision=HIGH, preferred_element_type=F32)


def halves(a):
    top = a.astype(BF16)
    return top, (a - top.astype(F32)).astype(BF16)


def spread(a, spread_matrix):
    top, rest = halves(a)
    return mm(jnp.concatenate([top, rest], axis=1), spread_matrix)


def gather_heads(a, gather_matrix):
    top, rest = halves(a)
    return mm(jnp.concatenate([top, rest], axis=1), gather_matrix)


def logistic(v):
    return 0.5 * jnp.tanh(0.5 * v) + 0.5


def softplus(v):
    u = jnp.exp(-jnp.abs(v))
    small = u * (1.0 - u * (0.5 - u * (1.0 / 3.0)))
    return jnp.maximum(v, 0.0) + jnp.where(u < 1e-3, small, jnp.log(1.0 + u))


def lower_ones(rows):
    t = lax.broadcasted_iota(jnp.int32, (rows, rows), 0)
    s = lax.broadcasted_iota(jnp.int32, (rows, rows), 1)
    return t >= s


def pair_masks():
    lane = lax.broadcasted_iota(jnp.int32, (1, LANES), 1)
    first = (lane < HEAD_DIM).astype(BF16)
    return first, (1.0 - first.astype(F32)).astype(BF16)


def both_halves(a):
    top, rest = halves(a)
    return jnp.concatenate([top, rest], axis=1)


def triple(a, b):
    a_top, a_rest = halves(a)
    b_top, b_rest = halves(b)
    return (
        jnp.concatenate([a_top, a_rest, a_top], axis=1),
        jnp.concatenate([b_top, b_top, b_rest], axis=1),
    )


def twice(a):
    return jnp.concatenate([a, a], axis=0)


def chunk_of(rows, width, reverse=0):
    if reverse:
        return pl.BlockSpec((rows, width), lambda c: (reverse - 1 - c, 0))
    return pl.BlockSpec((rows, width), lambda c: (c, 0))


def lanes_of(rows, reverse=0):
    if reverse:
        return pl.BlockSpec((8, rows), lambda c: (0, reverse - 1 - c))
    return pl.BlockSpec((8, rows), lambda c: (0, c))


def stack_of(rows, width, reverse=0):
    if reverse:
        return pl.BlockSpec((1, rows, width), lambda c: (reverse - 1 - c, 0, 0))
    return pl.BlockSpec((1, rows, width), lambda c: (c, 0, 0))


def whole_of(rows, width):
    return pl.BlockSpec((rows, width), lambda c: (0, 0))


def scalars_of():
    return pl.BlockSpec(memory_space=pltpu.SMEM)


def anywhere(count):
    return [pl.BlockSpec(memory_space=pltpu.HBM)] * count


def params_of(mebibytes):
    return pltpu.CompilerParams(
        dimension_semantics=("arbitrary",), vmem_limit_bytes=mebibytes * 1024 * 1024
    )


def shape(*dims, dtype=F32):
    return jax.ShapeDtypeStruct(dims, dtype)


CORE, FIRST, ODD, RIGHT, ALONG_X, ALONG_Y = range(6)


def ordered_call(kernel, ahead, in_specs, **options):
    count, extra = len(in_specs), len(ahead)

    def body(*refs):
        kernel(*refs[:count], *refs[count + extra :])

    call = pl.pallas_call(
        body, in_specs=list(in_specs) + [pl.BlockSpec(memory_space=pl.ANY)] * extra, **options
    )
    return lambda *operands: call(*operands, *ahead)


def cost(flops, moved):
    return pl.CostEstimate(flops=1, bytes_accessed=1, transcendentals=0)


def weight_copies(spec, where_ref, refs, buffer, sems, held):
    first, core = where_ref[FIRST], where_ref[CORE]
    _, near, (far_start, far_size) = spec
    rows = buffer.shape[0] // 2
    near_at = pl.ds(pl.multiple_of((1 - first) * rows, rows), rows)
    far = first * rows
    step = rows // 2
    copies = []
    column = 0
    for n, (start, size) in enumerate(near):
        copies.append(
            pltpu.make_async_copy(
                refs[2 * n if held else 2 * n + 1].at[:, start : start + size],
                buffer.at[near_at, column : column + size],
                sems.at[len(copies)],
            )
        )
        column += size
    for ref, which in ((refs[-2], core), (refs[-1], 1 - core)):
        part = buffer.at[pl.ds(pl.multiple_of(far + which * step, step), step)]
        source = ref.at[:, far_start : far_start + far_size]
        copies.append(pltpu.make_async_copy(source, part, sems.at[len(copies)]))
    return copies


def start_weights(spec, where_ref, refs, buffer, sems):
    for held in (True, False):

        @pl.when((where_ref[CORE] == spec[0]) == held)
        def _():
            for copy in weight_copies(spec, where_ref, refs, buffer, sems, held):
                copy.start()


def wait_weights(spec, where_ref, refs, buffer, sems):
    for copy in weight_copies(spec, where_ref, refs, buffer, sems, True):
        copy.wait()


def load_weights(spec, where_ref, refs, buffer, sems):
    start_weights(spec, where_ref, refs, buffer, sems)
    wait_weights(spec, where_ref, refs, buffer, sems)


def weight_scratch(weights):
    (_, _, (_, width)), arrays = weights
    return [pltpu.VMEM((2 * arrays[0].shape[0], width), BF16), pltpu.SemaphoreType.DMA((4,))]


def pieces_kernel(layer, parts, where_ref, *refs):
    out_ref, sems = refs[-2:]
    rows = out_ref.shape[0]
    mine = pl.ds(pl.multiple_of(where_ref[CORE] * rows, rows), rows)

    def copies(held):
        column = 0
        for n, (array, start, size) in enumerate(parts):
            source = refs[2 * array if held else 2 * array + 1]
            yield pltpu.make_async_copy(
                source.at[mine, start : start + size], out_ref.at[:, column : column + size], sems.at[n]
            )
            column += size

    for held in (True, False):

        @pl.when((where_ref[CORE] == layer) == held)
        def _():
            for copy in copies(held):
                copy.start()

    for copy in copies(True):
        copy.wait()


def pieces_call(where, layer, parts, arrays, *ahead):
    rows = arrays[0].shape[0] // 2
    total = sum(size for _, _, size in parts)
    return ordered_call(
        functools.partial(pieces_kernel, layer, parts),
        ahead,
        in_specs=[scalars_of()] + anywhere(len(arrays)),
        out_specs=pl.BlockSpec(memory_space=pltpu.VMEM),
        out_shape=shape(rows, total, dtype=BF16),
        scratch_shapes=[pltpu.SemaphoreType.DMA((len(parts),))],
        compiler_params=pltpu.CompilerParams(vmem_limit_bytes=8 * 1024 * 1024),
        cost_estimate=cost(0, 4 * rows * total),
        name="pieces",
    )(where, *arrays)


def joined(where_ref, refs, at, digits=(ODD, RIGHT)):
    quarter = refs[0].shape[0]
    rows = []
    for n in range(at.start // quarter, at.stop // quarter):
        half, place = divmod(n, 2)
        own, other = refs[2 * half][...].astype(F32), refs[2 * half + 1][...].astype(F32)
        rows.append(jnp.where(where_ref[digits[half]] == place, own, other))
    return rows[0] if len(rows) == 1 else jnp.concatenate(rows, axis=0)


def put_quarters(where_ref, value, refs, digits=(ODD, RIGHT)):
    quarter = value.shape[0] // 4
    for half in range(2):
        digit = where_ref[digits[half]]
        first = value[2 * half * quarter : (2 * half + 1) * quarter]
        second = value[(2 * half + 1) * quarter : (2 * half + 2) * quarter]
        refs[2 * half][...] = jnp.where(digit == 1, first, second).astype(refs[2 * half].dtype)
        refs[2 * half + 1][...] = jnp.where(digit == 1, second, first).astype(refs[2 * half + 1].dtype)


def quarter_shapes(length, model, kind):
    return [shape(length // 4, model, dtype=kind), shape(length // 4, model)] * 2


def merge_kernel(*refs):
    count = len(refs) // 3
    for a_ref, b_ref, out_ref in zip(refs[:count], refs[count : 2 * count], refs[2 * count :]):
        out_ref[...] = (a_ref[...].astype(F32) + b_ref[...].astype(F32)).astype(out_ref.dtype)


def merge_call(firsts, seconds, kind, *ahead):
    return ordered_call(
        merge_kernel,
        ahead,
        in_specs=[pl.BlockSpec(memory_space=pltpu.VMEM)] * (2 * len(firsts)),
        out_specs=[pl.BlockSpec(memory_space=pltpu.VMEM)] * len(firsts),
        out_shape=[shape(*a.shape, dtype=kind) for a in firsts],
        compiler_params=pltpu.CompilerParams(vmem_limit_bytes=10 * 1024 * 1024),
        cost_estimate=cost(0, 0),
        name="merge",
    )(*firsts, *seconds)


def hold_kernel(*refs):
    count = len(refs) // 2
    for in_ref, out_ref in zip(refs[:count], refs[count:]):
        out_ref[...] = in_ref[...]


def hold_call(arrays, *ahead):
    return ordered_call(
        hold_kernel,
        ahead,
        in_specs=[pl.BlockSpec(memory_space=pltpu.VMEM)] * len(arrays),
        out_specs=[pl.BlockSpec(memory_space=pltpu.VMEM)] * len(arrays),
        out_shape=[shape(*v.shape, dtype=v.dtype) for v in arrays],
        compiler_params=pltpu.CompilerParams(vmem_limit_bytes=12 * 1024 * 1024),
        cost_estimate=cost(0, 0),
        name="hold",
    )(*arrays)


def vector_kernel(mask_ref, a_ref, b_ref, c_ref, d_ref, out_ref):
    total = a_ref[...] + b_ref[...] + c_ref[...] + d_ref[...]
    out_ref[...] = jnp.where(mask_ref[...] > 0.0, total, a_ref[...])


def vector_call(mask, values):
    return pl.pallas_call(
        vector_kernel,
        in_specs=[pl.BlockSpec(memory_space=pltpu.VMEM)] * 5,
        out_specs=pl.BlockSpec(memory_space=pltpu.VMEM),
        out_shape=shape(*mask.shape),
        compiler_params=pltpu.CompilerParams(vmem_limit_bytes=4 * 1024 * 1024),
        cost_estimate=cost(0, 0),
        name="vector",
    )(mask, *values)


def join_kernel(where_ref, x_ref, t0, o0, t1, o1, out_ref):
    length = x_ref.shape[0]
    rows = min(SPAN, length)
    for r in range(length // rows):
        at = slice(r * rows, (r + 1) * rows)
        out_ref[at, :] = x_ref[at, :] + joined(where_ref, (t0, o0, t1, o1), at, (ODD, ODD))


def join_call(where, x, quarters, *ahead):
    return ordered_call(
        join_kernel,
        ahead,
        in_specs=[scalars_of()] + [pl.BlockSpec(memory_space=pltpu.VMEM)] * 5,
        out_specs=pl.BlockSpec(memory_space=pltpu.VMEM),
        out_shape=shape(*x.shape),
        compiler_params=pltpu.CompilerParams(vmem_limit_bytes=16 * 1024 * 1024),
        cost_estimate=cost(0, 0),
        name="join",
    )(where, x, *quarters)


TAPS, BIAS, SKIP, GATED, NORM, STEP, DECAY, PACK = 0, 4, 8, 9, 10, 12, 13, 16


def pack_kernel(taps_a, taps_b, bias_a, bias_b, skip, gated, norm, step, decay, pack_ref):
    width = taps_a.shape[1]
    half = norm.shape[1] // 2
    pack_ref[...] = jnp.zeros_like(pack_ref)
    pack_ref[TAPS : TAPS + CONV, :width] = taps_a[...]
    pack_ref[TAPS : TAPS + CONV, width:] = taps_b[...]
    pack_ref[BIAS : BIAS + 1, :width] = bias_a[...]
    pack_ref[BIAS : BIAS + 1, width:] = bias_b[...]
    pack_ref[SKIP : SKIP + 1, :width] = skip[...]
    pack_ref[GATED : GATED + 1, :width] = gated[...]
    pack_ref[NORM : NORM + 1, :half] = norm[:, :half]
    pack_ref[NORM + 1 : NORM + 2, :half] = norm[:, half:]
    pack_ref[STEP : STEP + 1, :LANES] = step[...]
    pack_ref[DECAY : DECAY + 1, :LANES] = decay[...]


def norm_row(pack_ref, half):
    return jnp.concatenate([pack_ref[NORM : NORM + 1, :half], pack_ref[NORM + 1 : NORM + 2, :half]], axis=1)


def front_kernel(
    spec,
    where_ref,
    x_ref,
    halo_ref,
    tok_ref,
    pack_ref,
    spread_ref,
    w0,
    w1,
    w2,
    w3,
    w4,
    w5,
    *refs,
):
    if spec[0] == 1:
        quarters, refs = refs[:4], refs[4:]
    else:
        quarters = None
    front_body(spec, where_ref, x_ref, halo_ref, tok_ref, pack_ref, spread_ref, (w0, w1, w2, w3, w4, w5), quarters, *refs)


def front_body(
    spec,
    where_ref,
    x_ref,
    halo_ref,
    tok_ref,
    pack_ref,
    spread_ref,
    held,
    quarters,
    sum_ref,
    normed_ref,
    inv_ref,
    pre_ref,
    conv_x_ref,
    conv_s_ref,
    raw_ref,
    step_ref,
    cum_ref,
    entry_ref,
    rate_ref,
    end_ref,
    end_rate_ref,
    weights,
    sems,
    ext,
    cols,
    state,
    total,
):
    rows, width = conv_x_ref.shape
    length, model = x_ref.shape
    both = width + 2 * NSTATE
    chunk = pl.program_id(0)

    @pl.when(chunk == 0)
    def _():
        start_weights(spec, where_ref, held, weights, sems)
        gain = norm_row(pack_ref, model // 2)

        def normalize(v):
            inv = lax.rsqrt(jnp.mean(v * v, axis=-1, keepdims=True) + EPS)
            return (v * inv * gain).astype(BF16), inv

        for r in range(length // rows):
            at = slice(r * rows, (r + 1) * rows)
            x = x_ref[at, :].astype(F32)
            if quarters is not None:
                x = x + joined(where_ref, quarters, at)
                sum_ref[at, :] = x
            normed, inv = normalize(x)
            normed_ref[at, :] = normed
            inv_ref[at, :] = jnp.broadcast_to(inv, (rows, LANES))
        halo, _ = normalize(halo_ref[...].astype(F32))
        wait_weights(spec, where_ref, held, weights, sems)
        ext[0:8, :] = mm(halo, weights[:, :both])
        cols[...] = mm(normed_ref[...], weights[...])
        state[...] = jnp.zeros_like(state)
        total[...] = jnp.ones_like(total)

    @pl.when(chunk > 0)
    def _():
        ext[0:8, :] = ext[rows : rows + 8, :]

    here = pl.ds(pl.multiple_of(chunk * rows, rows), rows)
    pre = cols[here, :both]
    raw = cols[here, both:]
    pre_ref[...] = pre
    raw_ref[...] = raw
    ext[8 : 8 + rows, :] = pre
    conv = pack_ref[BIAS : BIAS + 1, :] + pack_ref[TAPS : TAPS + 1, :] * pre
    for k in range(1, CONV):
        conv = conv + tok_ref[:, k : k + 1] * (
            pack_ref[TAPS + k : TAPS + k + 1, :] * ext[8 - k : 8 - k + rows, :]
        )
    conv_x_ref[...] = conv[:, :width]
    conv_s_ref[...] = conv[:, width:]
    conv_x = conv[:, :width]
    conv_b = conv[:, width : width + NSTATE]
    values = conv_x * logistic(conv_x)
    b_part = conv_b * logistic(conv_b)
    step = softplus(raw + pack_ref[STEP : STEP + 1, :LANES])
    decay = -jnp.exp(pack_ref[DECAY : DECAY + 1, :LANES]) * step
    cum = exact(lower_ones(rows).astype(F32), decay - BREAK * tok_ref[:, 0:1])
    step_ref[...] = step
    cum_ref[...] = cum
    last = cum[rows - 1 : rows, :]
    spread_matrix = spread_ref[...]
    carried = (spread(jnp.exp(last - cum) * step, spread_matrix) * values).astype(BF16)
    before = state[...]
    entry_ref[0] = before
    rate_ref[0] = total[...]
    kept = spread(jnp.exp(cum[rows - 8 : rows, :]), spread_matrix)[7:8, :]
    grown = mm(both_halves(b_part), carried, TN)
    new_state = kept * before + (grown[:NSTATE] + grown[NSTATE:])
    state[...] = new_state
    end_ref[...] = new_state
    new_total = total[...] * jnp.exp(last)
    total[...] = new_total
    end_rate_ref[...] = new_total


def front_call(where, x, halo, tok, pack, spread_matrix, weights, quarters, *ahead):
    length, model = x.shape
    all_width = weights[0][2][1]
    both = all_width - LANES
    width = both - 2 * NSTATE
    rows = min(SPAN, length)
    chunks = length // rows
    return ordered_call(
        functools.partial(front_kernel, weights[0]),
        ahead,
        grid=(chunks,),
        in_specs=[
            scalars_of(),
            whole_of(length, model),
            whole_of(8, model),
            chunk_of(rows, LANES),
            whole_of(PACK, both),
            whole_of(2 * LANES, width),
        ]
        + anywhere(6)
        + [whole_of(length // 4, model)] * len(quarters),
        out_specs=[
            whole_of(length, model) if quarters else whole_of(8, model),
            whole_of(length, model),
            whole_of(length, LANES),
            chunk_of(rows, both),
            chunk_of(rows, width),
            chunk_of(rows, 2 * NSTATE),
            chunk_of(rows, LANES),
            chunk_of(rows, LANES),
            chunk_of(rows, LANES),
            stack_of(NSTATE, width),
            stack_of(8, LANES),
            whole_of(NSTATE, width),
            whole_of(8, LANES),
        ],
        out_shape=[
            shape(length, model) if quarters else shape(8, model),
            shape(length, model, dtype=BF16),
            shape(length, LANES),
            shape(length, both),
            shape(length, width),
            shape(length, 2 * NSTATE),
            shape(length, LANES),
            shape(length, LANES),
            shape(length, LANES),
            shape(chunks, NSTATE, width),
            shape(chunks, 8, LANES),
            shape(NSTATE, width),
            shape(8, LANES),
        ],
        scratch_shapes=weight_scratch(weights)
        + [
            pltpu.VMEM((rows + 8, both), F32),
            pltpu.VMEM((length, all_width), F32),
            pltpu.VMEM((NSTATE, width), F32),
            pltpu.VMEM((8, LANES), F32),
        ],
        compiler_params=params_of(32),
        cost_estimate=cost(2 * length * model * all_width, 24 * length * width),
        name="front",
    )(where, x, halo, tok, pack, spread_matrix, *weights[1], *quarters)


def project_kernel(spec, where_ref, a_ref, w0, w1, w2, w3, out_ref, weights, sems):
    tile = out_ref.shape[1]

    @pl.when(pl.program_id(0) == 0)
    def _():
        load_weights(spec, where_ref, (w0, w1, w2, w3), weights, sems)

    at = pl.ds(pl.multiple_of(pl.program_id(0) * tile, tile), tile)
    out_ref[...] = mm(a_ref[...], weights[:, at])


def project_call(where, a, weights, *ahead):
    length, model = a.shape
    width = weights[0][2][1]
    tile = 2 * LANES
    return ordered_call(
        functools.partial(project_kernel, weights[0]),
        ahead,
        grid=(width // tile,),
        in_specs=[scalars_of(), whole_of(length, model)] + anywhere(4),
        out_specs=pl.BlockSpec((length, tile), lambda n: (0, n)),
        out_shape=shape(length, width),
        scratch_shapes=weight_scratch(weights),
        compiler_params=params_of(12),
        cost_estimate=cost(2 * length * model * width, 4 * length * width),
        name="project",
    )(where, a, *weights[1])


def mix_kernel(conv_x_ref, conv_s_ref, step_ref, cum_ref, entry_ref, spread_ref, y_ref):
    rows, width = conv_x_ref.shape
    conv_x = conv_x_ref[...]
    conv_s = conv_s_ref[...]
    values = conv_x * logistic(conv_x)
    bc = conv_s * logistic(conv_s)
    b_part, c_part = bc[:, :NSTATE], bc[:, NSTATE:]
    cum = cum_ref[...]
    spread_matrix = spread_ref[...]
    grown = spread(jnp.exp(cum), spread_matrix)
    stepped = (spread(step_ref[...], spread_matrix) * values).astype(BF16)
    from_entry = grown * mm(both_halves(c_part), twice(entry_ref[0].astype(BF16)))
    scores = jnp.where(lower_ones(rows), mm(*triple(c_part, b_part), NT), 0.0)
    cum_t = cum.T
    first, second = pair_masks()
    for j in range(width // LANES):
        parts = []
        for h in (2 * j, 2 * j + 1):
            gap = jnp.minimum(cum[:, h : h + 1] - cum_t[h : h + 1, :], 0.0)
            parts.append((scores * jnp.exp(gap)).astype(BF16))
        pair = stepped[:, j * LANES : (j + 1) * LANES]
        y_ref[:, j * LANES : (j + 1) * LANES] = from_entry[:, j * LANES : (j + 1) * LANES] + mm(
            jnp.concatenate(parts, axis=1), jnp.concatenate([pair * first, pair * second], axis=0)
        )


def mix_call(conv_x, conv_s, step, cum, entry, spread_matrix, *ahead):
    length, width = conv_x.shape
    rows = min(SPAN, length)
    return ordered_call(
        mix_kernel,
        ahead,
        grid=(length // rows,),
        in_specs=[
            chunk_of(rows, width),
            chunk_of(rows, 2 * NSTATE),
            chunk_of(rows, LANES),
            chunk_of(rows, LANES),
            stack_of(NSTATE, width),
            whole_of(2 * LANES, width),
        ],
        out_specs=chunk_of(rows, width),
        out_shape=shape(length, width),
        compiler_params=params_of(12),
        cost_estimate=cost(16 * length * rows * width, 12 * length * width),
        name="mix",
    )(conv_x, conv_s, step, cum, entry, spread_matrix)


def gate_kernel(
    with_dot,
    y_ref,
    z_ref,
    conv_x_ref,
    conv_s_ref,
    cum_ref,
    rate_ref,
    entry_ref,
    pack_ref,
    spread_ref,
    *refs,
):
    comb_ref, gated_ref, sums_ref = refs[-3:]
    rows, width = y_ref.shape
    spread_matrix = spread_ref[...]
    c_part = conv_s_ref[:, NSTATE:]
    c_part = c_part * logistic(c_part)
    reach = spread(rate_ref[0], spread_matrix)[0:1, :]
    grown = spread(jnp.exp(cum_ref[...]), spread_matrix)
    mixed = y_ref[...] + grown * mm(
        both_halves(c_part), twice((reach * entry_ref[...]).astype(BF16))
    )
    conv = conv_x_ref[...]
    comb = mixed + pack_ref[SKIP : SKIP + 1, :width] * (conv * logistic(conv))
    comb_ref[...] = comb
    z = z_ref[...]
    gated = comb * (z * logistic(z))
    gated_ref[...] = gated
    square = jnp.sum(gated * gated, axis=1, keepdims=True)
    lane = lax.broadcasted_iota(jnp.int32, (rows, LANES), 1)
    sums = jnp.where(lane == 0, square, 0.0)
    if with_dot:
        gain = pack_ref[GATED : GATED + 1, :width]
        dot = jnp.sum(gated * gain * refs[0][...], axis=1, keepdims=True)
        sums = jnp.where(lane == 1, dot, sums)
    sums_ref[...] = sums.T[0:8, :]


def gate_call(y, z, conv_x, conv_s, cum, rate, entry, pack, spread_matrix, *grad_scaled):
    length, width = y.shape
    rows = min(SPAN, length)
    chunks = length // rows
    return pl.pallas_call(
        functools.partial(gate_kernel, bool(grad_scaled)),
        grid=(chunks,),
        in_specs=[
            chunk_of(rows, width),
            chunk_of(rows, width),
            chunk_of(rows, width),
            chunk_of(rows, 2 * NSTATE),
            chunk_of(rows, LANES),
            stack_of(8, LANES),
            whole_of(NSTATE, width),
            whole_of(*pack.shape),
            whole_of(2 * LANES, width),
        ]
        + [chunk_of(rows, width)] * len(grad_scaled),
        out_specs=[chunk_of(rows, width), chunk_of(rows, width), lanes_of(rows)],
        out_shape=[shape(length, width), shape(length, width), shape(8, length)],
        compiler_params=params_of(12),
        cost_estimate=cost(4 * length * NSTATE * width, 28 * length * width),
        name="gate",
    )(y, z, conv_x, conv_s, cum, rate, entry, pack, spread_matrix, *grad_scaled)


def columns(lanes):
    rows = lanes.shape[1]
    return jnp.concatenate([lanes, jnp.zeros((LANES - 8, rows), F32)], axis=0).T


def out_kernel(
    spec, where_ref, gated_ref, sums_ref, pack_ref, w0, w1, w2, w3, low_ref, g0, k0, g1, k1, edge_ref, weights, sems
):
    tile = edge_ref.shape[1]
    length, width = gated_ref.shape

    @pl.when(pl.program_id(0) == 0)
    def _():
        start_weights(spec, where_ref, (w0, w1, w2, w3), weights, sems)
        gain = pack_ref[GATED : GATED + 1, :width]
        rows = min(SPAN, length)
        for r in range(length // rows):
            at = slice(r * rows, (r + 1) * rows)
            inv = lax.rsqrt(columns(sums_ref[:, at])[:, 0:1] * (1.0 / INNER) + EPS)
            low_ref[at, :] = (gated_ref[at, :] * inv * gain).astype(BF16)
        wait_weights(spec, where_ref, (w0, w1, w2, w3), weights, sems)

    at = pl.ds(pl.multiple_of(pl.program_id(0) * tile, tile), tile)
    branch = mm(low_ref[...], weights[at, :], NT)
    put_quarters(where_ref, branch, (g0, k0, g1, k1), (ODD, (RIGHT, ODD)[spec[0]]))
    edge_ref[...] = branch[length - 8 :]


def out_call(where, gated, sums, pack, weights, kind, *ahead):
    length, width = gated.shape
    model = 2 * weights[1][0].shape[0]
    tile = model // 4
    return ordered_call(
        functools.partial(out_kernel, weights[0]),
        ahead,
        grid=(model // tile,),
        in_specs=[scalars_of(), whole_of(length, width), whole_of(8, length), whole_of(*pack.shape)]
        + anywhere(4),
        out_specs=[
            whole_of(length, width),
        ]
        + [pl.BlockSpec((length // 4, tile), lambda n: (0, n))] * 4
        + [pl.BlockSpec((8, tile), lambda n: (0, n))],
        out_shape=[
            shape(length, width, dtype=BF16),
        ]
        + quarter_shapes(length, model, kind)
        + [shape(8, model)],
        scratch_shapes=weight_scratch(weights),
        compiler_params=params_of(14),
        cost_estimate=cost(2 * length * model * width, 8 * length * width),
        name="out",
    )(where, gated, sums, pack, *weights[1])


def finish_kernel(spec, where_ref, g_ref, x_ref, inv_ref, pack_ref, t0, o0, t1, o1, *refs):
    rows, model = g_ref.shape
    chunk = pl.program_id(0)
    *refs, grad = refs

    @pl.when(chunk == 0)
    def _():
        for r in range(grad.shape[0] // rows):
            at = slice(r * rows, (r + 1) * rows)
            grad[at, :] = joined(where_ref, (t0, o0, t1, o1), at).astype(BF16)

    gain = norm_row(pack_ref, model // 2)
    x = x_ref[...].astype(F32)
    inv = inv_ref[:, 0:1]
    weighted = grad[pl.ds(pl.multiple_of(chunk * rows, rows), rows), :].astype(F32) * gain
    mean = jnp.mean(weighted * x, axis=-1, keepdims=True)
    result = g_ref[...].astype(F32) + inv * weighted - x * (inv * inv * inv * mean)
    if spec is None:
        refs[0][...] = result
        return
    b0, b1, b2, b3, sums_ref, w0, w1, w2, w3, out_ref, low_ref, scaled_ref, new_sums_ref, weights, sems, branch = refs
    length = branch.shape[0]
    candidates = (w0, w1, w2, w3)

    @pl.when(chunk == 0)
    def _():
        start_weights(spec, where_ref, candidates, weights, sems)
        for r in range(length // rows):
            at = slice(r * rows, (r + 1) * rows)
            branch[at, :] = joined(where_ref, (b0, b1, b2, b3), at)

    out_ref[...] = result
    low = result.astype(BF16)
    low_ref[pl.ds(pl.multiple_of(chunk * rows, rows), rows), :] = low
    here = branch[pl.ds(pl.multiple_of(chunk * rows, rows), rows), :]
    dot = jnp.sum(low.astype(F32) * here, axis=1, keepdims=True)
    square = columns(sums_ref[...])[:, 0:1]
    dot = dot / lax.rsqrt(square * (1.0 / INNER) + EPS)
    lane = lax.broadcasted_iota(jnp.int32, (rows, LANES), 1)
    sums = jnp.where(lane == 0, square, jnp.where(lane == 1, dot, 0.0))
    new_sums_ref[...] = sums.T[0:8, :]

    @pl.when(chunk == pl.num_programs(0) - 1)
    def _():
        wait_weights(spec, where_ref, candidates, weights, sems)
        scaled_ref[...] = mm(low_ref[...], weights[...])


def finish_call(where, quarters, g, x, inv, pack, ahead, branch=None, sums=None, weights=None):
    length, model = g.shape
    rows = min(SPAN, length)
    in_specs = [
        scalars_of(),
        chunk_of(rows, model),
        chunk_of(rows, model),
        chunk_of(rows, LANES),
        whole_of(*pack.shape),
    ] + [whole_of(length // 4, model)] * 4
    out_specs = [chunk_of(rows, model)]
    out_shape = [shape(length, model)]
    scratch = [pltpu.VMEM((length, model), BF16)]
    more = ()
    if weights is not None:
        width = weights[0][2][1]
        in_specs += [whole_of(length // 4, model)] * 4 + [lanes_of(rows)] + anywhere(4)
        out_specs += [whole_of(length, model), whole_of(length, width), lanes_of(rows)]
        out_shape += [shape(length, model, dtype=BF16), shape(length, width), shape(8, length)]
        scratch = weight_scratch(weights) + [pltpu.VMEM((length, model), F32)] + scratch
        more = tuple(branch) + (sums,) + tuple(weights[1])
    return ordered_call(
        functools.partial(finish_kernel, None if weights is None else weights[0]),
        ahead,
        grid=(length // rows,),
        in_specs=in_specs,
        out_specs=out_specs,
        out_shape=out_shape,
        scratch_shapes=scratch,
        compiler_params=params_of(28),
        cost_estimate=cost(length * model * 800, 16 * length * model),
        name="finish",
    )(where, g, x, inv, pack, *quarters, *more)


def gate_back_kernel(
    scaled_ref,
    comb_ref,
    z_ref,
    conv_s_ref,
    cum_ref,
    sums_ref,
    pack_ref,
    spread_ref,
    dmix_ref,
    dz_ref,
    adj_ref,
    rate_ref,
    begin_ref,
    gain_ref,
    state,
    total,
):
    chunk = pl.program_id(0)
    rows, width = z_ref.shape

    @pl.when(chunk == 0)
    def _():
        state[...] = jnp.zeros_like(state)
        total[...] = jnp.ones_like(total)
        gain_ref[...] = jnp.zeros_like(gain_ref)

    sums = columns(sums_ref[...])
    inv = lax.rsqrt(sums[:, 0:1] * (1.0 / INNER) + EPS)
    dot = sums[:, 1:2]
    grad_scaled = scaled_ref[...]
    comb = comb_ref[...]
    z = z_ref[...]
    sig = logistic(z)
    act = z * sig
    gated = comb * act
    gain_ref[0:1, :] += jnp.sum(grad_scaled * (gated * inv), axis=0, keepdims=True)
    grad_gated = inv * (grad_scaled * pack_ref[GATED : GATED + 1, :width]) - gated * (inv * inv * inv * dot * (1.0 / INNER))
    dmix = grad_gated * act
    dmix_ref[...] = dmix
    dz_ref[...] = (grad_gated * comb * (sig * (1.0 + z * (1.0 - sig)))).astype(BF16)
    c_part = conv_s_ref[:, NSTATE:]
    c_part = c_part * logistic(c_part)
    cum = cum_ref[...]
    grown = spread(jnp.exp(cum), spread_ref[...])
    held = state[...]
    adj_ref[0] = held
    rate_ref[0] = total[...]
    added = mm(both_halves(c_part), (grown * dmix).astype(BF16), TN)
    new_state = grown[rows - 1 : rows, :] * held + (added[:NSTATE] + added[NSTATE:])
    state[...] = new_state
    begin_ref[...] = new_state
    total[...] = total[...] * jnp.exp(cum[rows - 1 : rows, :])


def gate_back_call(grad_scaled, comb, z, conv_s, cum, sums, pack, spread_matrix):
    length, width = z.shape
    rows = min(SPAN, length)
    chunks = length // rows
    return pl.pallas_call(
        gate_back_kernel,
        grid=(chunks,),
        in_specs=[
            chunk_of(rows, width, chunks),
            chunk_of(rows, width, chunks),
            chunk_of(rows, width, chunks),
            chunk_of(rows, 2 * NSTATE, chunks),
            chunk_of(rows, LANES, chunks),
            lanes_of(rows, chunks),
            whole_of(*pack.shape),
            whole_of(2 * LANES, width),
        ],
        out_specs=[
            chunk_of(rows, width, chunks),
            chunk_of(rows, width, chunks),
            stack_of(NSTATE, width, chunks),
            stack_of(8, LANES, chunks),
            whole_of(NSTATE, width),
            whole_of(8, width),
        ],
        out_shape=[
            shape(length, width),
            shape(length, width, dtype=BF16),
            shape(chunks, NSTATE, width),
            shape(chunks, 8, LANES),
            shape(NSTATE, width),
            shape(8, width),
        ],
        scratch_shapes=[pltpu.VMEM((NSTATE, width), F32), pltpu.VMEM((8, LANES), F32)],
        compiler_params=params_of(12),
        cost_estimate=cost(4 * length * NSTATE * width, 28 * length * width),
        name="gate_back",
    )(grad_scaled, comb, z, conv_s, cum, sums, pack, spread_matrix)


def mix_back_kernel(
    conv_x_ref,
    conv_s_ref,
    dmix_ref,
    step_ref,
    cum_ref,
    entry_ref,
    entry_rate_ref,
    entry_in_ref,
    adj_ref,
    spread_ref,
    gather_ref,
    ones_ref,
    grad_step_ref,
    grad_b_ref,
    grad_c_ref,
    decay_ref,
    skip_ref,
    flows,
):
    chunk = pl.program_id(0)
    rows, width = conv_x_ref.shape

    @pl.when(chunk == 0)
    def _():
        skip_ref[...] = jnp.zeros_like(skip_ref)

    spread_matrix = spread_ref[...]
    gather_matrix = gather_ref[...]
    conv = conv_x_ref[...]
    values = conv * logistic(conv)
    conv_s = conv_s_ref[...]
    bc = conv_s * logistic(conv_s)
    b_part, c_part = bc[:, :NSTATE], bc[:, NSTATE:]
    cum = cum_ref[...]
    dmix = dmix_ref[...]
    dmix_low = dmix.astype(BF16)
    last = cum[rows - 1 : rows, :]
    grown = spread(jnp.exp(cum), spread_matrix)
    left_wide = spread(jnp.exp(last - cum), spread_matrix)
    entry = entry_ref[0] + spread(entry_rate_ref[0], spread_matrix)[0:1, :] * entry_in_ref[...]
    adj = adj_ref[0]
    entry_low = entry.astype(BF16)
    adj_low = adj.astype(BF16)
    skip_ref[0:1, :] += jnp.sum(dmix * values, axis=0, keepdims=True)

    stepped = spread(step_ref[...], spread_matrix) * values
    stepped_low = stepped.astype(BF16)
    from_entry = grown * mm(both_halves(c_part), twice(entry_low))
    later = left_wide * mm(both_halves(b_part), twice(adj_low))
    grad_c = mm((grown * dmix).astype(BF16), entry_low, NT)
    grad_b = mm((left_wide * stepped).astype(BF16), adj_low, NT)

    t_after = lower_ones(rows).T
    scores = jnp.where(t_after, mm(*triple(b_part, c_part), NT), 0.0)
    cum_t = cum.T
    first, second = pair_masks()
    grad_scores = jnp.zeros((rows, rows), F32)
    for j in range(width // LANES):
        lanes = slice(j * LANES, (j + 1) * LANES)
        dmix_pair = dmix_low[:, lanes]
        stacked = jnp.concatenate([dmix_pair * first, dmix_pair * second], axis=0)
        grad_pair = mm(stepped_low[:, lanes], stacked, NT)
        parts = []
        for i in range(2):
            h = 2 * j + i
            gap = jnp.minimum(cum_t[h : h + 1, :] - cum[:, h : h + 1], 0.0)
            reach = jnp.exp(gap)
            mixing = scores * reach
            grad_mixing = grad_pair[:, i * rows : (i + 1) * rows]
            grad_scores = grad_scores + grad_mixing * reach
            flows[:, h * rows : (h + 1) * rows] = (grad_mixing * mixing).astype(BF16)
            parts.append(mixing.astype(BF16))
        grad_step_ref[:, lanes] = later[:, lanes] + mm(jnp.concatenate(parts, axis=1), stacked)
    grad_scores = jnp.where(t_after, grad_scores, 0.0)
    s_top, s_rest = halves(grad_scores)
    c_top, c_rest = halves(c_part)
    b_top, b_rest = halves(b_part)
    grad_b_ref[...] = grad_b + mm(
        jnp.concatenate([s_top, s_rest, s_top], axis=1),
        jnp.concatenate([c_top, c_top, c_rest], axis=0),
    )
    grad_c_ref[...] = grad_c + mm(
        jnp.concatenate([s_top, s_rest, s_top], axis=0),
        jnp.concatenate([b_top, b_top, b_rest], axis=0),
        TN,
    )

    out_flow = gather_heads(dmix * from_entry, gather_matrix)
    in_flow = gather_heads(later * stepped, gather_matrix)
    kept = jnp.sum(entry * adj, axis=0, keepdims=True) * grown[rows - 1 : rows, :]
    kept = gather_heads(jnp.broadcast_to(kept, (8, width)), gather_matrix)[0:1, :]
    flow = flows[...]
    source = mm(flow, ones_ref[...])
    target = mm(jnp.ones((8, rows), BF16), flow)
    heads = width // HEAD_DIM
    target = jnp.concatenate(
        [target[0:1, h * rows : (h + 1) * rows] for h in range(heads)]
        + [jnp.zeros((LANES - heads, rows), F32)],
        axis=0,
    ).T
    after = exact(t_after.astype(F32), target - source + out_flow)
    before = exact(lower_ones(rows).astype(F32), in_flow) - in_flow
    decay_ref[...] = kept + after + before


def mix_back_call(kept, dmix, adj, consts, *ahead):
    conv_x, conv_s, step, cum, _, entry, rate, entry_in = kept
    length, width = conv_x.shape
    rows = min(SPAN, length)
    chunks = length // rows
    spread_matrix, gather_matrix, ones = consts
    head_count = width // HEAD_DIM
    return ordered_call(
        mix_back_kernel,
        ahead,
        grid=(chunks,),
        in_specs=[
            chunk_of(rows, width),
            chunk_of(rows, 2 * NSTATE),
            chunk_of(rows, width),
            chunk_of(rows, LANES),
            chunk_of(rows, LANES),
            stack_of(NSTATE, width),
            stack_of(8, LANES),
            whole_of(NSTATE, width),
            stack_of(NSTATE, width),
            whole_of(2 * LANES, width),
            whole_of(2 * width, LANES),
            whole_of(head_count * rows, LANES),
        ],
        out_specs=[
            chunk_of(rows, width),
            chunk_of(rows, NSTATE),
            chunk_of(rows, NSTATE),
            chunk_of(rows, LANES),
            whole_of(8, width),
        ],
        out_shape=[
            shape(length, width),
            shape(length, NSTATE),
            shape(length, NSTATE),
            shape(length, LANES),
            shape(8, width),
        ],
        scratch_shapes=[pltpu.VMEM((rows, head_count * rows), BF16)],
        compiler_params=params_of(14),
        cost_estimate=cost(40 * length * rows * width, 20 * length * width),
        name="mix_back",
    )(conv_x, conv_s, dmix, step, cum, entry, rate, entry_in, adj, spread_matrix, gather_matrix, ones)


def later_kernel(
    conv_x_ref,
    conv_s_ref,
    dmix_ref,
    step_ref,
    cum_ref,
    raw_ref,
    entry_ref,
    entry_rate_ref,
    entry_in_ref,
    adj_rate_ref,
    adj_in_ref,
    grad_step_ref,
    grad_b_ref,
    grad_c_ref,
    decay_ref,
    pack_ref,
    spread_ref,
    gather_ref,
    grad_ref,
    grad_raw_ref,
    small_ref,
):
    chunk = pl.program_id(0)
    rows, width = conv_x_ref.shape

    @pl.when(chunk == 0)
    def _():
        small_ref[...] = jnp.zeros_like(small_ref)

    spread_matrix = spread_ref[...]
    gather_matrix = gather_ref[...]
    conv = conv_x_ref[...]
    sig = logistic(conv)
    values = conv * sig
    conv_s = conv_s_ref[...]
    sig_s = logistic(conv_s)
    b_part = conv_s[:, :NSTATE] * sig_s[:, :NSTATE]
    step = step_ref[...]
    cum = cum_ref[...]
    last = cum[rows - 1 : rows, :]
    step_wide = spread(step, spread_matrix)
    left_wide = spread(jnp.exp(last - cum), spread_matrix)
    kept = spread(jnp.exp(cum[rows - 8 : rows, :]), spread_matrix)[7:8, :]
    entry = entry_ref[0] + spread(entry_rate_ref[0], spread_matrix)[0:1, :] * entry_in_ref[...]
    adj = spread(adj_rate_ref[0], spread_matrix)[0:1, :] * adj_in_ref[...]
    adj_low = adj.astype(BF16)
    stepped = step_wide * values
    later = left_wide * mm(both_halves(b_part), twice(adj_low))
    grad_b = grad_b_ref[...] + mm((left_wide * stepped).astype(BF16), adj_low, NT)
    in_flow = gather_heads(later * stepped, gather_matrix)
    kept = jnp.sum(entry * adj, axis=0, keepdims=True) * kept
    kept = gather_heads(jnp.broadcast_to(kept, (8, width)), gather_matrix)[0:1, :]
    before = exact(lower_ones(rows).astype(F32), in_flow) - in_flow
    grad_decay = decay_ref[...] + kept + before
    grad_stepped = grad_step_ref[...] + later
    grad_step = gather_heads(grad_stepped * values, gather_matrix)
    grad_values = step_wide * grad_stepped + pack_ref[SKIP : SKIP + 1, :width] * dmix_ref[...]
    grad_ref[:, :width] = grad_values * (sig * (1.0 + conv * (1.0 - sig)))
    slope = sig_s * (1.0 + conv_s * (1.0 - sig_s))
    grad_ref[:, width : width + NSTATE] = grad_b * slope[:, :NSTATE]
    grad_ref[:, width + NSTATE :] = grad_c_ref[...] * slope[:, NSTATE:]
    rate = -jnp.exp(pack_ref[DECAY : DECAY + 1, :LANES])
    grad_raw = (grad_step + rate * grad_decay) * logistic(raw_ref[...] + pack_ref[STEP : STEP + 1, :LANES])
    grad_raw_ref[...] = grad_raw.astype(BF16)
    small_ref[0:1, :] += jnp.sum(grad_raw, axis=0, keepdims=True)
    small_ref[1:2, :] += jnp.sum(grad_decay * (rate * step), axis=0, keepdims=True)


def later_call(kept, dmix, adj_rate, adj_in, parts, pack, consts, *ahead):
    conv_x, conv_s, step, cum, raw, entry, rate, entry_in = kept
    length, width = conv_x.shape
    rows = min(SPAN, length)
    chunks = length // rows
    spread_matrix, gather_matrix, _ = consts
    return ordered_call(
        later_kernel,
        ahead,
        grid=(chunks,),
        in_specs=[
            chunk_of(rows, width),
            chunk_of(rows, 2 * NSTATE),
            chunk_of(rows, width),
            chunk_of(rows, LANES),
            chunk_of(rows, LANES),
            chunk_of(rows, LANES),
            stack_of(NSTATE, width),
            stack_of(8, LANES),
            whole_of(NSTATE, width),
            stack_of(8, LANES),
            whole_of(NSTATE, width),
            chunk_of(rows, width),
            chunk_of(rows, NSTATE),
            chunk_of(rows, NSTATE),
            chunk_of(rows, LANES),
            whole_of(*pack.shape),
            whole_of(2 * LANES, width),
            whole_of(2 * width, LANES),
        ],
        out_specs=[chunk_of(rows, width + 2 * NSTATE), chunk_of(rows, LANES), whole_of(8, LANES)],
        out_shape=[
            shape(length, width + 2 * NSTATE),
            shape(length, LANES, dtype=BF16),
            shape(8, LANES),
        ],
        compiler_params=params_of(14),
        cost_estimate=cost(8 * length * NSTATE * width, 24 * length * width),
        name="later",
    )(
        conv_x,
        conv_s,
        dmix,
        step,
        cum,
        raw,
        entry,
        rate,
        entry_in,
        adj_rate,
        adj_in,
        *parts,
        pack,
        spread_matrix,
        gather_matrix,
    )


def conv_back_kernel(
    chunks,
    front_spec,
    gate_spec,
    where_ref,
    grad_ref,
    pre_ref,
    raw_ref,
    dz_ref,
    low_ref,
    tok_ref,
    halo_ref,
    halo_tok_ref,
    pack_ref,
    x_ref,
    inv_ref,
    head_ref,
    skip_ref,
    gained_ref,
    gather_ref,
    f0,
    f1,
    f2,
    f3,
    f4,
    f5,
    z0,
    z1,
    z2,
    z3,
    *refs,
):
    if front_spec[0] == 0:
        above, refs = refs[0], refs[1:]
    else:
        above = None
    conv_back_body(
        chunks,
        front_spec,
        gate_spec,
        (where_ref, grad_ref, pre_ref, raw_ref, dz_ref, low_ref, tok_ref, halo_ref, halo_tok_ref, pack_ref, x_ref, inv_ref),
        (head_ref, skip_ref, gained_ref, gather_ref),
        (f0, f1, f2, f3, f4, f5),
        (z0, z1, z2, z3),
        above,
        *refs,
    )


def conv_back_body(
    chunks,
    front_spec,
    gate_spec,
    inputs,
    vectors,
    held_front,
    held_gate,
    above,
    keep_ref,
    send_ref,
    g0,
    k0,
    g1,
    k1,
    vector_ref,
    vector_send_ref,
    small_ref,
    front,
    front_sems,
    gate,
    gate_sems,
    ext,
    ext_tok,
    grads,
):
    where_ref, grad_ref, pre_ref, raw_ref, dz_ref, low_ref, tok_ref, halo_ref, halo_tok_ref, pack_ref, x_ref, inv_ref = inputs
    head_ref, skip_ref, gained_ref, gather_ref = vectors
    step = pl.program_id(0)
    rows, both = pre_ref.shape
    width = both - 2 * NSTATE
    tile = g0.shape[1]
    core = where_ref[CORE]

    @pl.when(step == 0)
    def _():
        start_weights(front_spec, where_ref, held_front, front, front_sems)
        start_weights(gate_spec, where_ref, held_gate, gate, gate_sems)
        ext[rows : rows + 8, :] = halo_ref[...]
        ext_tok[rows : rows + 8, :] = halo_tok_ref[...]
        small_ref[...] = jnp.zeros_like(small_ref)

    @pl.when(jnp.logical_and(step > 0, step < chunks))
    def _():
        ext[rows : rows + 8, :] = ext[0:8, :]
        ext_tok[rows : rows + 8, :] = ext_tok[0:8, :]

    @pl.when(step < chunks)
    def _():
        grad = grad_ref[...]
        ext[0:rows, :] = grad
        ext_tok[0:rows, :] = tok_ref[...]
        pre = pre_ref[...]
        out = pack_ref[TAPS : TAPS + 1, :] * grad
        small_ref[TAPS : TAPS + 1, :] += jnp.sum(grad * pre, axis=0, keepdims=True)
        small_ref[BIAS : BIAS + 1, :] += jnp.sum(grad, axis=0, keepdims=True)
        for k in range(1, CONV):
            shifted = ext_tok[k : k + rows, k : k + 1] * ext[k : k + rows, :]
            out = out + pack_ref[TAPS + k : TAPS + k + 1, :] * shifted
            small_ref[TAPS + k : TAPS + k + 1, :] += jnp.sum(shifted * pre, axis=0, keepdims=True)
        out_x = out[:, :width].astype(BF16)
        s_top, s_rest = halves(out[:, width:])
        raw = raw_ref[...]
        dz = dz_ref[...]
        at = pl.ds(pl.multiple_of((chunks - 1 - step) * rows, rows), rows)
        grads[at, :] = jnp.concatenate([out_x, s_top, raw, dz, s_rest], axis=1)
        low = low_ref[...]
        none = jnp.zeros((rows, LANES), BF16)
        halves_of = [dz, out_x, low, s_top, s_rest]
        for_lower = [v[:, : v.shape[1] // 2] for v in halves_of] + [raw]
        for_upper = [v[:, v.shape[1] // 2 :] for v in halves_of] + [none]

        @pl.when(core == 0)
        def _():
            keep_ref[...] = jnp.concatenate(for_lower, axis=1)
            send_ref[...] = jnp.concatenate(for_upper, axis=1)

        @pl.when(core == 1)
        def _():
            keep_ref[...] = jnp.concatenate(for_upper, axis=1)
            send_ref[...] = jnp.concatenate(for_lower, axis=1)

    @pl.when(step == chunks)
    def _():
        wait_weights(front_spec, where_ref, held_front, front, front_sems)
        wait_weights(gate_spec, where_ref, held_gate, gate, gate_sems)
        skip = gather_heads(skip_ref[...], gather_ref[...])
        small_ref[SKIP : SKIP + 1, :LANES] = skip[0:1, :]
        small_ref[GATED : GATED + 1, :width] = gained_ref[0:1, :]
        small_ref[STEP : STEP + 2, :LANES] = head_ref[0:2, :]

    for n in range(2 * front.shape[0] // (2 * tile)):

        @pl.when(step == chunks + n)
        def _():
            at = slice(n * tile, (n + 1) * tile)
            part = (
                mm(grads[:, : both + LANES], front[at, :], NT)
                + mm(grads[:, both + LANES : both + LANES + width], gate[at, :], NT)
                + mm(grads[:, both + LANES + width :], front[at, width:both], NT)
            )
            put_quarters(where_ref, part, (g0, k0, g1, k1))
            row = jnp.sum(part * (x_ref[...].astype(F32) * inv_ref[:, 0:1]), axis=0, keepdims=True)
            per_row = front.shape[0] // 2 // tile
            place = slice((n % per_row) * tile, (n % per_row + 1) * tile)
            small_ref[NORM + n // per_row : NORM + n // per_row + 1, place] = row

    @pl.when(step == pl.num_programs(0) - 1)
    def _():
        if above is None:
            vector_ref[...] = small_ref[...]
            vector_send_ref[...] = jnp.zeros_like(vector_send_ref)
            return
        small, other = small_ref[...], above[...]
        vector_ref[...] = jnp.where(core == 0, small, other)
        vector_send_ref[...] = jnp.where(core == 0, other, small)


def conv_back_call(
    where, grad, pre, grad_raw, dz, low, tok, halo, halo_tok, pack, x, inv, head, skip, gained, gather_matrix, front, gate, above, *ahead
):
    length, both = pre.shape
    width = both - 2 * NSTATE
    model = 2 * front[1][0].shape[0]
    rows = min(SPAN, length)
    chunks = length // rows
    tile = model // 4
    out_width = 3 * (width // 2) + 2 * NSTATE + LANES

    def chunk_spec(size):
        return pl.BlockSpec((rows, size), lambda c: (jnp.maximum(chunks - 1 - c, 0), 0))

    def tile_spec(rows_):
        return pl.BlockSpec((rows_, tile), lambda c: (0, jnp.maximum(c - chunks, 0)))

    return ordered_call(
        functools.partial(conv_back_kernel, chunks, front[0], gate[0]),
        ahead,
        grid=(chunks + model // tile,),
        in_specs=[
            scalars_of(),
            chunk_spec(both),
            chunk_spec(both),
            chunk_spec(LANES),
            chunk_spec(width),
            chunk_spec(width),
            chunk_spec(LANES),
            whole_of(8, both),
            whole_of(8, LANES),
            whole_of(*pack.shape),
            tile_spec(length),
            whole_of(length, LANES),
            whole_of(8, LANES),
            whole_of(8, width),
            whole_of(8, width),
            whole_of(2 * width, LANES),
        ]
        + anywhere(10)
        + [whole_of(*pack.shape)] * len(above),
        out_specs=[
            chunk_spec(out_width),
            chunk_spec(out_width),
        ]
        + [tile_spec(length // 4)] * 4
        + [whole_of(*pack.shape)] * 2,
        out_shape=[
            shape(length, out_width, dtype=BF16),
            shape(length, out_width, dtype=BF16),
        ]
        + quarter_shapes(length, model, BF16)
        + [shape(*pack.shape)] * 2,
        scratch_shapes=[pltpu.VMEM(pack.shape, F32)]
        + weight_scratch(front)
        + weight_scratch(gate)
        + [
            pltpu.VMEM((rows + 8, both), F32),
            pltpu.VMEM((rows + 8, LANES), F32),
            pltpu.VMEM((length, both + LANES + width + 2 * NSTATE), BF16),
        ],
        compiler_params=params_of(24),
        cost_estimate=cost(4 * length * model * both, 24 * length * width),
        name="conv_back",
    )(where, grad, pre, grad_raw, dz, low, tok, halo, halo_tok, pack, x, inv, head, skip, gained, gather_matrix, *front[1], *gate[1], *above)


def split_states(total, width):
    top, rest = halves(total[:, width : width + NSTATE])
    return jnp.concatenate(
        [total[:, :width].astype(BF16), top, rest, total[:, width + NSTATE :].astype(BF16)], axis=1
    )


def whole_states(value, width):
    value = value.astype(F32)
    states = value[:, width : width + NSTATE] + value[:, width + NSTATE : width + 2 * NSTATE]
    return jnp.concatenate([value[:, :width], states, value[:, width + 2 * NSTATE :]], axis=1)


def block_grads(n0, n1, g0, g1, keep_ref, got_ref):
    width = keep_ref.shape[1] - 2 * NSTATE - LANES
    inner = 2 * width // 3
    mine, theirs = n0[...], n1[...]
    main = mm(mine, keep_ref[:, :inner], TN) + mm(theirs, got_ref[:, :inner], TN)
    outer = mm(g0[...].astype(BF16), keep_ref[:, inner:width], TN) + mm(
        g1[...].astype(BF16), got_ref[:, inner:width], TN
    )
    rest = mm(mine, keep_ref[:, width:], TN) + mm(theirs, got_ref[:, width:], TN)
    states = rest[:, :NSTATE] + rest[:, NSTATE : 2 * NSTATE]
    return split_states(jnp.concatenate([main, outer, states, rest[:, 2 * NSTATE :]], axis=1), width)


def wgrad_plain_kernel(*refs):
    refs[-1][0] = block_grads(*refs[:-1])


def wgrad_relative_kernel(extra, where_ref, *refs):
    value = block_grads(*refs[:6])
    first_give, first_keep, second_give, second_keep = refs[6 + extra :]
    half = value.shape[0] // 2
    step = pl.program_id(0)

    @pl.when(step < 2)
    def _():
        first_give[0] = value[:half]

    @pl.when(step >= 2)
    def _():
        first_keep[0] = value[:half]

    @pl.when(step % 2 == 1)
    def _():
        second_give[0] = value[half:]

    @pl.when(step % 2 == 0)
    def _():
        second_keep[0] = value[half:]


def wgrad_call(where, spans, normed, normed_other, g_low, g_other, keep, got, *ahead):
    length, model = normed.shape
    size = keep.shape[1]
    blocks = spans[0] * spans[1]
    rows = model // blocks
    operands = (normed, normed_other, g_low, g_other, keep, got)
    if spans != (2, 2):
        grid_rows = max(rows, LANES)
        steps = model // grid_rows
        return pl.pallas_call(
            wgrad_plain_kernel,
            grid=(steps,),
            in_specs=[pl.BlockSpec((length, grid_rows), lambda b: (0, b))] * 4
            + [whole_of(*v.shape) for v in operands[4:]],
            out_specs=pl.BlockSpec((1, grid_rows, size), lambda b: (b, 0, 0)),
            out_shape=shape(steps, grid_rows, size, dtype=BF16),
            compiler_params=params_of(20),
            cost_estimate=cost(0, 0),
            name="wgrad",
        )(*operands).reshape(blocks, rows, size)

    def block_index(b, where_ref):
        x = jnp.where(b < 2, 1 - where_ref[ALONG_X], where_ref[ALONG_X])
        y = jnp.where(b % 2 == 1, 1 - where_ref[ALONG_Y], where_ref[ALONG_Y])
        return (0, 2 * x + y)

    def whole(v):
        return pl.BlockSpec(v.shape, lambda b, where_ref: (0,) * v.ndim)

    maps = [
        lambda b, where_ref: (jnp.minimum(b, 1), 0, 0),
        lambda b, where_ref: (jnp.maximum(b - 2, 0), 0, 0),
        lambda b, where_ref: (1 - b // 2, 0, 0),
        lambda b, where_ref: (1 - b // 2, 0, 0),
    ]
    return pl.pallas_call(
        functools.partial(wgrad_relative_kernel, len(ahead)),
        grid_spec=pltpu.PrefetchScalarGridSpec(
            num_scalar_prefetch=1,
            grid=(4,),
            in_specs=[pl.BlockSpec((length, rows), block_index)] * 4
            + [whole(v) for v in operands[4:]]
            + [pl.BlockSpec(memory_space=pl.ANY)] * len(ahead),
            out_specs=[pl.BlockSpec((1, rows // 2, size), m) for m in maps],
        ),
        out_shape=[shape(2, rows // 2, size, dtype=BF16)] * 4,
        compiler_params=params_of(20),
        cost_estimate=cost(0, 0),
        name="wgrad",
    )(where, *operands, *ahead)


def turn_kernel(*refs):
    for n in range(2):
        keep_ref, got_ref, give_ref, kept_ref = refs[n::2]
        width = keep_ref.shape[2] - 2 * NSTATE - LANES
        sums = [whole_states(keep_ref[m], width) + whole_states(got_ref[m], width) for m in range(2)]
        kept_ref[...] = sums[0]
        give_ref[...] = split_states(sums[1], width)


def turn_call(keeps, gots, *ahead):
    _, rows, size = keeps[0].shape
    outputs = ordered_call(
        turn_kernel,
        ahead,
        in_specs=[pl.BlockSpec(memory_space=pltpu.VMEM)] * 4,
        out_specs=[pl.BlockSpec(memory_space=pltpu.VMEM)] * 4,
        out_shape=[shape(rows, size, dtype=BF16)] * 2 + [shape(rows, size - NSTATE)] * 2,
        compiler_params=pltpu.CompilerParams(vmem_limit_bytes=16 * 1024 * 1024),
        cost_estimate=cost(0, 0),
        name="turn",
    )(*keeps, *gots)
    return outputs[:2], outputs[2:]


def summed_kernel(where_ref, first_keep, first_got, second_keep, second_got, *refs):
    rows = first_keep.shape[0]
    above, (matrices_ref, steps_ref, *states_refs) = (None, refs) if len(refs) == 3 else (refs[0], refs[1:])
    width = matrices_ref.shape[1]
    states = []
    for at, keep, got in ((slice(0, rows), first_keep, first_got), (slice(rows, 2 * rows), second_keep, second_got)):
        total = keep[...] + whole_states(got[...], width)
        matrices_ref[at, :] = total[:, :width].astype(BF16)
        states.append(total[:, width : width + NSTATE])
        steps_ref[at, :] = total[:, width + NSTATE :]
    states = jnp.concatenate(states, axis=0)
    if above is None:
        states_refs[0][...] = states
    else:
        put_quarters(where_ref, jnp.concatenate([states, above[...]], axis=1), states_refs)


def summed_call(where, operands, above, *ahead):
    rows, size = operands[1].shape
    width = size - 2 * NSTATE - LANES
    states = quarter_shapes(2 * rows, 2 * NSTATE, F32) if above else [shape(2 * rows, NSTATE)]
    return ordered_call(
        summed_kernel,
        ahead,
        in_specs=[scalars_of()] + [pl.BlockSpec(memory_space=pltpu.VMEM)] * (4 + len(above)),
        out_specs=[pl.BlockSpec(memory_space=pltpu.VMEM)] * (2 + len(states)),
        out_shape=[
            shape(2 * rows, width, dtype=BF16),
            shape(2 * rows, LANES),
        ]
        + states,
        compiler_params=pltpu.CompilerParams(vmem_limit_bytes=16 * 1024 * 1024),
        cost_estimate=cost(0, 0),
        name="summed",
    )(where, *operands, *above)


def renorm_kernel(x_ref, pack_ref, out_ref):
    gain = norm_row(pack_ref, x_ref.shape[1] // 2)
    x = x_ref[...].astype(F32)
    inv = lax.rsqrt(jnp.mean(x * x, axis=-1, keepdims=True) + EPS)
    out_ref[...] = (x * inv * gain).astype(BF16)


def renorm_call(x, pack, *ahead):
    length, model = x.shape
    rows = min(SPAN, length)
    return ordered_call(
        renorm_kernel,
        ahead,
        grid=(length // rows,),
        in_specs=[chunk_of(rows, model), whole_of(*pack.shape)],
        out_specs=chunk_of(rows, model),
        out_shape=shape(length, model, dtype=BF16),
        compiler_params=params_of(10),
        cost_estimate=cost(0, 0),
        name="renorm",
    )(x, pack)


def swap(value, axis):
    return lax.ppermute(value, axis, [(0, 1), (1, 0)])


def shifted_along(value, axis, by):
    count = lax.axis_size(axis)
    return lax.ppermute(
        value, axis, [(i, i + by) for i in range(count) if 0 <= i + by < count]
    )


def sum_over(value, axis):
    if lax.axis_size(axis) == 2:
        return value + swap(value, axis)
    return lax.psum(value, axis)


def sum_given(value, axis):
    if lax.axis_size(axis) == 2:
        return swap(value, axis)
    return lax.psum(value, axis) - value


def after(value, *earlier):
    for event in earlier:
        first = lax.slice(event, (0,) * event.ndim, (1,) * event.ndim).reshape(())
        value = value + (first.astype(F32) * 0.0).astype(value.dtype)
    return value


def carried_state(state, rate_wide, axis, backward):
    count = lax.axis_size(axis)
    if count == 2:
        return shifted_along(state, axis, -1 if backward else 1)
    here = lax.axis_index(axis)
    states = lax.all_gather(state, axis)
    rates = lax.all_gather(rate_wide, axis)
    result = jnp.zeros_like(state)
    for k in range(count):
        at = count - 1 - k if backward else k
        reached = at > here if backward else at < here
        result = jnp.where(reached, rates[at] * result + states[at], result)
    return result


def small_sum(value):
    count = lax.axis_size("tensor")
    total = value
    for by in range(1, count):
        total = total + lax.ppermute(
            value, "tensor", [(i, (i + by) % count) for i in range(count)]
        )
    return total


class TensorSum:
    NEAR = [(0, 1), (1, 0), (2, 3), (3, 2)]
    FAR = [(0, 2), (2, 0), (1, 3), (3, 1)]
    STEPS = ((NEAR, FAR, NEAR), (FAR, NEAR, FAR))

    def __init__(self, pieces):
        self.pieces = pieces
        self.given = self._send([give for _, give, _ in pieces], 0)
        self.kind = pieces[0][1].dtype

    def _send(self, arrays, step):
        return [
            lax.ppermute(v, "tensor", self.STEPS[half][step])
            for (half, _, _), v in zip(self.pieces, arrays)
        ]

    def _merge(self, firsts, seconds, ahead):
        if self.kind == jnp.float16:
            return [(a.astype(F32) + b.astype(F32)).astype(self.kind) for a, b in zip(firsts, seconds)]
        return merge_call(firsts, seconds, self.kind, *ahead)

    def add(self, *ahead):
        self.parts = self._merge([keep for _, _, keep in self.pieces], self.given, ahead)
        return self.parts[-1]

    def hold(self, *ahead):
        held = hold_call(self.parts, *ahead)
        self.given = self._send(held, 1)
        return held[-1]

    def across(self, *ahead):
        self.add(*ahead)
        self.given = self._send(self.parts, 1)
        return self.parts[-1]

    def total(self, *ahead):
        self.totals = self._merge(self.parts, self.given, ahead)
        return self.totals[-1]

    def spread(self, *ahead):
        held = hold_call(self.totals, *ahead)
        self.others = self._send(held, 2)
        return held[-1]

    def back(self, *ahead):
        self.total(*ahead)
        self.others = self._send(self.totals, 2)
        return self.totals[-1]

    def quarters(self):
        return [v for pair in zip(self.totals, self.others) for v in pair]


class ScatterSum:
    def __init__(self, value):
        self.whole = None
        if not isinstance(value, (list, tuple)):
            self.whole = lax.psum_scatter(value, ("fsdp", "context"), scatter_dimension=0, tiled=False)
            return
        self.keeps = [value[1], value[3]]
        self.given = [swap(value[0], "fsdp"), swap(value[2], "context")]

    def turn(self, *ahead):
        if self.whole is not None:
            return self.whole
        gives, self.keeps = turn_call(self.keeps, self.given, *ahead)
        self.given = [swap(gives[0], "context"), swap(gives[1], "fsdp")]
        return gives[0]

    def result(self, where, above, *ahead):
        if self.whole is not None:
            half = self.whole.shape[0] // 2
            none = jnp.zeros((half, self.whole.shape[1] - NSTATE), F32)
            operands = none, self.whole[:half], none, self.whole[half:]
        else:
            operands = self.keeps[0], self.given[0], self.keeps[1], self.given[1]
        return summed_call(where, operands, above, *ahead)


def rest_kernel(where_ref, t0, o0, t1, o1, steps0, steps1, out_ref):
    rows = steps0.shape[0]
    states = joined(where_ref, (t0, o0, t1, o1), slice(0, rows))
    out_ref[...] = jnp.concatenate(
        [states[:, :NSTATE], steps0[...], states[:, NSTATE:], steps1[...]], axis=1
    )


def rest_call(where, quarters, steps0, steps1, *ahead):
    return ordered_call(
        rest_kernel,
        ahead,
        in_specs=[scalars_of()] + [pl.BlockSpec(memory_space=pltpu.VMEM)] * 6,
        out_specs=pl.BlockSpec(memory_space=pltpu.VMEM),
        out_shape=shape(steps0.shape[0], 2 * (NSTATE + LANES)),
        compiler_params=pltpu.CompilerParams(vmem_limit_bytes=8 * 1024 * 1024),
        cost_estimate=cost(0, 0),
        name="rest",
    )(where, *quarters, steps0, steps1)


def matrices_kernel(where_ref, m0, r0, m1, r1, rest, rest_got, main_ref, states_ref, step_ref, out_ref):
    def put(lower, upper, lower_rest, upper_rest, column):
        half = main_ref.shape[3] // 2
        a, b = lower[...].astype(F32), upper[...].astype(F32)
        main_ref[0, :, 0, :] = jnp.concatenate([a[:, :half], b[:, :half]], axis=1)
        main_ref[0, :, 1, :] = jnp.concatenate([a[:, half : 2 * half], b[:, half : 2 * half]], axis=1)
        out_ref[0] = jnp.concatenate([a[:, 2 * half :], b[:, 2 * half :]], axis=1)
        states = slice(column, column + NSTATE)
        states_ref[0] = jnp.concatenate([lower_rest[:, states], upper_rest[:, states]], axis=1)
        step_ref[0] = lower_rest[:, column + NSTATE : column + NSTATE + step_ref.shape[2]]

    @pl.when(where_ref[CORE] == 0)
    def _():
        put(m0, r0, rest, rest_got, 0)

    @pl.when(where_ref[CORE] == 1)
    def _():
        put(r1, m1, rest_got, rest, NSTATE + LANES)


def matrices_call(where, heads, *arrays):
    rows, columns_ = arrays[0].shape
    half = columns_ // 3
    block = rows // 2

    def out_spec(*dims):
        return pl.BlockSpec((1, block) + dims, lambda r: (0, r) + (0,) * len(dims))

    return pl.pallas_call(
        matrices_kernel,
        grid=(2,),
        in_specs=[scalars_of()] + [pl.BlockSpec((block, v.shape[1]), lambda r: (r, 0)) for v in arrays],
        out_specs=[out_spec(2, 2 * half), out_spec(2 * NSTATE), out_spec(heads), out_spec(2 * half)],
        out_shape=[
            shape(1, rows, 2, 2 * half),
            shape(1, rows, 2 * NSTATE),
            shape(1, rows, heads),
            shape(1, rows, 2 * half),
        ],
        compiler_params=params_of(20),
        cost_estimate=cost(0, 0),
        name="matrices",
    )(where, *arrays)


def tokens_kernel(where_ref, own0, got0, own1, got1, *refs):
    out_ref, tick_ref = refs[-2:]
    tick_ref[...] = jnp.zeros_like(tick_ref)
    which = pl.program_id(0)
    core = where_ref[CORE]

    @pl.when(core == 0)
    def _():
        @pl.when(which == 0)
        def _():
            out_ref[0, 0] = own0[...]

        @pl.when(which == 1)
        def _():
            out_ref[0, 0] = got0[...].astype(F32)

    @pl.when(core == 1)
    def _():
        @pl.when(which == 0)
        def _():
            out_ref[0, 0] = got1[...].astype(F32)

        @pl.when(which == 1)
        def _():
            out_ref[0, 0] = own1[...]


def tokens_call(where, own0, got0, own1, got1, *ahead):
    length, model = own0.shape
    block = length // 2

    def spec(core, which):
        def index(s, r, where_ref):
            return (jnp.where((where_ref[CORE] == core) & (s == which), r, 0), 0)

        return pl.BlockSpec((block, model), index)

    return pl.pallas_call(
        tokens_kernel,
        grid_spec=pltpu.PrefetchScalarGridSpec(
            num_scalar_prefetch=1,
            grid=(2, length // block),
            in_specs=[spec(0, 0), spec(0, 1), spec(1, 1), spec(1, 0)]
            + [pl.BlockSpec(memory_space=pl.ANY)] * len(ahead),
            out_specs=[
                pl.BlockSpec((1, 1, block, model), lambda s, r, where_ref: (0, s, r, 0)),
                pl.BlockSpec((8, LANES), lambda s, r, where_ref: (0, 0)),
            ],
        ),
        out_shape=[shape(1, 2, length, model), shape(8, LANES)],
        compiler_params=pltpu.CompilerParams(
            dimension_semantics=("arbitrary", "arbitrary"), vmem_limit_bytes=20 * 1024 * 1024
        ),
        cost_estimate=cost(0, 16 * length * model),
        name="tokens",
    )(where, own0, got0, own1, got1, *ahead)


def shards(
    block_input,
    doc_start,
    cotangent,
    norm_gain,
    proj_main,
    proj_states,
    proj_step,
    conv_main,
    conv_main_bias,
    conv_states,
    conv_states_bias,
    step_bias,
    log_decay,
    skip_gain,
    gated_gain,
    proj_out,
):
    core = lax.axis_index("section")
    lower_core = core == 0
    length = block_input.shape[1]
    model = block_input.shape[2]
    heads = proj_step.shape[2]
    width = heads * HEAD_DIM
    half = width // 2
    both = width + 2 * NSTATE
    rows = min(SPAN, length)
    spans = lax.axis_size("fsdp"), lax.axis_size("context")
    x_index, y_index = lax.axis_index("fsdp"), lax.axis_index("context")
    z_index = lax.axis_index("tensor")
    place = jnp.stack([core, 1 - x_index, z_index % 2, z_index // 2, x_index, y_index]).astype(jnp.int32)

    main_own = lax.optimization_barrier(proj_main[0].reshape(-1, 2 * width))
    rest_own = jnp.concatenate(
        [proj_states[0], jnp.pad(proj_step[0], ((0, 0), (0, LANES - heads)))], axis=1
    )
    out_own = proj_out[0]
    main_near = swap(main_own, "section")
    rest_near = swap(rest_own, "section")
    out_near = swap(out_own, "section")
    rest_width = rest_own.shape[1]
    front_width = width + rest_width
    held = (main_own, main_near, rest_own, rest_near, out_own, out_near)
    front_part, gate_part, out_part = [(0, width, width), (1, 0, rest_width)], [(0, 0, width)], [(2, 0, width)]
    mains = (main_own, main_near)
    def weights_of(layer, far_arrays, front_at, gate_at, out_at):
        front = (layer, [(width, width), (0, rest_width)], (front_at, front_width))
        gate = (layer, [(0, width)], (gate_at, width))
        out = (layer, [(0, width)], (out_at, width))
        return (
            (front, mains + (rest_own, rest_near) + far_arrays),
            (gate, mains + far_arrays),
            (out, (out_own, out_near) + far_arrays),
        )

    def both_halves_of(far, *ahead):
        far = after(far, *ahead)
        return far, swap(far, "section")

    head_of = np.arange(width) // HEAD_DIM
    one_hot = (np.arange(LANES)[:, None] == head_of[None, :]).astype(np.float32)
    spread_matrix = jnp.asarray(np.concatenate([one_hot, one_hot], axis=0), BF16)
    gather_matrix = jnp.asarray(np.concatenate([one_hot.T, one_hot.T], axis=0), BF16)
    row_head = np.arange(heads * rows) // rows
    ones = jnp.asarray((row_head[:, None] == np.arange(LANES)[None, :]).astype(np.float32), BF16)
    consts = (spread_matrix, gather_matrix, ones)

    tokens = lax.dynamic_index_in_dim(block_input, core, 0, keepdims=False, allow_negative_indices=False)
    first_piece = pieces_call(place, 0, front_part, held[:4])
    cot = lax.dynamic_index_in_dim(cotangent, core, 0, keepdims=False, allow_negative_indices=False)
    tokens_other = lax.dynamic_index_in_dim(block_input, 1 - core, 0, keepdims=False, allow_negative_indices=False)
    cot_other = lax.dynamic_index_in_dim(cotangent, 1 - core, 0, keepdims=False, allow_negative_indices=False)
    starts = lax.dynamic_index_in_dim(doc_start, core, 0, keepdims=False, allow_negative_indices=False).astype(F32)
    front_far0 = swap(first_piece, "fsdp")
    gate_far0 = swap(after(pieces_call(place, 0, gate_part, held[:2]), front_far0), "fsdp")
    out_piece0 = pieces_call(place, 0, [(0, 0, width)], held[4:])
    earlier = shifted_along(after(starts[length - 8 :], first_piece), "context", 1)
    later = shifted_along(after(starts[:8], first_piece), "context", -1)
    line = jnp.concatenate([earlier, starts, later])
    keep = 1.0 - line
    one_back = keep[8:]
    two_back = one_back * keep[7:-1]
    three_back = two_back * keep[6:-2]
    tok_all = jnp.stack([line[8:], one_back, two_back, three_back], axis=1)
    tok_all = jnp.pad(tok_all, ((0, 0), (0, LANES - 4)))
    tok, tok_after = tok_all[:length], tok_all[length:]

    def head_lanes(row):
        return jnp.pad(row, ((0, 0), (0, LANES - heads)))

    pack_own = pl.pallas_call(
        pack_kernel,
        out_shape=shape(PACK, both),
        compiler_params=pltpu.CompilerParams(vmem_limit_bytes=4 * 1024 * 1024),
        name="pack",
    )(
        conv_main[0],
        conv_states[0],
        conv_main_bias,
        conv_states_bias,
        jnp.repeat(skip_gain, HEAD_DIM, axis=1),
        gated_gain,
        norm_gain,
        head_lanes(step_bias),
        head_lanes(log_decay),
    )
    pack_other = swap(pack_own, "section")
    packs = [jnp.where(core == layer, pack_own, pack_other) for layer in (0, 1)]

    def layer_front(x, halo, layer, weights, quarters, *ahead):
        front = front_call(
            place, x, halo, tok, packs[layer], spread_matrix, weights, quarters, *ahead
        )
        end, end_rate = front[-2:]
        rate_wide = jnp.repeat(end_rate[0:1, :heads], HEAD_DIM, axis=1)
        return front, rate_wide, carried_state(end, rate_wide, "context", False)

    def layer_rest(front, entry_in, y, z, layer, *grad_scaled):
        _, _, _, _, conv_x, conv_s, _, _, cum, _, rate, _, _ = front
        comb, gated, sums = gate_call(
            y, z, conv_x, conv_s, cum, rate, entry_in, packs[layer], spread_matrix, *grad_scaled
        )
        return comb, gated, small_sum(sums)

    def layer_gate_back(grad_scaled, sums, comb, z, front, rate_wide, layer):
        _, _, _, _, _, conv_s, _, _, cum, _, _, _, _ = front
        dmix, dz, adj, adj_rate, begin, gained = gate_back_call(
            grad_scaled, comb, z, conv_s, cum, sums, packs[layer], spread_matrix
        )
        adj_in = carried_state(begin, rate_wide, "context", True)
        return dmix, dz, adj, adj_rate, adj_in, gained

    def layer_mix_back(gate_back, front, entry_in, layer, ahead, before_later):
        _, _, _, _, conv_x, conv_s, raw, step, cum, entry, rate, _, _ = front
        kept = (conv_x, conv_s, step, cum, raw, entry, rate, entry_in)
        dmix, dz, adj, adj_rate, adj_in, gained = gate_back
        *parts, skip = mix_back_call(kept, dmix, adj, consts, *ahead)
        grad, grad_raw, head = later_call(
            kept, dmix, adj_rate, adj_in, parts, packs[layer], consts, *before_later(skip)
        )
        edge = shifted_along(grad[:8], "context", -1)
        return grad, grad_raw, dz, head, skip, gained, edge

    def layer_down(back, low, x, front, layer, front_weights, gate_weights, above, *ahead):
        grad, grad_raw, dz, head, skip, gained, edge = back
        keep, send, g0, k0, g1, k1, vector, vector_send = conv_back_call(
            place,
            grad,
            front[3],
            grad_raw,
            dz,
            low,
            tok,
            edge,
            tok_after,
            packs[layer],
            x,
            front[2],
            head,
            skip,
            gained,
            gather_matrix,
            front_weights,
            gate_weights,
            above,
            *ahead,
        )
        return keep, send, [(0, g0, k0), (1, g1, k1)], vector, vector_send

    fronts0 = weights_of(0, both_halves_of(front_far0), 0, 0, 0)[0]
    halo0 = shifted_along(after(tokens[length - 8 :], first_piece), "context", 1)
    front0, rate_wide0, entry0 = layer_front(
        tokens, halo0, 0, fronts0, (), packs[1]
    )
    normed0 = front0[1]
    gate_far0 = after(gate_far0, front0[-1])
    gates0 = weights_of(0, (gate_far0, swap(gate_far0, "section")), 0, 0, 0)[1]
    out_far0 = swap(after(out_piece0, gate_far0), "fsdp")
    y0 = mix_call(front0[4], front0[5], front0[7], front0[8], front0[9], spread_matrix)
    z0 = project_call(place, normed0, gates0)
    comb0, gated0, sums0 = layer_rest(front0, entry0, y0, z0, 0)
    out_far0 = after(out_far0, comb0)
    outs0 = weights_of(0, (out_far0, swap(out_far0, "section")), 0, 0, 0)[2]
    pieces1 = pieces_call(place, 1, front_part + gate_part + out_part, held, out_far0)
    far1 = swap(pieces1, "fsdp")
    low0, g0, k0, g1, k1, edge0 = out_call(place, gated0, sums0, packs[0], outs0, F32, pieces1)

    half16 = jnp.float16
    total0 = TensorSum([(0, g0.astype(half16), k0), (1, g1.astype(half16), k1)])
    halo1 = shifted_along(tokens[length - 8 :].astype(F32) + small_sum(edge0), "context", 1)
    total0.across()
    event = total0.back()
    fronts1, gates1, outs1 = weights_of(
        1, both_halves_of(far1, event), 0, front_width, front_width + width
    )
    grad_scaled1 = project_call(place, cot, outs1)
    normed_other0 = renorm_call(tokens_other, packs[0], edge0)
    branch0 = [v.astype(F32) for v in total0.quarters()]

    front1, rate_wide1, entry1 = layer_front(
        tokens, halo1, 1, fronts1, branch0
    )
    x1, normed1 = front1[:2]
    y1 = mix_call(front1[4], front1[5], front1[7], front1[8], front1[9], spread_matrix)
    z1 = project_call(place, normed1, gates1)
    comb1, gated1, sums1 = layer_rest(front1, entry1, y1, z1, 1, grad_scaled1)

    gate_back1 = layer_gate_back(grad_scaled1, sums1, comb1, z1, front1, rate_wide1, 1)
    low1, g0, k0, g1, k1, edge1 = out_call(place, gated1, sums1, packs[1], outs1, BF16)
    half_a = TensorSum([(0, g0, k0)])
    half_b = TensorSum([(0, g1, k1)])
    back1 = layer_mix_back(gate_back1, front1, entry1, 1, (edge1,), lambda tick: ())
    keep1, send1, pieces, small1, _ = layer_down(
        back1,
        low1,
        x1,
        front1,
        1,
        fronts1,
        gates1,
        (),
        half_a.across(back1[3]),
        half_b.add(back1[3]),
    )
    *gives, send1 = hold_call([give for _, give, _ in pieces] + [send1], half_a.total(keep1))
    total1 = TensorSum([(half, give, keep) for (half, _, keep), give in zip(pieces, gives)])
    received1 = swap(send1, "section")
    x1_other = swap(x1, "section")
    normed_other1 = renorm_call(x1_other, packs[1], keep1)
    matrices1 = wgrad_call(place, spans, normed1, normed_other1, cot, cot_other, keep1, received1)
    scatter1 = ScatterSum(matrices1)
    total1.across(jax.tree.leaves(matrices1)[0])
    event = scatter1.turn(total1.back())
    matrices1, steps1, states1 = scatter1.result(place, (), event)
    grad1, g_low0, grad_scaled0, sums0_back = finish_call(
        place, total1.quarters(), cot, x1, front1[2], packs[1], (steps1,), branch0, sums0, outs0
    )

    gate_back0 = layer_gate_back(grad_scaled0, sums0_back, comb0, z0, front0, rate_wide0, 0)
    ahead = half_b.hold(sums0_back), half_a.spread(sums0_back)
    back0 = layer_mix_back(
        gate_back0, front0, entry0, 0, ahead, lambda tick: ()
    )
    tick = back0[3]
    grad_got1 = swap(grad1, "section")
    keep0, send0, pieces, vector, vector_send = layer_down(
        back0,
        low0,
        tokens,
        front0,
        0,
        fronts0,
        gates0,
        (small1,),
        half_b.back(tick),
        half_a.others[0],
        grad_got1,
    )
    x2 = join_call(place, x1, half_a.quarters() + half_b.quarters(), keep0)
    *gives, send0 = hold_call([give for _, give, _ in pieces] + [send0], x2)
    total0 = TensorSum([(half, give, keep) for (half, _, keep), give in zip(pieces, gives)])
    received0 = swap(send0, "section")
    (vector,) = merge_call([vector], [swap(vector_send, "section")], F32)
    (vector,) = merge_call([vector], [sum_given(vector, "fsdp")], F32)
    (vector,) = merge_call([vector], [sum_given(vector, "context")], F32)
    matrices0 = wgrad_call(
        place,
        spans,
        normed0,
        normed_other0,
        g_low0,
        grad_got1,
        keep0,
        received0,
        vector,
    )
    scatter0 = ScatterSum(matrices0)
    event = total0.across(jax.tree.leaves(matrices0)[0])
    x2_other = swap(x2, "section")
    event = scatter0.turn(event)
    event = total0.back(event)
    layer_out, event = tokens_call(place, x1, x1_other, x2, x2_other, event)
    (vector,) = hold_call([vector], event)
    count = lax.axis_size("tensor")
    vectors = [vector] + [
        lax.ppermute(vector, "tensor", [(i, (i + by) % count) for i in range(count)])
        for by in range(1, count)
    ]
    row = np.arange(PACK)[:, None]
    lane = np.arange(both)[None, :]
    shared = ((row < SKIP) & (lane >= width)) | (row == NORM) | (row == NORM + 1)
    shared = jnp.asarray(shared.astype(np.float32))
    vector = vector_call(shared, vectors)
    matrices0, steps0, *states = scatter0.result(place, (states1,), event)
    states = TensorSum([(0, *states[:2]), (1, *states[2:])])
    matrices_got1 = swap(matrices1, "section")
    matrices_got0 = swap(matrices0, "section")
    grad0 = finish_call(
        place,
        total0.quarters(),
        grad1,
        tokens,
        front0[2],
        packs[0],
        (states.across(vector),),
    )[0]
    grad_got0 = swap(grad0.astype(BF16), "section")
    event = states.back(grad0)
    layer_in_grad, event = tokens_call(place, grad0, grad_got0, grad1, grad_got1, event)
    rest = rest_call(place, states.quarters(), steps0, steps1, event)
    grad_main, grad_states, grad_step, grad_out = matrices_call(
        place,
        heads,
        matrices0,
        matrices_got0,
        matrices1,
        matrices_got1,
        rest,
        swap(rest, "section"),
    )
    return (
        layer_out,
        layer_in_grad,
        vector[NORM : NORM + 2, : model // 2].reshape(1, model),
        grad_main,
        grad_states,
        grad_step,
        vector[None, TAPS : TAPS + CONV, :width],
        vector[BIAS : BIAS + 1, :width],
        vector[None, TAPS : TAPS + CONV, width:],
        vector[BIAS : BIAS + 1, width:],
        vector[STEP : STEP + 1, :heads],
        vector[DECAY : DECAY + 1, :heads],
        vector[SKIP : SKIP + 1, :heads],
        vector[GATED : GATED + 1, :width],
        grad_out,
    )


def solution(mesh):
    placed = (
        P("fsdp", "context", None),
        P("fsdp", "context"),
        P("fsdp", "context", None),
        P("section", None),
        P("section", "fsdp", None, "tensor"),
        P("section", "fsdp", None),
        P("section", "fsdp", "tensor"),
        P("section", None, "tensor"),
        P("section", "tensor"),
        P("section", None, None),
        P("section", None),
        P("section", "tensor"),
        P("section", "tensor"),
        P("section", "tensor"),
        P("section", "tensor"),
        P("section", "fsdp", "tensor"),
    )
    return jax.shard_map(
        shards,
        mesh=mesh,
        in_specs=placed,
        out_specs=(
            P("section", "fsdp", "context", None),
            P("section", "fsdp", "context", None),
            P("section", None),
            P("section", ("fsdp", "context"), None, "tensor"),
            P("section", ("fsdp", "context"), None),
            P("section", ("fsdp", "context"), "tensor"),
            P("section", None, "tensor"),
            P("section", "tensor"),
            P("section", None, None),
            P("section", None),
            P("section", "tensor"),
            P("section", "tensor"),
            P("section", "tensor"),
            P("section", "tensor"),
            P("section", ("fsdp", "context"), "tensor"),
        ),
        check_vma=False,
    )
```

```python
import functools

import jax
import jax.numpy as jnp
import numpy as np
from jax import lax
from jax.experimental import pallas as pl
from jax.experimental.pallas import tpu as pltpu
from jax.sharding import PartitionSpec as P

HEAD_DIM = 64
NSTATE = 128
CONV = 4
SPAN = 128
INNER = 3072
LANES = 128
EPS = 1e-05
BREAK = 128.0
HIGH = lax.Precision.HIGHEST
F32 = jnp.float32
BF16 = jnp.bfloat16

NT = (((1,), (1,)), ((), ()))
TN = (((0,), (0,)), ((), ()))


def mm(a, b, dims=(((1,), (0,)), ((), ()))):
    return lax.dot_general(a, b, dims, preferred_element_type=F32)


def exact(a, b):
    return lax.dot_general(a, b, (((1,), (0,)), ((), ())), precision=HIGH, preferred_element_type=F32)


def halves(a):
    top = a.astype(BF16)
    return top, (a - top.astype(F32)).astype(BF16)


def spread(a, spread_matrix):
    top, rest = halves(a)
    return mm(jnp.concatenate([top, rest], axis=1), spread_matrix)


def gather_heads(a, gather_matrix):
    top, rest = halves(a)
    return mm(jnp.concatenate([top, rest], axis=1), gather_matrix)


def logistic(v):
    return 0.5 * jnp.tanh(0.5 * v) + 0.5


def softplus(v):
    u = jnp.exp(-jnp.abs(v))
    small = u * (1.0 - u * (0.5 - u * (1.0 / 3.0)))
    return jnp.maximum(v, 0.0) + jnp.where(u < 1e-3, small, jnp.log(1.0 + u))


def lower_ones(rows):
    t = lax.broadcasted_iota(jnp.int32, (rows, rows), 0)
    s = lax.broadcasted_iota(jnp.int32, (rows, rows), 1)
    return t >= s


def pair_masks():
    lane = lax.broadcasted_iota(jnp.int32, (1, LANES), 1)
    first = (lane < HEAD_DIM).astype(BF16)
    return first, (1.0 - first.astype(F32)).astype(BF16)


def both_halves(a):
    top, rest = halves(a)
    return jnp.concatenate([top, rest], axis=1)


def triple(a, b):
    a_top, a_rest = halves(a)
    b_top, b_rest = halves(b)
    return (
        jnp.concatenate([a_top, a_rest, a_top], axis=1),
        jnp.concatenate([b_top, b_top, b_rest], axis=1),
    )


def twice(a):
    return jnp.concatenate([a, a], axis=0)


def chunk_of(rows, width, reverse=0):
    if reverse:
        return pl.BlockSpec((rows, width), lambda c: (reverse - 1 - c, 0))
    return pl.BlockSpec((rows, width), lambda c: (c, 0))


def lanes_of(rows, reverse=0):
    if reverse:
        return pl.BlockSpec((8, rows), lambda c: (0, reverse - 1 - c))
    return pl.BlockSpec((8, rows), lambda c: (0, c))


def stack_of(rows, width, reverse=0):
    if reverse:
        return pl.BlockSpec((1, rows, width), lambda c: (reverse - 1 - c, 0, 0))
    return pl.BlockSpec((1, rows, width), lambda c: (c, 0, 0))


def whole_of(rows, width):
    return pl.BlockSpec((rows, width), lambda c: (0, 0))


def scalars_of():
    return pl.BlockSpec(memory_space=pltpu.SMEM)


def anywhere(count):
    return [pl.BlockSpec(memory_space=pltpu.HBM)] * count


def params_of(mebibytes):
    return pltpu.CompilerParams(
        dimension_semantics=("arbitrary",), vmem_limit_bytes=mebibytes * 1024 * 1024
    )


def shape(*dims, dtype=F32):
    return jax.ShapeDtypeStruct(dims, dtype)


CORE, FIRST, ODD, RIGHT, ALONG_X, ALONG_Y = range(6)


def ordered_call(kernel, ahead, in_specs, **options):
    count, extra = len(in_specs), len(ahead)

    def body(*refs):
        kernel(*refs[:count], *refs[count + extra :])

    call = pl.pallas_call(
        body, in_specs=list(in_specs) + [pl.BlockSpec(memory_space=pl.ANY)] * extra, **options
    )
    return lambda *operands: call(*operands, *ahead)


def cost(flops, moved):
    return pl.CostEstimate(flops=1, bytes_accessed=1, transcendentals=0)


def weight_copies(spec, where_ref, refs, buffer, sems, held):
    first, core = where_ref[FIRST], where_ref[CORE]
    _, near, (far_start, far_size) = spec
    rows = buffer.shape[0] // 2
    near_at = pl.ds(pl.multiple_of((1 - first) * rows, rows), rows)
    far = first * rows
    step = rows // 2
    copies = []
    column = 0
    for n, (start, size) in enumerate(near):
        copies.append(
            pltpu.make_async_copy(
                refs[2 * n if held else 2 * n + 1].at[:, start : start + size],
                buffer.at[near_at, column : column + size],
                sems.at[len(copies)],
            )
        )
        column += size
    for ref, which in ((refs[-2], core), (refs[-1], 1 - core)):
        part = buffer.at[pl.ds(pl.multiple_of(far + which * step, step), step)]
        source = ref.at[:, far_start : far_start + far_size]
        copies.append(pltpu.make_async_copy(source, part, sems.at[len(copies)]))
    return copies


def start_weights(spec, where_ref, refs, buffer, sems):
    for held in (True, False):

        @pl.when((where_ref[CORE] == spec[0]) == held)
        def _():
            for copy in weight_copies(spec, where_ref, refs, buffer, sems, held):
                copy.start()


def wait_weights(spec, where_ref, refs, buffer, sems):
    for copy in weight_copies(spec, where_ref, refs, buffer, sems, True):
        copy.wait()


def load_weights(spec, where_ref, refs, buffer, sems):
    start_weights(spec, where_ref, refs, buffer, sems)
    wait_weights(spec, where_ref, refs, buffer, sems)


def weight_scratch(weights):
    (_, _, (_, width)), arrays = weights
    return [pltpu.VMEM((2 * arrays[0].shape[0], width), BF16), pltpu.SemaphoreType.DMA((4,))]


def pieces_kernel(layer, parts, where_ref, *refs):
    out_ref, sems = refs[-2:]
    rows = out_ref.shape[0]
    mine = pl.ds(pl.multiple_of(where_ref[CORE] * rows, rows), rows)

    def copies(held):
        column = 0
        for n, (array, start, size) in enumerate(parts):
            source = refs[2 * array if held else 2 * array + 1]
            yield pltpu.make_async_copy(
                source.at[mine, start : start + size], out_ref.at[:, column : column + size], sems.at[n]
            )
            column += size

    for held in (True, False):

        @pl.when((where_ref[CORE] == layer) == held)
        def _():
            for copy in copies(held):
                copy.start()

    for copy in copies(True):
        copy.wait()


def pieces_call(where, layer, parts, arrays, *ahead):
    rows = arrays[0].shape[0] // 2
    total = sum(size for _, _, size in parts)
    return ordered_call(
        functools.partial(pieces_kernel, layer, parts),
        ahead,
        in_specs=[scalars_of()] + anywhere(len(arrays)),
        out_specs=pl.BlockSpec(memory_space=pltpu.VMEM),
        out_shape=shape(rows, total, dtype=BF16),
        scratch_shapes=[pltpu.SemaphoreType.DMA((len(parts),))],
        compiler_params=pltpu.CompilerParams(vmem_limit_bytes=8 * 1024 * 1024),
        cost_estimate=cost(0, 4 * rows * total),
        name="pieces",
    )(where, *arrays)


def joined(where_ref, refs, at, digits=(ODD, RIGHT)):
    quarter = refs[0].shape[0]
    rows = []
    for n in range(at.start // quarter, at.stop // quarter):
        half, place = divmod(n, 2)
        own, other = refs[2 * half][...].astype(F32), refs[2 * half + 1][...].astype(F32)
        rows.append(jnp.where(where_ref[digits[half]] == place, own, other))
    return rows[0] if len(rows) == 1 else jnp.concatenate(rows, axis=0)


def put_quarters(where_ref, value, refs, digits=(ODD, RIGHT)):
    quarter = value.shape[0] // 4
    for half in range(2):
        digit = where_ref[digits[half]]
        first = value[2 * half * quarter : (2 * half + 1) * quarter]
        second = value[(2 * half + 1) * quarter : (2 * half + 2) * quarter]
        refs[2 * half][...] = jnp.where(digit == 1, first, second).astype(refs[2 * half].dtype)
        refs[2 * half + 1][...] = jnp.where(digit == 1, second, first).astype(refs[2 * half + 1].dtype)


def quarter_shapes(length, model, kind):
    return [shape(length // 4, model, dtype=kind), shape(length // 4, model)] * 2


def merge_kernel(*refs):
    count = len(refs) // 3
    for a_ref, b_ref, out_ref in zip(refs[:count], refs[count : 2 * count], refs[2 * count :]):
        out_ref[...] = (a_ref[...].astype(F32) + b_ref[...].astype(F32)).astype(out_ref.dtype)


def merge_call(firsts, seconds, kind, *ahead):
    return ordered_call(
        merge_kernel,
        ahead,
        in_specs=[pl.BlockSpec(memory_space=pltpu.VMEM)] * (2 * len(firsts)),
        out_specs=[pl.BlockSpec(memory_space=pltpu.VMEM)] * len(firsts),
        out_shape=[shape(*a.shape, dtype=kind) for a in firsts],
        compiler_params=pltpu.CompilerParams(vmem_limit_bytes=10 * 1024 * 1024),
        cost_estimate=cost(0, 0),
        name="merge",
    )(*firsts, *seconds)


def hold_kernel(*refs):
    count = len(refs) // 2
    for in_ref, out_ref in zip(refs[:count], refs[count:]):
        out_ref[...] = in_ref[...]


def hold_call(arrays, *ahead):
    return ordered_call(
        hold_kernel,
        ahead,
        in_specs=[pl.BlockSpec(memory_space=pltpu.VMEM)] * len(arrays),
        out_specs=[pl.BlockSpec(memory_space=pltpu.VMEM)] * len(arrays),
        out_shape=[shape(*v.shape, dtype=v.dtype) for v in arrays],
        compiler_params=pltpu.CompilerParams(vmem_limit_bytes=12 * 1024 * 1024),
        cost_estimate=cost(0, 0),
        name="hold",
    )(*arrays)


def vector_kernel(mask_ref, a_ref, b_ref, c_ref, d_ref, out_ref):
    total = a_ref[...] + b_ref[...] + c_ref[...] + d_ref[...]
    out_ref[...] = jnp.where(mask_ref[...] > 0.0, total, a_ref[...])


def vector_call(mask, values, *ahead):
    return ordered_call(
        vector_kernel,
        ahead,
        in_specs=[pl.BlockSpec(memory_space=pltpu.VMEM)] * 5,
        out_specs=pl.BlockSpec(memory_space=pltpu.VMEM),
        out_shape=shape(*mask.shape),
        compiler_params=pltpu.CompilerParams(vmem_limit_bytes=4 * 1024 * 1024),
        cost_estimate=cost(0, 0),
        name="vector",
    )(mask, *values)


def join_kernel(where_ref, x_ref, t0, o0, t1, o1, out_ref):
    length = x_ref.shape[0]
    rows = min(SPAN, length)
    for r in range(length // rows):
        at = slice(r * rows, (r + 1) * rows)
        out_ref[at, :] = x_ref[at, :] + joined(where_ref, (t0, o0, t1, o1), at, (ODD, ODD))


def join_call(where, x, quarters, *ahead):
    return ordered_call(
        join_kernel,
        ahead,
        in_specs=[scalars_of()] + [pl.BlockSpec(memory_space=pltpu.VMEM)] * 5,
        out_specs=pl.BlockSpec(memory_space=pltpu.VMEM),
        out_shape=shape(*x.shape),
        compiler_params=pltpu.CompilerParams(vmem_limit_bytes=16 * 1024 * 1024),
        cost_estimate=cost(0, 0),
        name="join",
    )(where, x, *quarters)


TAPS, BIAS, SKIP, GATED, NORM, STEP, DECAY, PACK = 0, 4, 8, 9, 10, 12, 13, 16


def pack_kernel(taps_a, taps_b, bias_a, bias_b, skip, gated, norm, step, decay, pack_ref):
    width = taps_a.shape[1]
    half = norm.shape[1] // 2
    pack_ref[...] = jnp.zeros_like(pack_ref)
    pack_ref[TAPS : TAPS + CONV, :width] = taps_a[...]
    pack_ref[TAPS : TAPS + CONV, width:] = taps_b[...]
    pack_ref[BIAS : BIAS + 1, :width] = bias_a[...]
    pack_ref[BIAS : BIAS + 1, width:] = bias_b[...]
    pack_ref[SKIP : SKIP + 1, :width] = skip[...]
    pack_ref[GATED : GATED + 1, :width] = gated[...]
    pack_ref[NORM : NORM + 1, :half] = norm[:, :half]
    pack_ref[NORM + 1 : NORM + 2, :half] = norm[:, half:]
    pack_ref[STEP : STEP + 1, :LANES] = step[...]
    pack_ref[DECAY : DECAY + 1, :LANES] = decay[...]


def norm_row(pack_ref, half):
    return jnp.concatenate([pack_ref[NORM : NORM + 1, :half], pack_ref[NORM + 1 : NORM + 2, :half]], axis=1)


def front_kernel(
    spec,
    where_ref,
    x_ref,
    halo_ref,
    tok_ref,
    pack_ref,
    spread_ref,
    w0,
    w1,
    w2,
    w3,
    w4,
    w5,
    *refs,
):
    if spec[0] == 1:
        quarters, refs = refs[:4], refs[4:]
    else:
        quarters = None
    front_body(spec, where_ref, x_ref, halo_ref, tok_ref, pack_ref, spread_ref, (w0, w1, w2, w3, w4, w5), quarters, *refs)


def front_body(
    spec,
    where_ref,
    x_ref,
    halo_ref,
    tok_ref,
    pack_ref,
    spread_ref,
    held,
    quarters,
    sum_ref,
    normed_ref,
    inv_ref,
    pre_ref,
    conv_x_ref,
    conv_s_ref,
    raw_ref,
    step_ref,
    cum_ref,
    entry_ref,
    rate_ref,
    end_ref,
    end_rate_ref,
    weights,
    sems,
    ext,
    cols,
    state,
    total,
):
    rows, width = conv_x_ref.shape
    length, model = x_ref.shape
    both = width + 2 * NSTATE
    chunk = pl.program_id(0)

    @pl.when(chunk == 0)
    def _():
        start_weights(spec, where_ref, held, weights, sems)
        gain = norm_row(pack_ref, model // 2)

        def normalize(v):
            inv = lax.rsqrt(jnp.mean(v * v, axis=-1, keepdims=True) + EPS)
            return (v * inv * gain).astype(BF16), inv

        for r in range(length // rows):
            at = slice(r * rows, (r + 1) * rows)
            x = x_ref[at, :].astype(F32)
            if quarters is not None:
                x = x + joined(where_ref, quarters, at)
                sum_ref[at, :] = x
            normed, inv = normalize(x)
            normed_ref[at, :] = normed
            inv_ref[at, :] = jnp.broadcast_to(inv, (rows, LANES))
        halo, _ = normalize(halo_ref[...].astype(F32))
        wait_weights(spec, where_ref, held, weights, sems)
        ext[0:8, :] = mm(halo, weights[:, :both])
        cols[...] = mm(normed_ref[...], weights[...])
        state[...] = jnp.zeros_like(state)
        total[...] = jnp.ones_like(total)

    @pl.when(chunk > 0)
    def _():
        ext[0:8, :] = ext[rows : rows + 8, :]

    here = pl.ds(pl.multiple_of(chunk * rows, rows), rows)
    pre = cols[here, :both]
    raw = cols[here, both:]
    pre_ref[...] = pre
    raw_ref[...] = raw
    ext[8 : 8 + rows, :] = pre
    conv = pack_ref[BIAS : BIAS + 1, :] + pack_ref[TAPS : TAPS + 1, :] * pre
    for k in range(1, CONV):
        conv = conv + tok_ref[:, k : k + 1] * (
            pack_ref[TAPS + k : TAPS + k + 1, :] * ext[8 - k : 8 - k + rows, :]
        )
    conv_x_ref[...] = conv[:, :width]
    conv_s_ref[...] = conv[:, width:]
    conv_x = conv[:, :width]
    conv_b = conv[:, width : width + NSTATE]
    values = conv_x * logistic(conv_x)
    b_part = conv_b * logistic(conv_b)
    step = softplus(raw + pack_ref[STEP : STEP + 1, :LANES])
    decay = -jnp.exp(pack_ref[DECAY : DECAY + 1, :LANES]) * step
    cum = exact(lower_ones(rows).astype(F32), decay - BREAK * tok_ref[:, 0:1])
    step_ref[...] = step
    cum_ref[...] = cum
    last = cum[rows - 1 : rows, :]
    spread_matrix = spread_ref[...]
    carried = (spread(jnp.exp(last - cum) * step, spread_matrix) * values).astype(BF16)
    before = state[...]
    entry_ref[0] = before
    rate_ref[0] = total[...]
    kept = spread(jnp.exp(cum[rows - 8 : rows, :]), spread_matrix)[7:8, :]
    grown = mm(both_halves(b_part), carried, TN)
    new_state = kept * before + (grown[:NSTATE] + grown[NSTATE:])
    state[...] = new_state
    end_ref[...] = new_state
    new_total = total[...] * jnp.exp(last)
    total[...] = new_total
    end_rate_ref[...] = new_total


def front_call(where, x, halo, tok, pack, spread_matrix, weights, quarters, *ahead):
    length, model = x.shape
    all_width = weights[0][2][1]
    both = all_width - LANES
    width = both - 2 * NSTATE
    rows = min(SPAN, length)
    chunks = length // rows
    return ordered_call(
        functools.partial(front_kernel, weights[0]),
        ahead,
        grid=(chunks,),
        in_specs=[
            scalars_of(),
            whole_of(length, model),
            whole_of(8, model),
            chunk_of(rows, LANES),
            whole_of(PACK, both),
            whole_of(2 * LANES, width),
        ]
        + anywhere(6)
        + [whole_of(length // 4, model)] * len(quarters),
        out_specs=[
            whole_of(length, model) if quarters else whole_of(8, model),
            whole_of(length, model),
            whole_of(length, LANES),
            chunk_of(rows, both),
            chunk_of(rows, width),
            chunk_of(rows, 2 * NSTATE),
            chunk_of(rows, LANES),
            chunk_of(rows, LANES),
            chunk_of(rows, LANES),
            stack_of(NSTATE, width),
            stack_of(8, LANES),
            whole_of(NSTATE, width),
            whole_of(8, LANES),
        ],
        out_shape=[
            shape(length, model) if quarters else shape(8, model),
            shape(length, model, dtype=BF16),
            shape(length, LANES),
            shape(length, both),
            shape(length, width),
            shape(length, 2 * NSTATE),
            shape(length, LANES),
            shape(length, LANES),
            shape(length, LANES),
            shape(chunks, NSTATE, width),
            shape(chunks, 8, LANES),
            shape(NSTATE, width),
            shape(8, LANES),
        ],
        scratch_shapes=weight_scratch(weights)
        + [
            pltpu.VMEM((rows + 8, both), F32),
            pltpu.VMEM((length, all_width), F32),
            pltpu.VMEM((NSTATE, width), F32),
            pltpu.VMEM((8, LANES), F32),
        ],
        compiler_params=params_of(32),
        cost_estimate=cost(2 * length * model * all_width, 24 * length * width),
        name="front",
    )(where, x, halo, tok, pack, spread_matrix, *weights[1], *quarters)


def project_kernel(spec, where_ref, a_ref, w0, w1, w2, w3, out_ref, weights, sems):
    tile = out_ref.shape[1]

    @pl.when(pl.program_id(0) == 0)
    def _():
        load_weights(spec, where_ref, (w0, w1, w2, w3), weights, sems)

    at = pl.ds(pl.multiple_of(pl.program_id(0) * tile, tile), tile)
    out_ref[...] = mm(a_ref[...], weights[:, at])


def project_call(where, a, weights, *ahead):
    length, model = a.shape
    width = weights[0][2][1]
    tile = 2 * LANES
    return ordered_call(
        functools.partial(project_kernel, weights[0]),
        ahead,
        grid=(width // tile,),
        in_specs=[scalars_of(), whole_of(length, model)] + anywhere(4),
        out_specs=pl.BlockSpec((length, tile), lambda n: (0, n)),
        out_shape=shape(length, width),
        scratch_shapes=weight_scratch(weights),
        compiler_params=params_of(12),
        cost_estimate=cost(2 * length * model * width, 4 * length * width),
        name="project",
    )(where, a, *weights[1])


def mix_kernel(conv_x_ref, conv_s_ref, step_ref, cum_ref, entry_ref, spread_ref, y_ref):
    rows, width = conv_x_ref.shape
    conv_x = conv_x_ref[...]
    conv_s = conv_s_ref[...]
    values = conv_x * logistic(conv_x)
    bc = conv_s * logistic(conv_s)
    b_part, c_part = bc[:, :NSTATE], bc[:, NSTATE:]
    cum = cum_ref[...]
    spread_matrix = spread_ref[...]
    grown = spread(jnp.exp(cum), spread_matrix)
    stepped = (spread(step_ref[...], spread_matrix) * values).astype(BF16)
    from_entry = grown * mm(both_halves(c_part), twice(entry_ref[0].astype(BF16)))
    scores = jnp.where(lower_ones(rows), mm(*triple(c_part, b_part), NT), 0.0)
    cum_t = cum.T
    first, second = pair_masks()
    for j in range(width // LANES):
        parts = []
        for h in (2 * j, 2 * j + 1):
            gap = jnp.minimum(cum[:, h : h + 1] - cum_t[h : h + 1, :], 0.0)
            parts.append((scores * jnp.exp(gap)).astype(BF16))
        pair = stepped[:, j * LANES : (j + 1) * LANES]
        y_ref[:, j * LANES : (j + 1) * LANES] = from_entry[:, j * LANES : (j + 1) * LANES] + mm(
            jnp.concatenate(parts, axis=1), jnp.concatenate([pair * first, pair * second], axis=0)
        )


def mix_call(conv_x, conv_s, step, cum, entry, spread_matrix, *ahead):
    length, width = conv_x.shape
    rows = min(SPAN, length)
    return ordered_call(
        mix_kernel,
        ahead,
        grid=(length // rows,),
        in_specs=[
            chunk_of(rows, width),
            chunk_of(rows, 2 * NSTATE),
            chunk_of(rows, LANES),
            chunk_of(rows, LANES),
            stack_of(NSTATE, width),
            whole_of(2 * LANES, width),
        ],
        out_specs=chunk_of(rows, width),
        out_shape=shape(length, width),
        compiler_params=params_of(12),
        cost_estimate=cost(16 * length * rows * width, 12 * length * width),
        name="mix",
    )(conv_x, conv_s, step, cum, entry, spread_matrix)


def gate_kernel(
    with_dot,
    y_ref,
    z_ref,
    conv_x_ref,
    conv_s_ref,
    cum_ref,
    rate_ref,
    entry_ref,
    pack_ref,
    spread_ref,
    *refs,
):
    comb_ref, gated_ref, sums_ref = refs[-3:]
    rows, width = y_ref.shape
    spread_matrix = spread_ref[...]
    c_part = conv_s_ref[:, NSTATE:]
    c_part = c_part * logistic(c_part)
    reach = spread(rate_ref[0], spread_matrix)[0:1, :]
    grown = spread(jnp.exp(cum_ref[...]), spread_matrix)
    mixed = y_ref[...] + grown * mm(
        both_halves(c_part), twice((reach * entry_ref[...]).astype(BF16))
    )
    conv = conv_x_ref[...]
    comb = mixed + pack_ref[SKIP : SKIP + 1, :width] * (conv * logistic(conv))
    comb_ref[...] = comb
    z = z_ref[...]
    gated = comb * (z * logistic(z))
    gated_ref[...] = gated
    square = jnp.sum(gated * gated, axis=1, keepdims=True)
    lane = lax.broadcasted_iota(jnp.int32, (rows, LANES), 1)
    sums = jnp.where(lane == 0, square, 0.0)
    if with_dot:
        gain = pack_ref[GATED : GATED + 1, :width]
        dot = jnp.sum(gated * gain * refs[0][...], axis=1, keepdims=True)
        sums = jnp.where(lane == 1, dot, sums)
    sums_ref[...] = sums.T[0:8, :]


def gate_call(y, z, conv_x, conv_s, cum, rate, entry, pack, spread_matrix, *grad_scaled):
    length, width = y.shape
    rows = min(SPAN, length)
    chunks = length // rows
    return pl.pallas_call(
        functools.partial(gate_kernel, bool(grad_scaled)),
        grid=(chunks,),
        in_specs=[
            chunk_of(rows, width),
            chunk_of(rows, width),
            chunk_of(rows, width),
            chunk_of(rows, 2 * NSTATE),
            chunk_of(rows, LANES),
            stack_of(8, LANES),
            whole_of(NSTATE, width),
            whole_of(*pack.shape),
            whole_of(2 * LANES, width),
        ]
        + [chunk_of(rows, width)] * len(grad_scaled),
        out_specs=[chunk_of(rows, width), chunk_of(rows, width), lanes_of(rows)],
        out_shape=[shape(length, width), shape(length, width), shape(8, length)],
        compiler_params=params_of(12),
        cost_estimate=cost(4 * length * NSTATE * width, 28 * length * width),
        name="gate",
    )(y, z, conv_x, conv_s, cum, rate, entry, pack, spread_matrix, *grad_scaled)


def columns(lanes):
    rows = lanes.shape[1]
    return jnp.concatenate([lanes, jnp.zeros((LANES - 8, rows), F32)], axis=0).T


def out_kernel(
    spec, where_ref, gated_ref, sums_ref, pack_ref, w0, w1, w2, w3, low_ref, g0, k0, g1, k1, edge_ref, weights, sems
):
    tile = edge_ref.shape[1]
    length, width = gated_ref.shape

    @pl.when(pl.program_id(0) == 0)
    def _():
        start_weights(spec, where_ref, (w0, w1, w2, w3), weights, sems)
        gain = pack_ref[GATED : GATED + 1, :width]
        rows = min(SPAN, length)
        for r in range(length // rows):
            at = slice(r * rows, (r + 1) * rows)
            inv = lax.rsqrt(columns(sums_ref[:, at])[:, 0:1] * (1.0 / INNER) + EPS)
            low_ref[at, :] = (gated_ref[at, :] * inv * gain).astype(BF16)
        wait_weights(spec, where_ref, (w0, w1, w2, w3), weights, sems)

    at = pl.ds(pl.multiple_of(pl.program_id(0) * tile, tile), tile)
    branch = mm(low_ref[...], weights[at, :], NT)
    put_quarters(where_ref, branch, (g0, k0, g1, k1), (ODD, (RIGHT, ODD)[spec[0]]))
    edge_ref[...] = branch[length - 8 :]


def out_call(where, gated, sums, pack, weights, kind, *ahead):
    length, width = gated.shape
    model = 2 * weights[1][0].shape[0]
    tile = model // 4
    return ordered_call(
        functools.partial(out_kernel, weights[0]),
        ahead,
        grid=(model // tile,),
        in_specs=[scalars_of(), whole_of(length, width), whole_of(8, length), whole_of(*pack.shape)]
        + anywhere(4),
        out_specs=[
            whole_of(length, width),
        ]
        + [pl.BlockSpec((length // 4, tile), lambda n: (0, n))] * 4
        + [pl.BlockSpec((8, tile), lambda n: (0, n))],
        out_shape=[
            shape(length, width, dtype=BF16),
        ]
        + quarter_shapes(length, model, kind)
        + [shape(8, model)],
        scratch_shapes=weight_scratch(weights),
        compiler_params=params_of(14),
        cost_estimate=cost(2 * length * model * width, 8 * length * width),
        name="out",
    )(where, gated, sums, pack, *weights[1])


def finish_kernel(spec, where_ref, g_ref, x_ref, inv_ref, pack_ref, t0, o0, t1, o1, *refs):
    rows, model = g_ref.shape
    chunk = pl.program_id(0)
    *refs, grad = refs

    @pl.when(chunk == 0)
    def _():
        for r in range(grad.shape[0] // rows):
            at = slice(r * rows, (r + 1) * rows)
            grad[at, :] = joined(where_ref, (t0, o0, t1, o1), at).astype(BF16)

    gain = norm_row(pack_ref, model // 2)
    x = x_ref[...].astype(F32)
    inv = inv_ref[:, 0:1]
    weighted = grad[pl.ds(pl.multiple_of(chunk * rows, rows), rows), :].astype(F32) * gain
    mean = jnp.mean(weighted * x, axis=-1, keepdims=True)
    result = g_ref[...].astype(F32) + inv * weighted - x * (inv * inv * inv * mean)
    if spec is None:
        refs[0][...] = result
        return
    b0, b1, b2, b3, sums_ref, w0, w1, w2, w3, out_ref, low_ref, scaled_ref, new_sums_ref, weights, sems, branch = refs
    length = branch.shape[0]
    candidates = (w0, w1, w2, w3)

    @pl.when(chunk == 0)
    def _():
        start_weights(spec, where_ref, candidates, weights, sems)
        for r in range(length // rows):
            at = slice(r * rows, (r + 1) * rows)
            branch[at, :] = joined(where_ref, (b0, b1, b2, b3), at)

    out_ref[...] = result
    low = result.astype(BF16)
    low_ref[pl.ds(pl.multiple_of(chunk * rows, rows), rows), :] = low
    here = branch[pl.ds(pl.multiple_of(chunk * rows, rows), rows), :]
    dot = jnp.sum(low.astype(F32) * here, axis=1, keepdims=True)
    square = columns(sums_ref[...])[:, 0:1]
    dot = dot / lax.rsqrt(square * (1.0 / INNER) + EPS)
    lane = lax.broadcasted_iota(jnp.int32, (rows, LANES), 1)
    sums = jnp.where(lane == 0, square, jnp.where(lane == 1, dot, 0.0))
    new_sums_ref[...] = sums.T[0:8, :]

    @pl.when(chunk == pl.num_programs(0) - 1)
    def _():
        wait_weights(spec, where_ref, candidates, weights, sems)
        scaled_ref[...] = mm(low_ref[...], weights[...])


def finish_call(where, quarters, g, x, inv, pack, ahead, branch=None, sums=None, weights=None):
    length, model = g.shape
    rows = min(SPAN, length)
    in_specs = [
        scalars_of(),
        chunk_of(rows, model),
        chunk_of(rows, model),
        chunk_of(rows, LANES),
        whole_of(*pack.shape),
    ] + [whole_of(length // 4, model)] * 4
    out_specs = [chunk_of(rows, model)]
    out_shape = [shape(length, model)]
    scratch = [pltpu.VMEM((length, model), BF16)]
    more = ()
    if weights is not None:
        width = weights[0][2][1]
        in_specs += [whole_of(length // 4, model)] * 4 + [lanes_of(rows)] + anywhere(4)
        out_specs += [whole_of(length, model), whole_of(length, width), lanes_of(rows)]
        out_shape += [shape(length, model, dtype=BF16), shape(length, width), shape(8, length)]
        scratch = weight_scratch(weights) + [pltpu.VMEM((length, model), F32)] + scratch
        more = tuple(branch) + (sums,) + tuple(weights[1])
    return ordered_call(
        functools.partial(finish_kernel, None if weights is None else weights[0]),
        ahead,
        grid=(length // rows,),
        in_specs=in_specs,
        out_specs=out_specs,
        out_shape=out_shape,
        scratch_shapes=scratch,
        compiler_params=params_of(28),
        cost_estimate=cost(length * model * 800, 16 * length * model),
        name="finish",
    )(where, g, x, inv, pack, *quarters, *more)


def gate_back_kernel(
    scaled_ref,
    comb_ref,
    z_ref,
    conv_s_ref,
    cum_ref,
    sums_ref,
    pack_ref,
    spread_ref,
    dmix_ref,
    dz_ref,
    adj_ref,
    rate_ref,
    begin_ref,
    gain_ref,
    state,
    total,
):
    chunk = pl.program_id(0)
    rows, width = z_ref.shape

    @pl.when(chunk == 0)
    def _():
        state[...] = jnp.zeros_like(state)
        total[...] = jnp.ones_like(total)
        gain_ref[...] = jnp.zeros_like(gain_ref)

    sums = columns(sums_ref[...])
    inv = lax.rsqrt(sums[:, 0:1] * (1.0 / INNER) + EPS)
    dot = sums[:, 1:2]
    grad_scaled = scaled_ref[...]
    comb = comb_ref[...]
    z = z_ref[...]
    sig = logistic(z)
    act = z * sig
    gated = comb * act
    gain_ref[0:1, :] += jnp.sum(grad_scaled * (gated * inv), axis=0, keepdims=True)
    grad_gated = inv * (grad_scaled * pack_ref[GATED : GATED + 1, :width]) - gated * (inv * inv * inv * dot * (1.0 / INNER))
    dmix = grad_gated * act
    dmix_ref[...] = dmix
    dz_ref[...] = (grad_gated * comb * (sig * (1.0 + z * (1.0 - sig)))).astype(BF16)
    c_part = conv_s_ref[:, NSTATE:]
    c_part = c_part * logistic(c_part)
    cum = cum_ref[...]
    grown = spread(jnp.exp(cum), spread_ref[...])
    held = state[...]
    adj_ref[0] = held
    rate_ref[0] = total[...]
    added = mm(both_halves(c_part), (grown * dmix).astype(BF16), TN)
    new_state = grown[rows - 1 : rows, :] * held + (added[:NSTATE] + added[NSTATE:])
    state[...] = new_state
    begin_ref[...] = new_state
    total[...] = total[...] * jnp.exp(cum[rows - 1 : rows, :])


def gate_back_call(grad_scaled, comb, z, conv_s, cum, sums, pack, spread_matrix, *ahead):
    length, width = z.shape
    rows = min(SPAN, length)
    chunks = length // rows
    return ordered_call(
        gate_back_kernel,
        ahead,
        grid=(chunks,),
        in_specs=[
            chunk_of(rows, width, chunks),
            chunk_of(rows, width, chunks),
            chunk_of(rows, width, chunks),
            chunk_of(rows, 2 * NSTATE, chunks),
            chunk_of(rows, LANES, chunks),
            lanes_of(rows, chunks),
            whole_of(*pack.shape),
            whole_of(2 * LANES, width),
        ],
        out_specs=[
            chunk_of(rows, width, chunks),
            chunk_of(rows, width, chunks),
            stack_of(NSTATE, width, chunks),
            stack_of(8, LANES, chunks),
            whole_of(NSTATE, width),
            whole_of(8, width),
        ],
        out_shape=[
            shape(length, width),
            shape(length, width, dtype=BF16),
            shape(chunks, NSTATE, width),
            shape(chunks, 8, LANES),
            shape(NSTATE, width),
            shape(8, width),
        ],
        scratch_shapes=[pltpu.VMEM((NSTATE, width), F32), pltpu.VMEM((8, LANES), F32)],
        compiler_params=params_of(12),
        cost_estimate=cost(4 * length * NSTATE * width, 28 * length * width),
        name="gate_back",
    )(grad_scaled, comb, z, conv_s, cum, sums, pack, spread_matrix)


def mix_back_kernel(
    conv_x_ref,
    conv_s_ref,
    dmix_ref,
    step_ref,
    cum_ref,
    entry_ref,
    entry_rate_ref,
    entry_in_ref,
    adj_ref,
    spread_ref,
    gather_ref,
    ones_ref,
    grad_step_ref,
    grad_b_ref,
    grad_c_ref,
    decay_ref,
    skip_ref,
    flows,
):
    chunk = pl.program_id(0)
    rows, width = conv_x_ref.shape

    @pl.when(chunk == 0)
    def _():
        skip_ref[...] = jnp.zeros_like(skip_ref)

    spread_matrix = spread_ref[...]
    gather_matrix = gather_ref[...]
    conv = conv_x_ref[...]
    values = conv * logistic(conv)
    conv_s = conv_s_ref[...]
    bc = conv_s * logistic(conv_s)
    b_part, c_part = bc[:, :NSTATE], bc[:, NSTATE:]
    cum = cum_ref[...]
    dmix = dmix_ref[...]
    dmix_low = dmix.astype(BF16)
    last = cum[rows - 1 : rows, :]
    grown = spread(jnp.exp(cum), spread_matrix)
    left_wide = spread(jnp.exp(last - cum), spread_matrix)
    entry = entry_ref[0] + spread(entry_rate_ref[0], spread_matrix)[0:1, :] * entry_in_ref[...]
    adj = adj_ref[0]
    entry_low = entry.astype(BF16)
    adj_low = adj.astype(BF16)
    skip_ref[0:1, :] += jnp.sum(dmix * values, axis=0, keepdims=True)

    stepped = spread(step_ref[...], spread_matrix) * values
    stepped_low = stepped.astype(BF16)
    from_entry = grown * mm(both_halves(c_part), twice(entry_low))
    later = left_wide * mm(both_halves(b_part), twice(adj_low))
    grad_c = mm((grown * dmix).astype(BF16), entry_low, NT)
    grad_b = mm((left_wide * stepped).astype(BF16), adj_low, NT)

    t_after = lower_ones(rows).T
    scores = jnp.where(t_after, mm(*triple(b_part, c_part), NT), 0.0)
    cum_t = cum.T
    first, second = pair_masks()
    grad_scores = jnp.zeros((rows, rows), F32)
    for j in range(width // LANES):
        lanes = slice(j * LANES, (j + 1) * LANES)
        dmix_pair = dmix_low[:, lanes]
        stacked = jnp.concatenate([dmix_pair * first, dmix_pair * second], axis=0)
        grad_pair = mm(stepped_low[:, lanes], stacked, NT)
        parts = []
        for i in range(2):
            h = 2 * j + i
            gap = jnp.minimum(cum_t[h : h + 1, :] - cum[:, h : h + 1], 0.0)
            reach = jnp.exp(gap)
            mixing = scores * reach
            grad_mixing = grad_pair[:, i * rows : (i + 1) * rows]
            grad_scores = grad_scores + grad_mixing * reach
            flows[:, h * rows : (h + 1) * rows] = (grad_mixing * mixing).astype(BF16)
            parts.append(mixing.astype(BF16))
        grad_step_ref[:, lanes] = later[:, lanes] + mm(jnp.concatenate(parts, axis=1), stacked)
    grad_scores = jnp.where(t_after, grad_scores, 0.0)
    s_top, s_rest = halves(grad_scores)
    c_top, c_rest = halves(c_part)
    b_top, b_rest = halves(b_part)
    grad_b_ref[...] = grad_b + mm(
        jnp.concatenate([s_top, s_rest, s_top], axis=1),
        jnp.concatenate([c_top, c_top, c_rest], axis=0),
    )
    grad_c_ref[...] = grad_c + mm(
        jnp.concatenate([s_top, s_rest, s_top], axis=0),
        jnp.concatenate([b_top, b_top, b_rest], axis=0),
        TN,
    )

    out_flow = gather_heads(dmix * from_entry, gather_matrix)
    in_flow = gather_heads(later * stepped, gather_matrix)
    kept = jnp.sum(entry * adj, axis=0, keepdims=True) * grown[rows - 1 : rows, :]
    kept = gather_heads(jnp.broadcast_to(kept, (8, width)), gather_matrix)[0:1, :]
    flow = flows[...]
    source = mm(flow, ones_ref[...])
    target = mm(jnp.ones((8, rows), BF16), flow)
    heads = width // HEAD_DIM
    target = jnp.concatenate(
        [target[0:1, h * rows : (h + 1) * rows] for h in range(heads)]
        + [jnp.zeros((LANES - heads, rows), F32)],
        axis=0,
    ).T
    after = exact(t_after.astype(F32), target - source + out_flow)
    before = exact(lower_ones(rows).astype(F32), in_flow) - in_flow
    decay_ref[...] = kept + after + before


def mix_back_call(kept, dmix, adj, consts, *ahead):
    conv_x, conv_s, step, cum, _, entry, rate, entry_in = kept
    length, width = conv_x.shape
    rows = min(SPAN, length)
    chunks = length // rows
    spread_matrix, gather_matrix, ones = consts
    head_count = width // HEAD_DIM
    return ordered_call(
        mix_back_kernel,
        ahead,
        grid=(chunks,),
        in_specs=[
            chunk_of(rows, width),
            chunk_of(rows, 2 * NSTATE),
            chunk_of(rows, width),
            chunk_of(rows, LANES),
            chunk_of(rows, LANES),
            stack_of(NSTATE, width),
            stack_of(8, LANES),
            whole_of(NSTATE, width),
            stack_of(NSTATE, width),
            whole_of(2 * LANES, width),
            whole_of(2 * width, LANES),
            whole_of(head_count * rows, LANES),
        ],
        out_specs=[
            chunk_of(rows, width),
            chunk_of(rows, NSTATE),
            chunk_of(rows, NSTATE),
            chunk_of(rows, LANES),
            whole_of(8, width),
        ],
        out_shape=[
            shape(length, width),
            shape(length, NSTATE),
            shape(length, NSTATE),
            shape(length, LANES),
            shape(8, width),
        ],
        scratch_shapes=[pltpu.VMEM((rows, head_count * rows), BF16)],
        compiler_params=params_of(14),
        cost_estimate=cost(40 * length * rows * width, 20 * length * width),
        name="mix_back",
    )(conv_x, conv_s, dmix, step, cum, entry, rate, entry_in, adj, spread_matrix, gather_matrix, ones)


def later_kernel(
    conv_x_ref,
    conv_s_ref,
    dmix_ref,
    step_ref,
    cum_ref,
    raw_ref,
    entry_ref,
    entry_rate_ref,
    entry_in_ref,
    adj_rate_ref,
    adj_in_ref,
    grad_step_ref,
    grad_b_ref,
    grad_c_ref,
    decay_ref,
    pack_ref,
    spread_ref,
    gather_ref,
    grad_ref,
    grad_raw_ref,
    small_ref,
):
    chunk = pl.program_id(0)
    rows, width = conv_x_ref.shape

    @pl.when(chunk == 0)
    def _():
        small_ref[...] = jnp.zeros_like(small_ref)

    spread_matrix = spread_ref[...]
    gather_matrix = gather_ref[...]
    conv = conv_x_ref[...]
    sig = logistic(conv)
    values = conv * sig
    conv_s = conv_s_ref[...]
    sig_s = logistic(conv_s)
    b_part = conv_s[:, :NSTATE] * sig_s[:, :NSTATE]
    step = step_ref[...]
    cum = cum_ref[...]
    last = cum[rows - 1 : rows, :]
    step_wide = spread(step, spread_matrix)
    left_wide = spread(jnp.exp(last - cum), spread_matrix)
    kept = spread(jnp.exp(cum[rows - 8 : rows, :]), spread_matrix)[7:8, :]
    entry = entry_ref[0] + spread(entry_rate_ref[0], spread_matrix)[0:1, :] * entry_in_ref[...]
    adj = spread(adj_rate_ref[0], spread_matrix)[0:1, :] * adj_in_ref[...]
    adj_low = adj.astype(BF16)
    stepped = step_wide * values
    later = left_wide * mm(both_halves(b_part), twice(adj_low))
    grad_b = grad_b_ref[...] + mm((left_wide * stepped).astype(BF16), adj_low, NT)
    in_flow = gather_heads(later * stepped, gather_matrix)
    kept = jnp.sum(entry * adj, axis=0, keepdims=True) * kept
    kept = gather_heads(jnp.broadcast_to(kept, (8, width)), gather_matrix)[0:1, :]
    before = exact(lower_ones(rows).astype(F32), in_flow) - in_flow
    grad_decay = decay_ref[...] + kept + before
    grad_stepped = grad_step_ref[...] + later
    grad_step = gather_heads(grad_stepped * values, gather_matrix)
    grad_values = step_wide * grad_stepped + pack_ref[SKIP : SKIP + 1, :width] * dmix_ref[...]
    grad_ref[:, :width] = grad_values * (sig * (1.0 + conv * (1.0 - sig)))
    slope = sig_s * (1.0 + conv_s * (1.0 - sig_s))
    grad_ref[:, width : width + NSTATE] = grad_b * slope[:, :NSTATE]
    grad_ref[:, width + NSTATE :] = grad_c_ref[...] * slope[:, NSTATE:]
    rate = -jnp.exp(pack_ref[DECAY : DECAY + 1, :LANES])
    grad_raw = (grad_step + rate * grad_decay) * logistic(raw_ref[...] + pack_ref[STEP : STEP + 1, :LANES])
    grad_raw_ref[...] = grad_raw.astype(BF16)
    small_ref[0:1, :] += jnp.sum(grad_raw, axis=0, keepdims=True)
    small_ref[1:2, :] += jnp.sum(grad_decay * (rate * step), axis=0, keepdims=True)


def later_call(kept, dmix, adj_rate, adj_in, parts, pack, consts, *ahead):
    conv_x, conv_s, step, cum, raw, entry, rate, entry_in = kept
    length, width = conv_x.shape
    rows = min(SPAN, length)
    chunks = length // rows
    spread_matrix, gather_matrix, _ = consts
    return ordered_call(
        later_kernel,
        ahead,
        grid=(chunks,),
        in_specs=[
            chunk_of(rows, width),
            chunk_of(rows, 2 * NSTATE),
            chunk_of(rows, width),
            chunk_of(rows, LANES),
            chunk_of(rows, LANES),
            chunk_of(rows, LANES),
            stack_of(NSTATE, width),
            stack_of(8, LANES),
            whole_of(NSTATE, width),
            stack_of(8, LANES),
            whole_of(NSTATE, width),
            chunk_of(rows, width),
            chunk_of(rows, NSTATE),
            chunk_of(rows, NSTATE),
            chunk_of(rows, LANES),
            whole_of(*pack.shape),
            whole_of(2 * LANES, width),
            whole_of(2 * width, LANES),
        ],
        out_specs=[chunk_of(rows, width + 2 * NSTATE), chunk_of(rows, LANES), whole_of(8, LANES)],
        out_shape=[
            shape(length, width + 2 * NSTATE),
            shape(length, LANES, dtype=BF16),
            shape(8, LANES),
        ],
        compiler_params=params_of(14),
        cost_estimate=cost(8 * length * NSTATE * width, 24 * length * width),
        name="later",
    )(
        conv_x,
        conv_s,
        dmix,
        step,
        cum,
        raw,
        entry,
        rate,
        entry_in,
        adj_rate,
        adj_in,
        *parts,
        pack,
        spread_matrix,
        gather_matrix,
    )


def conv_back_kernel(
    chunks,
    front_spec,
    gate_spec,
    where_ref,
    grad_ref,
    pre_ref,
    raw_ref,
    dz_ref,
    low_ref,
    tok_ref,
    halo_ref,
    halo_tok_ref,
    pack_ref,
    x_ref,
    inv_ref,
    head_ref,
    skip_ref,
    gained_ref,
    gather_ref,
    f0,
    f1,
    f2,
    f3,
    f4,
    f5,
    z0,
    z1,
    z2,
    z3,
    *refs,
):
    if front_spec[0] == 0:
        above, refs = refs[0], refs[1:]
    else:
        above = None
    conv_back_body(
        chunks,
        front_spec,
        gate_spec,
        (where_ref, grad_ref, pre_ref, raw_ref, dz_ref, low_ref, tok_ref, halo_ref, halo_tok_ref, pack_ref, x_ref, inv_ref),
        (head_ref, skip_ref, gained_ref, gather_ref),
        (f0, f1, f2, f3, f4, f5),
        (z0, z1, z2, z3),
        above,
        *refs,
    )


def conv_back_body(
    chunks,
    front_spec,
    gate_spec,
    inputs,
    vectors,
    held_front,
    held_gate,
    above,
    keep_ref,
    send_ref,
    g0,
    k0,
    g1,
    k1,
    vector_ref,
    vector_send_ref,
    small_ref,
    front,
    front_sems,
    gate,
    gate_sems,
    ext,
    ext_tok,
    grads,
):
    where_ref, grad_ref, pre_ref, raw_ref, dz_ref, low_ref, tok_ref, halo_ref, halo_tok_ref, pack_ref, x_ref, inv_ref = inputs
    head_ref, skip_ref, gained_ref, gather_ref = vectors
    step = pl.program_id(0)
    rows, both = pre_ref.shape
    width = both - 2 * NSTATE
    tile = g0.shape[1]
    core = where_ref[CORE]

    @pl.when(step == 0)
    def _():
        start_weights(front_spec, where_ref, held_front, front, front_sems)
        start_weights(gate_spec, where_ref, held_gate, gate, gate_sems)
        ext[rows : rows + 8, :] = halo_ref[...]
        ext_tok[rows : rows + 8, :] = halo_tok_ref[...]
        small_ref[...] = jnp.zeros_like(small_ref)

    @pl.when(jnp.logical_and(step > 0, step < chunks))
    def _():
        ext[rows : rows + 8, :] = ext[0:8, :]
        ext_tok[rows : rows + 8, :] = ext_tok[0:8, :]

    @pl.when(step < chunks)
    def _():
        grad = grad_ref[...]
        ext[0:rows, :] = grad
        ext_tok[0:rows, :] = tok_ref[...]
        pre = pre_ref[...]
        out = pack_ref[TAPS : TAPS + 1, :] * grad
        small_ref[TAPS : TAPS + 1, :] += jnp.sum(grad * pre, axis=0, keepdims=True)
        small_ref[BIAS : BIAS + 1, :] += jnp.sum(grad, axis=0, keepdims=True)
        for k in range(1, CONV):
            shifted = ext_tok[k : k + rows, k : k + 1] * ext[k : k + rows, :]
            out = out + pack_ref[TAPS + k : TAPS + k + 1, :] * shifted
            small_ref[TAPS + k : TAPS + k + 1, :] += jnp.sum(shifted * pre, axis=0, keepdims=True)
        out_x = out[:, :width].astype(BF16)
        s_top, s_rest = halves(out[:, width:])
        raw = raw_ref[...]
        dz = dz_ref[...]
        at = pl.ds(pl.multiple_of((chunks - 1 - step) * rows, rows), rows)
        grads[at, :] = jnp.concatenate([out_x, s_top, raw, dz, s_rest], axis=1)
        low = low_ref[...]
        none = jnp.zeros((rows, LANES), BF16)
        halves_of = [dz, out_x, low, s_top, s_rest]
        for_lower = [v[:, : v.shape[1] // 2] for v in halves_of] + [raw]
        for_upper = [v[:, v.shape[1] // 2 :] for v in halves_of] + [none]

        @pl.when(core == 0)
        def _():
            keep_ref[...] = jnp.concatenate(for_lower, axis=1)
            send_ref[...] = jnp.concatenate(for_upper, axis=1)

        @pl.when(core == 1)
        def _():
            keep_ref[...] = jnp.concatenate(for_upper, axis=1)
            send_ref[...] = jnp.concatenate(for_lower, axis=1)

    @pl.when(step == chunks)
    def _():
        wait_weights(front_spec, where_ref, held_front, front, front_sems)
        wait_weights(gate_spec, where_ref, held_gate, gate, gate_sems)
        skip = gather_heads(skip_ref[...], gather_ref[...])
        small_ref[SKIP : SKIP + 1, :LANES] = skip[0:1, :]
        small_ref[GATED : GATED + 1, :width] = gained_ref[0:1, :]
        small_ref[STEP : STEP + 2, :LANES] = head_ref[0:2, :]

    for n in range(2 * front.shape[0] // (2 * tile)):

        @pl.when(step == chunks + n)
        def _():
            at = slice(n * tile, (n + 1) * tile)
            part = (
                mm(grads[:, : both + LANES], front[at, :], NT)
                + mm(grads[:, both + LANES : both + LANES + width], gate[at, :], NT)
                + mm(grads[:, both + LANES + width :], front[at, width:both], NT)
            )
            put_quarters(where_ref, part, (g0, k0, g1, k1))
            row = jnp.sum(part * (x_ref[...].astype(F32) * inv_ref[:, 0:1]), axis=0, keepdims=True)
            per_row = front.shape[0] // 2 // tile
            place = slice((n % per_row) * tile, (n % per_row + 1) * tile)
            small_ref[NORM + n // per_row : NORM + n // per_row + 1, place] = row

    @pl.when(step == pl.num_programs(0) - 1)
    def _():
        if above is None:
            vector_ref[...] = small_ref[...]
            vector_send_ref[...] = jnp.zeros_like(vector_send_ref)
            return
        small, other = small_ref[...], above[...]
        vector_ref[...] = jnp.where(core == 0, small, other)
        vector_send_ref[...] = jnp.where(core == 0, other, small)


def conv_back_call(
    where, grad, pre, grad_raw, dz, low, tok, halo, halo_tok, pack, x, inv, head, skip, gained, gather_matrix, front, gate, above, *ahead
):
    length, both = pre.shape
    width = both - 2 * NSTATE
    model = 2 * front[1][0].shape[0]
    rows = min(SPAN, length)
    chunks = length // rows
    tile = model // 4
    out_width = 3 * (width // 2) + 2 * NSTATE + LANES

    def chunk_spec(size):
        return pl.BlockSpec((rows, size), lambda c: (jnp.maximum(chunks - 1 - c, 0), 0))

    def tile_spec(rows_):
        return pl.BlockSpec((rows_, tile), lambda c: (0, jnp.maximum(c - chunks, 0)))

    return ordered_call(
        functools.partial(conv_back_kernel, chunks, front[0], gate[0]),
        ahead,
        grid=(chunks + model // tile,),
        in_specs=[
            scalars_of(),
            chunk_spec(both),
            chunk_spec(both),
            chunk_spec(LANES),
            chunk_spec(width),
            chunk_spec(width),
            chunk_spec(LANES),
            whole_of(8, both),
            whole_of(8, LANES),
            whole_of(*pack.shape),
            tile_spec(length),
            whole_of(length, LANES),
            whole_of(8, LANES),
            whole_of(8, width),
            whole_of(8, width),
            whole_of(2 * width, LANES),
        ]
        + anywhere(10)
        + [whole_of(*pack.shape)] * len(above),
        out_specs=[
            chunk_spec(out_width),
            chunk_spec(out_width),
        ]
        + [tile_spec(length // 4)] * 4
        + [whole_of(*pack.shape)] * 2,
        out_shape=[
            shape(length, out_width, dtype=BF16),
            shape(length, out_width, dtype=BF16),
        ]
        + quarter_shapes(length, model, BF16)
        + [shape(*pack.shape)] * 2,
        scratch_shapes=[pltpu.VMEM(pack.shape, F32)]
        + weight_scratch(front)
        + weight_scratch(gate)
        + [
            pltpu.VMEM((rows + 8, both), F32),
            pltpu.VMEM((rows + 8, LANES), F32),
            pltpu.VMEM((length, both + LANES + width + 2 * NSTATE), BF16),
        ],
        compiler_params=params_of(24),
        cost_estimate=cost(4 * length * model * both, 24 * length * width),
        name="conv_back",
    )(where, grad, pre, grad_raw, dz, low, tok, halo, halo_tok, pack, x, inv, head, skip, gained, gather_matrix, *front[1], *gate[1], *above)


def split_states(total, width):
    top, rest = halves(total[:, width : width + NSTATE])
    return jnp.concatenate(
        [total[:, :width].astype(BF16), top, rest, total[:, width + NSTATE :].astype(BF16)], axis=1
    )


def whole_states(value, width):
    value = value.astype(F32)
    states = value[:, width : width + NSTATE] + value[:, width + NSTATE : width + 2 * NSTATE]
    return jnp.concatenate([value[:, :width], states, value[:, width + 2 * NSTATE :]], axis=1)


def block_grads(n0, n1, g0, g1, keep_ref, got_ref):
    width = keep_ref.shape[1] - 2 * NSTATE - LANES
    inner = 2 * width // 3
    mine, theirs = n0[...], n1[...]
    main = mm(mine, keep_ref[:, :inner], TN) + mm(theirs, got_ref[:, :inner], TN)
    outer = mm(g0[...].astype(BF16), keep_ref[:, inner:width], TN) + mm(
        g1[...].astype(BF16), got_ref[:, inner:width], TN
    )
    rest = mm(mine, keep_ref[:, width:], TN) + mm(theirs, got_ref[:, width:], TN)
    states = rest[:, :NSTATE] + rest[:, NSTATE : 2 * NSTATE]
    return split_states(jnp.concatenate([main, outer, states, rest[:, 2 * NSTATE :]], axis=1), width)


def wgrad_plain_kernel(*refs):
    refs[-1][0] = block_grads(*refs[:-1])


def wgrad_relative_kernel(extra, alike, where_ref, *refs):
    value = block_grads(*refs[:6])
    first_give, first_keep, second_give, second_keep = refs[6 + extra :]
    half = value.shape[0] // 2
    step = pl.program_id(0)

    first_sent = step % 2 == 1 if alike else step < 2

    @pl.when(first_sent)
    def _():
        first_give[0] = value[:half]

    @pl.when(jnp.logical_not(first_sent))
    def _():
        first_keep[0] = value[:half]

    @pl.when(step % 2 == 1)
    def _():
        second_give[0] = value[half:]

    @pl.when(step % 2 == 0)
    def _():
        second_keep[0] = value[half:]


def wgrad_call(where, spans, alike, normed, normed_other, g_low, g_other, keep, got, *ahead):
    length, model = normed.shape
    size = keep.shape[1]
    blocks = spans[0] * spans[1]
    rows = model // blocks
    operands = (normed, normed_other, g_low, g_other, keep, got)
    if spans != (2, 2):
        grid_rows = max(rows, LANES)
        steps = model // grid_rows
        return pl.pallas_call(
            wgrad_plain_kernel,
            grid=(steps,),
            in_specs=[pl.BlockSpec((length, grid_rows), lambda b: (0, b))] * 4
            + [whole_of(*v.shape) for v in operands[4:]],
            out_specs=pl.BlockSpec((1, grid_rows, size), lambda b: (b, 0, 0)),
            out_shape=shape(steps, grid_rows, size, dtype=BF16),
            compiler_params=params_of(20),
            cost_estimate=cost(0, 0),
            name="wgrad",
        )(*operands).reshape(blocks, rows, size)

    def block_index(b, where_ref):
        x = jnp.where(b < 2, 1 - where_ref[ALONG_X], where_ref[ALONG_X])
        y = jnp.where(b % 2 == 1, 1 - where_ref[ALONG_Y], where_ref[ALONG_Y])
        return (0, 2 * x + y)

    def whole(v):
        return pl.BlockSpec(v.shape, lambda b, where_ref: (0,) * v.ndim)

    maps = [
        lambda b, where_ref: (jnp.minimum(b, 1), 0, 0),
        lambda b, where_ref: (jnp.maximum(b - 2, 0), 0, 0),
        lambda b, where_ref: (1 - b // 2, 0, 0),
        lambda b, where_ref: (1 - b // 2, 0, 0),
    ]
    if alike:
        maps = maps[2:] * 2
    return pl.pallas_call(
        functools.partial(wgrad_relative_kernel, len(ahead), alike),
        grid_spec=pltpu.PrefetchScalarGridSpec(
            num_scalar_prefetch=1,
            grid=(4,),
            in_specs=[pl.BlockSpec((length, rows), block_index)] * 4
            + [whole(v) for v in operands[4:]]
            + [pl.BlockSpec(memory_space=pl.ANY)] * len(ahead),
            out_specs=[pl.BlockSpec((1, rows // 2, size), m) for m in maps],
        ),
        out_shape=[shape(2, rows // 2, size, dtype=BF16)] * 4,
        compiler_params=params_of(20),
        cost_estimate=cost(0, 0),
        name="wgrad",
    )(where, *operands, *ahead)


def turn_kernel(*refs):
    for n in range(2):
        keep_ref, got_ref, give_ref, kept_ref = refs[n::2]
        width = keep_ref.shape[2] - 2 * NSTATE - LANES
        sums = [whole_states(keep_ref[m], width) + whole_states(got_ref[m], width) for m in range(2)]
        kept_ref[...] = sums[0]
        give_ref[...] = split_states(sums[1], width)


def turn_call(keeps, gots, *ahead):
    _, rows, size = keeps[0].shape
    outputs = ordered_call(
        turn_kernel,
        ahead,
        in_specs=[pl.BlockSpec(memory_space=pltpu.VMEM)] * 4,
        out_specs=[pl.BlockSpec(memory_space=pltpu.VMEM)] * 4,
        out_shape=[shape(rows, size, dtype=BF16)] * 2 + [shape(rows, size - NSTATE)] * 2,
        compiler_params=pltpu.CompilerParams(vmem_limit_bytes=16 * 1024 * 1024),
        cost_estimate=cost(0, 0),
        name="turn",
    )(*keeps, *gots)
    return outputs[:2], outputs[2:]


def summed_kernel(where_ref, first_keep, first_got, second_keep, second_got, *refs):
    rows = first_keep.shape[0]
    above, outs = (None, refs) if len(refs) == 3 else (refs[:2], refs[2:])
    matrices_ref, steps_ref = outs[:2]
    width = matrices_ref.shape[1]
    lower = where_ref[CORE] == 0
    states = []
    for at, keep, got in ((slice(0, rows), first_keep, first_got), (slice(rows, 2 * rows), second_keep, second_got)):
        total = keep[...] + whole_states(got[...], width)
        matrices = total[:, :width].astype(BF16)
        states.append(total[:, width : width + NSTATE])
        steps_ref[at, :] = total[:, width + NSTATE :]
        if above is None:
            matrices_ref[at, :] = matrices
        else:
            other = above[0][at, :]
            matrices_ref[at, :] = jnp.where(lower, matrices, other)
            outs[2][at, :] = jnp.where(lower, other, matrices)
    states = jnp.concatenate(states, axis=0)
    if above is None:
        outs[2][...] = states
    else:
        put_quarters(where_ref, jnp.concatenate([states, above[1][...]], axis=1), outs[3:])


def summed_call(where, operands, above, *ahead):
    rows, size = operands[1].shape
    width = size - 2 * NSTATE - LANES
    matrices = shape(2 * rows, width, dtype=BF16)
    more = [matrices] + quarter_shapes(2 * rows, 2 * NSTATE, F32) if above else [shape(2 * rows, NSTATE)]
    outs = [matrices, shape(2 * rows, LANES)] + more
    return ordered_call(
        summed_kernel,
        ahead,
        in_specs=[scalars_of()] + [pl.BlockSpec(memory_space=pltpu.VMEM)] * (4 + len(above)),
        out_specs=[pl.BlockSpec(memory_space=pltpu.VMEM)] * len(outs),
        out_shape=outs,
        compiler_params=pltpu.CompilerParams(vmem_limit_bytes=16 * 1024 * 1024),
        cost_estimate=cost(0, 0),
        name="summed",
    )(where, *operands, *above)


def renorm_kernel(x_ref, pack_ref, out_ref):
    gain = norm_row(pack_ref, x_ref.shape[1] // 2)
    x = x_ref[...].astype(F32)
    inv = lax.rsqrt(jnp.mean(x * x, axis=-1, keepdims=True) + EPS)
    out_ref[...] = (x * inv * gain).astype(BF16)


def renorm_call(x, pack, *ahead):
    length, model = x.shape
    rows = min(SPAN, length)
    return ordered_call(
        renorm_kernel,
        ahead,
        grid=(length // rows,),
        in_specs=[chunk_of(rows, model), whole_of(*pack.shape)],
        out_specs=chunk_of(rows, model),
        out_shape=shape(length, model, dtype=BF16),
        compiler_params=params_of(10),
        cost_estimate=cost(0, 0),
        name="renorm",
    )(x, pack)


def swap(value, axis):
    return lax.ppermute(value, axis, [(0, 1), (1, 0)])


def shifted_along(value, axis, by):
    count = lax.axis_size(axis)
    return lax.ppermute(
        value, axis, [(i, i + by) for i in range(count) if 0 <= i + by < count]
    )


def sum_over(value, axis):
    if lax.axis_size(axis) == 2:
        return value + swap(value, axis)
    return lax.psum(value, axis)


def sum_given(value, axis):
    if lax.axis_size(axis) == 2:
        return swap(value, axis)
    return lax.psum(value, axis) - value


def after(value, *earlier):
    for event in earlier:
        first = lax.slice(event, (0,) * event.ndim, (1,) * event.ndim).reshape(())
        value = value + (first.astype(F32) * 0.0).astype(value.dtype)
    return value


def carried_state(state, rate_wide, axis, backward):
    count = lax.axis_size(axis)
    if count == 2:
        return shifted_along(state.astype(BF16), axis, -1 if backward else 1).astype(F32)
    here = lax.axis_index(axis)
    states = lax.all_gather(state, axis)
    rates = lax.all_gather(rate_wide, axis)
    result = jnp.zeros_like(state)
    for k in range(count):
        at = count - 1 - k if backward else k
        reached = at > here if backward else at < here
        result = jnp.where(reached, rates[at] * result + states[at], result)
    return result


def small_sum(value):
    count = lax.axis_size("tensor")
    total = value
    for by in range(1, count):
        total = total + lax.ppermute(
            value, "tensor", [(i, (i + by) % count) for i in range(count)]
        )
    return total


class TensorSum:
    NEAR = [(0, 1), (1, 0), (2, 3), (3, 2)]
    FAR = [(0, 2), (2, 0), (1, 3), (3, 1)]
    STEPS = ((NEAR, FAR, NEAR), (FAR, NEAR, FAR))

    def __init__(self, pieces):
        self.pieces = pieces
        self.given = self._send([give for _, give, _ in pieces], 0)
        self.kind = pieces[0][1].dtype

    def _send(self, arrays, step):
        return [
            lax.ppermute(v, "tensor", self.STEPS[half][step])
            for (half, _, _), v in zip(self.pieces, arrays)
        ]

    def _merge(self, firsts, seconds, ahead):
        if self.kind == jnp.float16:
            firsts, seconds = [v.astype(F32) for v in firsts], [v.astype(F32) for v in seconds]
            merged = merge_call(firsts, seconds, F32, *ahead)
            self.event = merged[-1]
            return [v.astype(self.kind) for v in merged]
        return merge_call(firsts, seconds, self.kind, *ahead)

    def add(self, *ahead):
        self.parts = self._merge([keep for _, _, keep in self.pieces], self.given, ahead)
        return self.parts[-1]

    def hold(self, *ahead):
        held = hold_call(self.parts, *ahead)
        self.given = self._send(held, 1)
        return held[-1]

    def across(self, *ahead):
        self.add(*ahead)
        self.given = self._send(self.parts, 1)
        return self.parts[-1]

    def total(self, *ahead):
        self.totals = self._merge(self.parts, self.given, ahead)
        return self.totals[-1]

    def spread(self, *ahead):
        held = hold_call(self.totals, *ahead)
        self.others = self._send(held, 2)
        return held[-1]

    def back(self, *ahead):
        self.total(*ahead)
        self.others = self._send(self.totals, 2)
        return self.totals[-1]

    def quarters(self):
        return [v for pair in zip(self.totals, self.others) for v in pair]


class ScatterSum:
    def __init__(self, value, alike, *ahead):
        self.whole = None
        self.orders = (("context", "fsdp") if alike else ("fsdp", "context"), ("context", "fsdp"))
        if not isinstance(value, (list, tuple)):
            self.whole = lax.psum_scatter(value, ("fsdp", "context"), scatter_dimension=0, tiled=False)
            return
        self.keeps = [value[1], value[3]]
        gives = hold_call([value[0], value[2]], *ahead)
        self.given = [swap(give, order[0]) for give, order in zip(gives, self.orders)]

    def turn(self, *ahead):
        if self.whole is not None:
            return self.whole
        gives, self.keeps = turn_call(self.keeps, self.given, *ahead)
        self.given = [swap(give, order[1]) for give, order in zip(gives, self.orders)]
        return gives[0]

    def result(self, where, above, *ahead):
        if self.whole is not None:
            half = self.whole.shape[0] // 2
            none = jnp.zeros((half, self.whole.shape[1] - NSTATE), F32)
            operands = none, self.whole[:half], none, self.whole[half:]
        else:
            operands = self.keeps[0], self.given[0], self.keeps[1], self.given[1]
        return summed_call(where, operands, above, *ahead)


def rest_kernel(where_ref, t0, o0, t1, o1, steps0, steps1, own_ref, send_ref):
    rows = steps0.shape[0]
    states = joined(where_ref, (t0, o0, t1, o1), slice(0, rows))
    first = jnp.concatenate([states[:, :NSTATE], steps0[...]], axis=1)
    second = jnp.concatenate([states[:, NSTATE:], steps1[...]], axis=1)
    lower = where_ref[CORE] == 0
    own_ref[...] = jnp.where(lower, first, second)
    send_ref[...] = jnp.where(lower, second, first)


def rest_call(where, quarters, steps0, steps1, *ahead):
    return ordered_call(
        rest_kernel,
        ahead,
        in_specs=[scalars_of()] + [pl.BlockSpec(memory_space=pltpu.VMEM)] * 6,
        out_specs=[pl.BlockSpec(memory_space=pltpu.VMEM)] * 2,
        out_shape=[shape(steps0.shape[0], NSTATE + LANES)] * 2,
        compiler_params=pltpu.CompilerParams(vmem_limit_bytes=8 * 1024 * 1024),
        cost_estimate=cost(0, 0),
        name="rest",
    )(where, *quarters, steps0, steps1)


def matrices_kernel(where_ref, own, got, rest, rest_got, main_ref, states_ref, step_ref, out_ref):
    def put(lower, upper, lower_rest, upper_rest):
        half = main_ref.shape[3] // 2
        a, b = lower[...].astype(F32), upper[...].astype(F32)
        main_ref[0, :, 0, :] = jnp.concatenate([a[:, :half], b[:, :half]], axis=1)
        main_ref[0, :, 1, :] = jnp.concatenate([a[:, half : 2 * half], b[:, half : 2 * half]], axis=1)
        out_ref[0] = jnp.concatenate([a[:, 2 * half :], b[:, 2 * half :]], axis=1)
        states_ref[0] = jnp.concatenate([lower_rest[:, :NSTATE], upper_rest[:, :NSTATE]], axis=1)
        step_ref[0] = lower_rest[:, NSTATE : NSTATE + step_ref.shape[2]]

    @pl.when(where_ref[CORE] == 0)
    def _():
        put(own, got, rest, rest_got)

    @pl.when(where_ref[CORE] == 1)
    def _():
        put(got, own, rest_got, rest)


def matrices_call(where, heads, *arrays):
    rows, columns_ = arrays[0].shape
    half = columns_ // 3
    block = rows // 2

    def out_spec(*dims):
        return pl.BlockSpec((1, block) + dims, lambda r: (0, r) + (0,) * len(dims))

    return pl.pallas_call(
        matrices_kernel,
        grid=(2,),
        in_specs=[scalars_of()] + [pl.BlockSpec((block, v.shape[1]), lambda r: (r, 0)) for v in arrays],
        out_specs=[out_spec(2, 2 * half), out_spec(2 * NSTATE), out_spec(heads), out_spec(2 * half)],
        out_shape=[
            shape(1, rows, 2, 2 * half),
            shape(1, rows, 2 * NSTATE),
            shape(1, rows, heads),
            shape(1, rows, 2 * half),
        ],
        compiler_params=params_of(20),
        cost_estimate=cost(0, 0),
        name="matrices",
    )(where, *arrays)


def tokens_kernel(where_ref, own0, got0, own1, got1, *refs):
    out_ref, tick_ref = refs[-2:]
    tick_ref[...] = jnp.zeros_like(tick_ref)
    which = pl.program_id(0)
    core = where_ref[CORE]

    @pl.when(core == 0)
    def _():
        @pl.when(which == 0)
        def _():
            out_ref[0, 0] = own0[...]

        @pl.when(which == 1)
        def _():
            out_ref[0, 0] = got0[...].astype(F32)

    @pl.when(core == 1)
    def _():
        @pl.when(which == 0)
        def _():
            out_ref[0, 0] = got1[...].astype(F32)

        @pl.when(which == 1)
        def _():
            out_ref[0, 0] = own1[...]


def tokens_call(where, own0, got0, own1, got1, *ahead):
    length, model = own0.shape
    block = length // 2

    def spec(core, which):
        def index(s, r, where_ref):
            return (jnp.where((where_ref[CORE] == core) & (s == which), r, 0), 0)

        return pl.BlockSpec((block, model), index)

    return pl.pallas_call(
        tokens_kernel,
        grid_spec=pltpu.PrefetchScalarGridSpec(
            num_scalar_prefetch=1,
            grid=(2, length // block),
            in_specs=[spec(0, 0), spec(0, 1), spec(1, 1), spec(1, 0)]
            + [pl.BlockSpec(memory_space=pl.ANY)] * len(ahead),
            out_specs=[
                pl.BlockSpec((1, 1, block, model), lambda s, r, where_ref: (0, s, r, 0)),
                pl.BlockSpec((8, LANES), lambda s, r, where_ref: (0, 0)),
            ],
        ),
        out_shape=[shape(1, 2, length, model), shape(8, LANES)],
        compiler_params=pltpu.CompilerParams(
            dimension_semantics=("arbitrary", "arbitrary"), vmem_limit_bytes=20 * 1024 * 1024
        ),
        cost_estimate=cost(0, 16 * length * model),
        name="tokens",
    )(where, own0, got0, own1, got1, *ahead)


def shards(
    block_input,
    doc_start,
    cotangent,
    norm_gain,
    proj_main,
    proj_states,
    proj_step,
    conv_main,
    conv_main_bias,
    conv_states,
    conv_states_bias,
    step_bias,
    log_decay,
    skip_gain,
    gated_gain,
    proj_out,
):
    core = lax.axis_index("section")
    lower_core = core == 0
    length = block_input.shape[1]
    model = block_input.shape[2]
    heads = proj_step.shape[2]
    width = heads * HEAD_DIM
    half = width // 2
    both = width + 2 * NSTATE
    rows = min(SPAN, length)
    spans = lax.axis_size("fsdp"), lax.axis_size("context")
    x_index, y_index = lax.axis_index("fsdp"), lax.axis_index("context")
    z_index = lax.axis_index("tensor")
    place = jnp.stack([core, 1 - x_index, z_index % 2, z_index // 2, x_index, y_index]).astype(jnp.int32)

    main_own = lax.optimization_barrier(proj_main[0].reshape(-1, 2 * width))
    rest_own = jnp.concatenate(
        [proj_states[0], jnp.pad(proj_step[0], ((0, 0), (0, LANES - heads)))], axis=1
    )
    out_own = proj_out[0]
    main_near = swap(main_own, "section")
    rest_near = swap(rest_own, "section")
    out_near = swap(out_own, "section")
    rest_width = rest_own.shape[1]
    front_width = width + rest_width
    held = (main_own, main_near, rest_own, rest_near, out_own, out_near)
    front_part, gate_part, out_part = [(0, width, width), (1, 0, rest_width)], [(0, 0, width)], [(2, 0, width)]
    mains = (main_own, main_near)
    def weights_of(layer, far_arrays, front_at, gate_at, out_at):
        front = (layer, [(width, width), (0, rest_width)], (front_at, front_width))
        gate = (layer, [(0, width)], (gate_at, width))
        out = (layer, [(0, width)], (out_at, width))
        return (
            (front, mains + (rest_own, rest_near) + far_arrays),
            (gate, mains + far_arrays),
            (out, (out_own, out_near) + far_arrays),
        )

    def both_halves_of(far, *ahead):
        far = after(far, *ahead)
        return far, swap(far, "section")

    head_of = np.arange(width) // HEAD_DIM
    one_hot = (np.arange(LANES)[:, None] == head_of[None, :]).astype(np.float32)
    spread_matrix = jnp.asarray(np.concatenate([one_hot, one_hot], axis=0), BF16)
    gather_matrix = jnp.asarray(np.concatenate([one_hot.T, one_hot.T], axis=0), BF16)
    row_head = np.arange(heads * rows) // rows
    ones = jnp.asarray((row_head[:, None] == np.arange(LANES)[None, :]).astype(np.float32), BF16)
    consts = (spread_matrix, gather_matrix, ones)

    tokens = lax.dynamic_index_in_dim(block_input, core, 0, keepdims=False, allow_negative_indices=False)
    first_piece = pieces_call(place, 0, front_part, held[:4])
    cot = lax.dynamic_index_in_dim(cotangent, core, 0, keepdims=False, allow_negative_indices=False)
    tokens_other = lax.dynamic_index_in_dim(block_input, 1 - core, 0, keepdims=False, allow_negative_indices=False)
    cot_other = lax.dynamic_index_in_dim(cotangent, 1 - core, 0, keepdims=False, allow_negative_indices=False)
    starts = lax.dynamic_index_in_dim(doc_start, core, 0, keepdims=False, allow_negative_indices=False).astype(F32)
    front_far0 = swap(first_piece, "fsdp")
    gate_far0 = swap(after(pieces_call(place, 0, gate_part, held[:2]), front_far0), "fsdp")
    out_piece0 = pieces_call(place, 0, [(0, 0, width)], held[4:])
    earlier = shifted_along(after(starts[length - 8 :], first_piece), "context", 1)
    later = shifted_along(after(starts[:8], first_piece), "context", -1)
    line = jnp.concatenate([earlier, starts, later])
    keep = 1.0 - line
    one_back = keep[8:]
    two_back = one_back * keep[7:-1]
    three_back = two_back * keep[6:-2]
    tok_all = jnp.stack([line[8:], one_back, two_back, three_back], axis=1)
    tok_all = jnp.pad(tok_all, ((0, 0), (0, LANES - 4)))
    tok, tok_after = tok_all[:length], tok_all[length:]

    def head_lanes(row):
        return jnp.pad(row, ((0, 0), (0, LANES - heads)))

    pack_own = pl.pallas_call(
        pack_kernel,
        out_shape=shape(PACK, both),
        compiler_params=pltpu.CompilerParams(vmem_limit_bytes=4 * 1024 * 1024),
        name="pack",
    )(
        conv_main[0],
        conv_states[0],
        conv_main_bias,
        conv_states_bias,
        jnp.repeat(skip_gain, HEAD_DIM, axis=1),
        gated_gain,
        norm_gain,
        head_lanes(step_bias),
        head_lanes(log_decay),
    )
    pack_other = swap(pack_own, "section")
    packs = [jnp.where(core == layer, pack_own, pack_other) for layer in (0, 1)]

    def layer_front(x, halo, layer, weights, quarters, *ahead):
        front = front_call(
            place, x, halo, tok, packs[layer], spread_matrix, weights, quarters, *ahead
        )
        end, end_rate = front[-2:]
        rate_wide = jnp.repeat(end_rate[0:1, :heads], HEAD_DIM, axis=1)
        return front, rate_wide, carried_state(end, rate_wide, "context", False)

    def layer_rest(front, entry_in, y, z, layer, *grad_scaled):
        _, _, _, _, conv_x, conv_s, _, _, cum, _, rate, _, _ = front
        comb, gated, sums = gate_call(
            y, z, conv_x, conv_s, cum, rate, entry_in, packs[layer], spread_matrix, *grad_scaled
        )
        return comb, gated, small_sum(sums)

    def layer_gate_back(grad_scaled, sums, comb, z, front, rate_wide, layer, *ahead):
        _, _, _, _, _, conv_s, _, _, cum, _, _, _, _ = front
        dmix, dz, adj, adj_rate, begin, gained = gate_back_call(
            grad_scaled, comb, z, conv_s, cum, sums, packs[layer], spread_matrix, *ahead
        )
        adj_in = carried_state(begin, rate_wide, "context", True)
        return dmix, dz, adj, adj_rate, adj_in, gained

    def layer_mix_back(gate_back, front, entry_in, layer, ahead, before_later):
        _, _, _, _, conv_x, conv_s, raw, step, cum, entry, rate, _, _ = front
        kept = (conv_x, conv_s, step, cum, raw, entry, rate, entry_in)
        dmix, dz, adj, adj_rate, adj_in, gained = gate_back
        *parts, skip = mix_back_call(kept, dmix, adj, consts, *ahead)
        grad, grad_raw, head = later_call(
            kept, dmix, adj_rate, adj_in, parts, packs[layer], consts, *before_later(skip)
        )
        edge = shifted_along(grad[:8], "context", -1)
        return grad, grad_raw, dz, head, skip, gained, edge

    def layer_down(back, low, x, front, layer, front_weights, gate_weights, above, *ahead):
        grad, grad_raw, dz, head, skip, gained, edge = back
        keep, send, g0, k0, g1, k1, vector, vector_send = conv_back_call(
            place,
            grad,
            front[3],
            grad_raw,
            dz,
            low,
            tok,
            edge,
            tok_after,
            packs[layer],
            x,
            front[2],
            head,
            skip,
            gained,
            gather_matrix,
            front_weights,
            gate_weights,
            above,
            *ahead,
        )
        return keep, send, [(0, g0, k0), (1, g1, k1)], vector, vector_send

    fronts0 = weights_of(0, both_halves_of(front_far0), 0, 0, 0)[0]
    halo0 = shifted_along(after(tokens[length - 8 :], first_piece), "context", 1)
    front0, rate_wide0, entry0 = layer_front(
        tokens, halo0, 0, fronts0, (), packs[1]
    )
    normed0 = front0[1]
    y0 = mix_call(front0[4], front0[5], front0[7], front0[8], front0[9], spread_matrix)
    gate_far0 = after(gate_far0, y0)
    gates0 = weights_of(0, (gate_far0, swap(gate_far0, "section")), 0, 0, 0)[1]
    out_far0 = swap(after(out_piece0, gate_far0), "fsdp")
    z0 = project_call(place, normed0, gates0)
    comb0, gated0, sums0 = layer_rest(front0, entry0, y0, z0, 0)
    out_far0 = after(out_far0, comb0)
    outs0 = weights_of(0, (out_far0, swap(out_far0, "section")), 0, 0, 0)[2]
    pieces1 = pieces_call(place, 1, front_part, held[:4], out_far0)
    front_far1 = swap(pieces1, "fsdp")
    rest_piece1 = pieces_call(place, 1, gate_part + out_part, held)
    low0, g0, k0, g1, k1, edge0 = out_call(place, gated0, sums0, packs[0], outs0, F32, pieces1)

    half16 = jnp.float16
    total0 = TensorSum([(0, g0.astype(half16), k0), (1, g1.astype(half16), k1)])
    event = total0.across()
    edge0, rest_piece1 = hold_call([edge0, rest_piece1], total0.event)
    rest_far1 = swap(rest_piece1, "fsdp")
    edge0 = tokens[length - 8 :].astype(F32) + small_sum(edge0)
    halo1 = shifted_along(edge0, "context", 1)
    front_far1 = after(front_far1, event)
    fronts1 = weights_of(1, (front_far1, swap(front_far1, "section")), 0, 0, 0)[0]
    total0.back()
    normed_other0 = renorm_call(tokens_other, packs[0], edge0)
    branch0 = [v.astype(F32) for v in total0.quarters()]

    front1, rate_wide1, entry1 = layer_front(
        tokens, halo1, 1, fronts1, branch0
    )
    x1, normed1 = front1[:2]
    rest_far1 = after(rest_far1, edge0)
    _, gates1, outs1 = weights_of(1, (rest_far1, swap(rest_far1, "section")), 0, 0, width)
    grad_scaled1 = project_call(place, cot, outs1)
    y1 = mix_call(front1[4], front1[5], front1[7], front1[8], front1[9], spread_matrix)
    z1 = project_call(place, normed1, gates1)
    comb1, gated1, sums1 = layer_rest(front1, entry1, y1, z1, 1, grad_scaled1)

    gate_back1 = layer_gate_back(grad_scaled1, sums1, comb1, z1, front1, rate_wide1, 1)
    low1, g0, k0, g1, k1, edge1 = out_call(place, gated1, sums1, packs[1], outs1, BF16)
    half_a = TensorSum([(0, g0, k0)])
    half_b = TensorSum([(0, g1, k1)])
    back1 = layer_mix_back(gate_back1, front1, entry1, 1, (edge1,), lambda tick: ())
    keep1, send1, pieces, small1, _ = layer_down(
        back1,
        low1,
        x1,
        front1,
        1,
        fronts1,
        gates1,
        (),
        half_a.across(back1[3]),
        half_b.add(back1[3]),
    )
    *gives, send1 = hold_call([give for _, give, _ in pieces] + [send1], half_a.total(keep1))
    total1 = TensorSum([(half, give, keep) for (half, _, keep), give in zip(pieces, gives)])
    received1 = swap(send1, "section")
    x1_other = swap(x1, "section")
    normed_other1 = renorm_call(x1_other, packs[1], keep1)
    matrices1 = wgrad_call(place, spans, False, normed1, normed_other1, cot, cot_other, keep1, received1)
    event = total1.across(jax.tree.leaves(matrices1)[0])
    scatter1 = ScatterSum(matrices1, False, event)
    event = scatter1.turn(total1.back())
    grad1, g_low0, grad_scaled0, sums0_back = finish_call(
        place, total1.quarters(), cot, x1, front1[2], packs[1], (event,), branch0, sums0, outs0
    )

    matrices1, steps1, states1 = scatter1.result(place, (), sums0_back)
    gate_back0 = layer_gate_back(grad_scaled0, sums0_back, comb0, z0, front0, rate_wide0, 0)
    ahead = half_b.hold(sums0_back), half_a.spread(sums0_back)
    back0 = layer_mix_back(
        gate_back0, front0, entry0, 0, ahead, lambda tick: (steps1,)
    )
    tick = back0[3]
    grad_got1 = swap(grad1, "section")
    keep0, send0, pieces, vector, vector_send = layer_down(
        back0,
        low0,
        tokens,
        front0,
        0,
        fronts0,
        gates0,
        (small1,),
        half_b.back(tick),
        half_a.others[0],
        grad_got1,
    )
    x2 = join_call(place, x1, half_a.quarters() + half_b.quarters(), keep0)
    *gives, send0 = hold_call([give for _, give, _ in pieces] + [send0], x2)
    total0 = TensorSum([(half, give, keep) for (half, _, keep), give in zip(pieces, gives)])
    received0 = swap(send0, "section")
    matrices0 = wgrad_call(
        place,
        spans,
        False,
        normed0,
        normed_other0,
        g_low0,
        grad_got1,
        keep0,
        received0,
    )
    event = total0.across(jax.tree.leaves(matrices0)[0])
    scatter0 = ScatterSum(matrices0, False, event)
    (vector,) = merge_call([vector], [swap(vector_send, "section")], F32, event)
    vector_got = sum_given(vector, "fsdp")
    x2_other = swap(x2, "section")
    event = scatter0.turn(total0.back(vector))
    layer_out, event = tokens_call(place, x1, x1_other, x2, x2_other, event)
    matrices, steps0, matrices_send, *states = scatter0.result(place, (matrices1, states1), event)
    (vector,) = merge_call([vector], [vector_got], F32, steps0)
    (vector,) = merge_call([vector], [sum_given(vector, "context")], F32)
    count = lax.axis_size("tensor")
    vectors = [vector] + [
        lax.ppermute(vector, "tensor", [(i, (i + by) % count) for i in range(count)])
        for by in range(1, count)
    ]
    row = np.arange(PACK)[:, None]
    lane = np.arange(both)[None, :]
    shared = ((row < SKIP) & (lane >= width)) | (row == NORM) | (row == NORM + 1)
    shared = jnp.asarray(shared.astype(np.float32))
    states = TensorSum([(0, *states[:2]), (1, *states[2:])])
    matrices_got = swap(matrices_send, "section")
    grad0 = finish_call(
        place,
        total0.quarters(),
        grad1,
        tokens,
        front0[2],
        packs[0],
        (states.across(steps0), vector),
    )[0]
    grad_got0 = swap(grad0.astype(BF16), "section")
    event = states.back(grad0)
    layer_in_grad, event = tokens_call(place, grad0, grad_got0, grad1, grad_got1, event)
    vector = vector_call(shared, vectors, event)
    rest, rest_send = rest_call(place, states.quarters(), steps0, steps1, event)
    grad_main, grad_states, grad_step, grad_out = matrices_call(
        place, heads, matrices, matrices_got, rest, swap(rest_send, "section")
    )
    return (
        layer_out,
        layer_in_grad,
        vector[NORM : NORM + 2, : model // 2].reshape(1, model),
        grad_main,
        grad_states,
        grad_step,
        vector[None, TAPS : TAPS + CONV, :width],
        vector[BIAS : BIAS + 1, :width],
        vector[None, TAPS : TAPS + CONV, width:],
        vector[BIAS : BIAS + 1, width:],
        vector[STEP : STEP + 1, :heads],
        vector[DECAY : DECAY + 1, :heads],
        vector[SKIP : SKIP + 1, :heads],
        vector[GATED : GATED + 1, :width],
        grad_out,
    )


def solution(mesh):
    placed = (
        P("fsdp", "context", None),
        P("fsdp", "context"),
        P("fsdp", "context", None),
        P("section", None),
        P("section", "fsdp", None, "tensor"),
        P("section", "fsdp", None),
        P("section", "fsdp", "tensor"),
        P("section", None, "tensor"),
        P("section", "tensor"),
        P("section", None, None),
        P("section", None),
        P("section", "tensor"),
        P("section", "tensor"),
        P("section", "tensor"),
        P("section", "tensor"),
        P("section", "fsdp", "tensor"),
    )
    return jax.shard_map(
        shards,
        mesh=mesh,
        in_specs=placed,
        out_specs=(
            P("section", "fsdp", "context", None),
            P("section", "fsdp", "context", None),
            P("section", None),
            P("section", ("fsdp", "context"), None, "tensor"),
            P("section", ("fsdp", "context"), None),
            P("section", ("fsdp", "context"), "tensor"),
            P("section", None, "tensor"),
            P("section", "tensor"),
            P("section", None, None),
            P("section", None),
            P("section", "tensor"),
            P("section", "tensor"),
            P("section", "tensor"),
            P("section", "tensor"),
            P("section", ("fsdp", "context"), "tensor"),
        ),
        check_vma=False,
    )
```
